32 devices in a mesh: dp: 16 (over z, y, x), tensor: 2 (over core).
Axes of the slice: x: 2, y: 2, z: 4, core: 2. Of those that a mesh axis runs over, the one named last changes fastest.
Arguments:
- tokens: bfloat16 [16384, 768], P('dp', 'tensor'), may hold values from -6 to 6
- cotangent: bfloat16 [16384, 768], P('dp', 'tensor'), may hold values from -6 to 6
- seq_lengths: int32 [16, 5], P('dp'), may hold values from 0 to 768, as said below
- attn_in: float32 [3, 768, 768], P(None, 'dp', 'tensor'), may hold values from -0.28867513 to 0.28867513
- attn_out: float32 [768, 768], P('tensor', 'dp'), may hold values from -0.21650635 to 0.21650635
- ffn_up: float32 [768, 3072], P('dp', 'tensor'), may hold values from -0.21650635 to 0.21650635
- ffn_down: float32 [3072, 768], P('tensor', 'dp'), may hold values from -0.108253175 to 0.108253175
- first_attn_in: float32 [3, 768, 768], P(None, 'dp', 'tensor'), may hold values from -40 to 40
- second_attn_in: float32 [3, 768, 768], P(None, 'dp', 'tensor'), may hold values from 131.072 to 524.288
- first_attn_out: float32 [768, 768], P('tensor', 'dp'), may hold values from -128 to 128
- second_attn_out: float32 [768, 768], P('tensor', 'dp'), may hold values from 36.864 to 147.456
- first_ffn_up: float32 [768, 3072], P('dp', 'tensor'), may hold values from -80 to 80
- second_ffn_up: float32 [768, 3072], P('dp', 'tensor'), may hold values from 16.384 to 65.536
- first_ffn_down: float32 [3072, 768], P('tensor', 'dp'), may hold values from -128 to 128
- second_ffn_down: float32 [3072, 768], P('tensor', 'dp'), may hold values from 36.864 to 147.456
- width_norm_params: float32 [6, 768], P(None, 'tensor'), may hold values from -1.1 to 2.6
- first_width_norms: float32 [6, 768], P(None, 'tensor'), may hold values from -128 to 128
- second_width_norms: float32 [6, 768], P(None, 'tensor'), may hold values from 36.864 to 147.456
- hidden_norm_params: float32 [2, 3072], P(None, 'tensor'), may hold values from -1.1 to 2.6
- first_hidden_norms: float32 [2, 3072], P(None, 'tensor'), may hold values from -128 to 128
- second_hidden_norms: float32 [2, 3072], P(None, 'tensor'), may hold values from 36.864 to 147.456
Outputs:
- block_output: float32 [16384, 768], P('dp', 'tensor')
- grad_tokens: float32 [16384, 768], P('dp', 'tensor')
- new_attn_in: float32 [3, 768, 768], P(None, 'dp', 'tensor')
- new_attn_out: float32 [768, 768], P('tensor', 'dp')
- new_ffn_up: float32 [768, 3072], P('dp', 'tensor')
- new_ffn_down: float32 [3072, 768], P('tensor', 'dp')
- moment_attn_in: float32 [3, 768, 768], P(None, 'dp', 'tensor')
- moment_attn_out: float32 [768, 768], P('tensor', 'dp')
- moment_ffn_up: float32 [768, 3072], P('dp', 'tensor')
- moment_ffn_down: float32 [3072, 768], P('tensor', 'dp')
- square_attn_in: float32 [3, 768, 768], P(None, 'dp', 'tensor')
- square_attn_out: float32 [768, 768], P('tensor', 'dp')
- square_ffn_up: float32 [768, 3072], P('dp', 'tensor')
- square_ffn_down: float32 [3072, 768], P('tensor', 'dp')
- new_width_norms: float32 [6, 768], P(None, 'tensor')
- moment_width_norms: float32 [6, 768], P(None, 'tensor')
- square_width_norms: float32 [6, 768], P(None, 'tensor')
- new_hidden_norms: float32 [2, 3072], P(None, 'tensor')
- moment_hidden_norms: float32 [2, 3072], P(None, 'tensor')
- square_hidden_norms: float32 [2, 3072], P(None, 'tensor')
The draws below stay inside these ranges and needn't reach their ends.
Inputs may be any that keep to these rules, and one draw needn't show every extreme that they name: `seq_lengths`: row i lists the lengths of the sequences of pack i in slot order: exactly one is 768, each other is 0 (an empty slot) or a multiple of 64, and the row sums to 1024.
All inputs are finite; a program needn't handle non-finite values.
Results may differ from the reference program's by a relative error of at most 0.014.
The reference program's roundings to bfloat16 on the way count: a program that leaves them out, or rounds other values in their place, can miss the bound.
Values may be sent and summed in bfloat16 or wider, within the bound.
No kernel may reach another device: no remote copies, remote signals or barrier semaphores. Data moves between devices by JAX's collectives and lax.ppermute only.
A program may use at most 128 MiB of HBM per device.

```python
import math
import jax
import jax.numpy as jnp
from jax import lax

MODEL_WIDTH = 768
H = 12
HD = 64
FEEDFORWARD_UNITS = 3072
TOK_DEV = 1024
MINLEN = 64
STEP = 10
MOST = 768
SEQS = 5
TOKENS = 16384
N_DP = 16


def ramp_along(shape, dim, low_end, high_end):
    length = shape[dim]
    fraction = jnp.arange(length, dtype=jnp.float32) / max(length - 1, 1)
    broadcast_shape = [1] * len(shape)
    broadcast_shape[dim] = length
    return (low_end + (high_end - low_end) * fraction).reshape(broadcast_shape)


def ramped_weight(noise, shape, fan_in, dp_dim, tensor_dim, dp_range, tensor_range, factor):
    dp_ramp = ramp_along(shape, dp_dim, dp_range[0], dp_range[1])
    tensor_ramp = ramp_along(shape, tensor_dim, tensor_range[0], tensor_range[1])
    return factor * fan_in ** (-0.5) * noise * dp_ramp * tensor_ramp


def ramped_norms(noise, shape, gain_range):
    parity = (jnp.arange(shape[0]) % 2 == 0)[:, None]
    gains = ramp_along(shape, 1, gain_range[0], gain_range[1]) * (1.0 + 0.15 * noise)
    return jnp.where(parity, gains, 0.3 * noise)


def draw_tokens(key, part):
    key = jax.random.fold_in(key, 11)
    shape = (TOKENS, MODEL_WIDTH)
    noise = jnp.clip(jax.random.normal(key, shape, jnp.float32), -3.5, 3.5)
    return (noise * ramp_along(shape, 1, 0.5, 1.5)).astype(jnp.bfloat16)


def draw_cotangent(key, part):
    key = jax.random.fold_in(key, 12)
    shape = (TOKENS, MODEL_WIDTH)
    noise = jnp.clip(jax.random.normal(key, shape, jnp.float32), -3.5, 3.5)
    return (noise * ramp_along(shape, 1, 0.5, 1.5)).astype(jnp.bfloat16)


def draw_seq_lengths(key, part):
    key = jax.random.fold_in(key, 13)
    pick_key, order_key = jax.random.split(key)
    unit_count = SEQS - 1
    bucket_ids = jax.random.randint(pick_key, (N_DP, unit_count), 0, unit_count)
    counts = jnp.sum((bucket_ids[:, :, None] == jnp.arange(unit_count, dtype=jnp.int32)[None, None, :]).astype(jnp.int32), axis=1)
    slot_lengths = jnp.concatenate([jnp.full((N_DP, 1), MOST, jnp.int32), counts * MINLEN], axis=1)
    slot_order = jax.vmap(lambda sub_key: jax.random.permutation(sub_key, SEQS))(jax.random.split(order_key, N_DP))
    return jnp.take_along_axis(slot_lengths, slot_order, axis=1).astype(jnp.int32)


def weight_noise(key, shape):
    return jnp.clip(jax.random.normal(key, shape, jnp.float32), -3.5, 3.5)


def draw_attn_in(key, part):
    key = jax.random.fold_in(key, 14)
    shape = (3, MODEL_WIDTH, MODEL_WIDTH)
    return ramped_weight(weight_noise(key, shape), shape, MODEL_WIDTH, 1, 2, (0.7, 1.2), (0.6, 1.4), 1.2)


def draw_attn_out(key, part):
    key = jax.random.fold_in(key, 15)
    shape = (MODEL_WIDTH, MODEL_WIDTH)
    return ramped_weight(weight_noise(key, shape), shape, MODEL_WIDTH, 1, 0, (0.7, 1.2), (0.6, 1.4), 1.0)


def draw_ffn_up(key, part):
    key = jax.random.fold_in(key, 16)
    shape = (MODEL_WIDTH, FEEDFORWARD_UNITS)
    return ramped_weight(weight_noise(key, shape), shape, MODEL_WIDTH, 0, 1, (0.7, 1.2), (0.6, 1.4), 1.0)


def draw_ffn_down(key, part):
    key = jax.random.fold_in(key, 17)
    shape = (FEEDFORWARD_UNITS, MODEL_WIDTH)
    return ramped_weight(weight_noise(key, shape), shape, FEEDFORWARD_UNITS, 1, 0, (0.7, 1.2), (0.6, 1.4), 1.0)


def draw_width_norm_params(key, part):
    key = jax.random.fold_in(key, 18)
    shape = (6, MODEL_WIDTH)
    return ramped_norms(weight_noise(key, shape), shape, (0.5, 1.5))


def draw_hidden_norm_params(key, part):
    key = jax.random.fold_in(key, 19)
    shape = (2, FEEDFORWARD_UNITS)
    return ramped_norms(weight_noise(key, shape), shape, (0.5, 1.5))


def steps_of(stream_key, dims, cuts, least, high):
    def one(dim, parts):
        steps = jax.random.uniform(jax.random.fold_in(jax.random.fold_in(stream_key, 6), dim), (parts,), jnp.float32, least / len(cuts), high / len(cuts))
        return jnp.repeat(jnp.exp(steps), dims[dim] // parts).reshape((-1,) + (1,) * (len(dims) - dim - 1))

    level = one(*cuts[0])
    for cut in cuts[1:]:
        level = level * one(*cut)
    return level


def bell_draw(key, dims, width, reach, pieces=(), kind=jnp.bfloat16):
    values = jax.random.normal(key, dims, jnp.float32) * width
    if len(pieces) > 0:
        values = steps_of(key, dims, pieces, -0.22, 0.18) * values
    return jnp.clip(values, min=-reach, max=reach).astype(kind)


def setup_inputs(seed: int = 0) -> dict:
    key_of = jax.random.split(jax.random.key(seed), 22)
    tokens = draw_tokens(jax.random.fold_in(key_of[21], 71), 0)
    cotangent = draw_cotangent(jax.random.fold_in(key_of[21], 71), 0)
    seq_lengths = draw_seq_lengths(jax.random.fold_in(key_of[21], 71), 0)
    attn_in = draw_attn_in(jax.random.fold_in(key_of[21], 71), 0)
    attn_out = draw_attn_out(jax.random.fold_in(key_of[21], 71), 0)
    ffn_up = draw_ffn_up(jax.random.fold_in(key_of[21], 71), 0)
    ffn_down = draw_ffn_down(jax.random.fold_in(key_of[21], 71), 0)
    first_attn_in = bell_draw(key_of[7], (3, MODEL_WIDTH, MODEL_WIDTH), (0.055 * TOKENS ** 0.5), 40.0, ((1, 16), (2, 2)), jnp.float32)
    second_attn_in = jnp.clip(jnp.exp(math.log(524.288) - 1.3862944 * jax.random.uniform(key_of[8], (3, MODEL_WIDTH, MODEL_WIDTH), jnp.float32) ** steps_of(key_of[8], (3, MODEL_WIDTH, MODEL_WIDTH), ((1, 16), (2, 2)), -0.2, 0.2)), 131.072, 524.288)
    first_attn_out = bell_draw(key_of[9], (MODEL_WIDTH, MODEL_WIDTH), (0.165 * TOKENS ** 0.5), 128.0, ((0, 2), (1, 16)), jnp.float32)
    second_attn_out = jnp.clip(jnp.exp(math.log(147.456) - 1.3862944 * jax.random.uniform(key_of[10], (MODEL_WIDTH, MODEL_WIDTH), jnp.float32) ** steps_of(key_of[10], (MODEL_WIDTH, MODEL_WIDTH), ((0, 2), (1, 16)), -0.2, 0.2)), 36.864, 147.456)
    first_ffn_up = bell_draw(key_of[11], (MODEL_WIDTH, FEEDFORWARD_UNITS), (0.11 * TOKENS ** 0.5), 80.0, ((0, 16), (1, 2)), jnp.float32)
    second_ffn_up = jnp.clip(jnp.exp(math.log(65.536) - 1.3862944 * jax.random.uniform(key_of[12], (MODEL_WIDTH, FEEDFORWARD_UNITS), jnp.float32) ** steps_of(key_of[12], (MODEL_WIDTH, FEEDFORWARD_UNITS), ((0, 16), (1, 2)), -0.2, 0.2)), 16.384, 65.536)
    first_ffn_down = bell_draw(key_of[13], (FEEDFORWARD_UNITS, MODEL_WIDTH), (0.165 * TOKENS ** 0.5), 128.0, ((0, 2), (1, 16)), jnp.float32)
    second_ffn_down = jnp.clip(jnp.exp(math.log(147.456) - 1.3862944 * jax.random.uniform(key_of[14], (FEEDFORWARD_UNITS, MODEL_WIDTH), jnp.float32) ** steps_of(key_of[14], (FEEDFORWARD_UNITS, MODEL_WIDTH), ((0, 2), (1, 16)), -0.2, 0.2)), 36.864, 147.456)
    width_norm_params = draw_width_norm_params(jax.random.fold_in(key_of[21], 71), 0)
    first_width_norms = bell_draw(key_of[16], (6, MODEL_WIDTH), (0.165 * TOKENS ** 0.5), 128.0, ((1, 2),), jnp.float32)
    second_width_norms = jnp.clip(jnp.exp(math.log(147.456) - 1.3862944 * jax.random.uniform(key_of[17], (6, MODEL_WIDTH), jnp.float32) ** steps_of(key_of[17], (6, MODEL_WIDTH), ((1, 2),), -0.2, 0.2)), 36.864, 147.456)
    hidden_norm_params = draw_hidden_norm_params(jax.random.fold_in(key_of[21], 71), 0)
    first_hidden_norms = bell_draw(key_of[19], (2, FEEDFORWARD_UNITS), (0.165 * TOKENS ** 0.5), 128.0, ((1, 2),), jnp.float32)
    second_hidden_norms = jnp.clip(jnp.exp(math.log(147.456) - 1.3862944 * jax.random.uniform(key_of[20], (2, FEEDFORWARD_UNITS), jnp.float32) ** steps_of(key_of[20], (2, FEEDFORWARD_UNITS), ((1, 2),), -0.2, 0.2)), 36.864, 147.456)
    return dict(tokens=tokens, cotangent=cotangent, seq_lengths=seq_lengths, attn_in=attn_in, attn_out=attn_out, ffn_up=ffn_up, ffn_down=ffn_down, first_attn_in=first_attn_in, second_attn_in=second_attn_in, first_attn_out=first_attn_out, second_attn_out=second_attn_out, first_ffn_up=first_ffn_up, second_ffn_up=second_ffn_up, first_ffn_down=first_ffn_down, second_ffn_down=second_ffn_down, width_norm_params=width_norm_params, first_width_norms=first_width_norms, second_width_norms=second_width_norms, hidden_norm_params=hidden_norm_params, first_hidden_norms=first_hidden_norms, second_hidden_norms=second_hidden_norms)


EPS_NORM = 1e-05
BETA_ONE = 0.9
BETA_TWO = 0.999
EPS_ADAM = 1e-06
DECAY = 0.01
RATE = 0.25
MASKED = -1e+30
HIGH = lax.Precision.HIGHEST

@jax.custom_vjp
def low(v):
    return lax.optimization_barrier(v.astype(jnp.bfloat16)).astype(jnp.float32)

@jax.custom_vjp
def low_back(v):
    return v

def low_keep(v):
    return (low(v), None)

def low_pass(kept, grad):
    return (grad,)

def back_keep(v):
    return (v, None)

def back_low(kept, grad):
    return (low(grad),)
low.defvjp(low_keep, low_pass)
low_back.defvjp(back_keep, back_low)

def layer_norm(source, gain_row, bias_row):
    row_mean = lax.optimization_barrier(jnp.mean(source, axis=-1, keepdims=True))
    centred = source - row_mean
    variance = lax.optimization_barrier(jnp.mean(centred * centred, axis=-1, keepdims=True))
    return centred * lax.rsqrt(variance + EPS_NORM) * gain_row + bias_row

def pack_layer(weights, tokens, lengths):
    attn_in, attn_out, ffn_up, ffn_down, width_norm_params, hidden_norm_params = weights
    tok_rows = tokens.shape[0]
    seq_ends = jnp.cumsum(lengths)
    position = jnp.arange(tok_rows, dtype=jnp.int32)
    segment = lax.optimization_barrier(jnp.sum((position[:, None] >= seq_ends[None, :]).astype(jnp.int32), axis=1))
    allowed = (segment[:, None] == segment[None, :]) & (position[None, :] <= position[:, None])
    normed_in = low(layer_norm(tokens, width_norm_params[0], width_norm_params[1]))
    mixed = jnp.einsum('pd,cdf->cpf', normed_in, attn_in, precision=HIGH)
    query = low_back(low(mixed[0])).reshape(tok_rows, H, HD)
    key_heads = low_back(low(mixed[1])).reshape(tok_rows, H, HD)
    value_heads = low_back(low(mixed[2])).reshape(tok_rows, H, HD)
    scores = low_back(jnp.einsum('qhd,khd->hqk', query, key_heads, precision=HIGH) * HD ** (-0.5))
    scores = jnp.where(allowed[None], scores, MASKED)
    attn_probs = low(jax.nn.softmax(scores, axis=-1))
    attention_result = jnp.einsum('hqk,khd->qhd', attn_probs, value_heads, precision=HIGH).reshape(tok_rows, H * HD)
    attention_result = low_back(attention_result)
    inner_rows = low(layer_norm(attention_result, width_norm_params[2], width_norm_params[3]))
    residual_stream = tokens + low_back(jnp.dot(inner_rows, attn_out, precision=HIGH))
    normed_mid = low(layer_norm(residual_stream, width_norm_params[4], width_norm_params[5]))
    raised = low_back(jnp.dot(normed_mid, ffn_up, precision=HIGH))
    hidden_rows = low(layer_norm(jax.nn.gelu(raised, approximate=False), hidden_norm_params[0], hidden_norm_params[1]))
    return residual_stream + low_back(jnp.dot(hidden_rows, ffn_down, precision=HIGH))

def forward(tokens, attn_in, attn_out, ffn_up, ffn_down, width_norm_params, hidden_norm_params, lengths):
    weights = (low(attn_in), low(attn_out), low(ffn_up), low(ffn_down), width_norm_params, hidden_norm_params)
    packs = tokens.reshape(N_DP, TOK_DEV, MODEL_WIDTH)
    layer = jax.checkpoint(pack_layer)
    result = lax.map(lambda item: layer(weights, item[0], item[1]), (packs, lengths))
    return result.reshape(N_DP * TOK_DEV, MODEL_WIDTH)

def adam_moments(grad, first, second):
    new_first = BETA_ONE * first + (1.0 - BETA_ONE) * grad
    new_second = BETA_TWO * second + (1.0 - BETA_TWO) * grad * grad
    step_dir = new_first / (1.0 - BETA_ONE ** STEP) / (jnp.sqrt(new_second / (1.0 - BETA_TWO ** STEP)) + EPS_ADAM)
    return (new_first, new_second, step_dir)

def lamb_matrix(master, grad, first, second):
    new_first, new_second, step_dir = adam_moments(grad, first, second)
    update = step_dir + DECAY * master
    ratio = jnp.sqrt(jnp.sum(master * master) / (jnp.sum(update * update) + 1e-06))
    return (master - RATE * ratio * update, new_first, new_second)

def lamb_rows(master, grad, first, second):
    new_first, new_second, step_dir = adam_moments(grad, first, second)
    ratio = jnp.sqrt(lax.optimization_barrier(jnp.sum(master * master, axis=1, keepdims=True)) / (lax.optimization_barrier(jnp.sum(step_dir * step_dir, axis=1, keepdims=True)) + 1e-06))
    return (master - RATE * ratio * step_dir, new_first, new_second)

def reference(tokens, cotangent, seq_lengths, attn_in, attn_out, ffn_up, ffn_down, first_attn_in, second_attn_in, first_attn_out, second_attn_out, first_ffn_up, second_ffn_up, first_ffn_down, second_ffn_down, width_norm_params, first_width_norms, second_width_norms, hidden_norm_params, first_hidden_norms, second_hidden_norms):

    def run(tok_in, w_in, w_out, w_up, w_down, norms_width, norms_hidden):
        return forward(tok_in, w_in, w_out, w_up, w_down, norms_width, norms_hidden, seq_lengths)
    block_output, pull = jax.vjp(run, tokens.astype(jnp.float32), attn_in, attn_out, ffn_up, ffn_down, width_norm_params, hidden_norm_params)
    grads = pull(cotangent.astype(jnp.float32))
    grad_tokens = grads[0]
    new_in, moment_in, square_in = lamb_matrix(attn_in, grads[1], first_attn_in, second_attn_in)
    new_out, moment_out, square_out = lamb_matrix(attn_out, grads[2], first_attn_out, second_attn_out)
    new_up, moment_up, square_up = lamb_matrix(ffn_up, grads[3], first_ffn_up, second_ffn_up)
    new_down, moment_down, square_down = lamb_matrix(ffn_down, grads[4], first_ffn_down, second_ffn_down)
    new_width, moment_width, square_width = lamb_rows(width_norm_params, grads[5], first_width_norms, second_width_norms)
    new_hidden, moment_hidden, square_hidden = lamb_rows(hidden_norm_params, grads[6], first_hidden_norms, second_hidden_norms)
    return (block_output, grad_tokens, new_in, new_out, new_up, new_down, moment_in, moment_out, moment_up, moment_down, square_in, square_out, square_up, square_down, new_width, moment_width, square_width, new_hidden, moment_hidden, square_hidden)
```

```python
import jax
import jax.numpy as jnp
from jax import lax
from jax.sharding import PartitionSpec as P

MODEL_WIDTH = 768
HD = 64
FEEDFORWARD_UNITS = 3072
STEP = 10


EPS_NORM = 1e-05
BETA_ONE = 0.9
BETA_TWO = 0.999
EPS_ADAM = 1e-06
DECAY = 0.01
RATE = 0.25
MASKED = -1e30
LOW = jnp.bfloat16
F32 = jnp.float32


def dp_digits(count):
    if count == 16:
        return (4, 2, 2)
    if count == 128:
        return (4, 4, 8)
    return (count, 1, 1)


class Ring:
    def __init__(self, count):
        self.digits = dp_digits(count)
        self.strides = (self.digits[1] * self.digits[2], self.digits[2], 1)
        self.count = count

    def place(self, dim):
        return (lax.axis_index("dp") // self.strides[dim]) % self.digits[dim]

    def offsets(self, dim):
        return range(1, self.digits[dim])

    def send(self, source, dim, offset):
        radix, stride = self.digits[dim], self.strides[dim]
        pairs = []
        for device in range(self.count):
            digit = (device // stride) % radix
            partner = digit ^ offset if radix & (radix - 1) == 0 else (digit + offset) % radix
            pairs.append((device, device + (partner - digit) * stride))
        return lax.ppermute(source, "dp", pairs)

    def there(self, place, dim, offset, back):
        radix = self.digits[dim]
        if radix & (radix - 1) == 0:
            return place ^ offset
        return (place - offset) % radix if back else (place + offset) % radix

    def gather(self, source, dim):
        radix = self.digits[dim]
        if radix == 1:
            return source[None]
        here = self.place(dim)
        arrived = [source] + [self.send(source, dim, offset) for offset in self.offsets(dim)]
        if radix == 2:
            first = jnp.where(here == 0, arrived[0], arrived[1])
            second = jnp.where(here == 0, arrived[1], arrived[0])
            return jnp.stack([first, second])
        whole = jnp.zeros((radix,) + source.shape, source.dtype)
        for offset, block in enumerate(arrived):
            owner = self.there(here, dim, offset, True)
            whole = lax.dynamic_update_index_in_dim(whole, block, owner, 0)
        return whole

    def reduce(self, source, axis, dim):
        radix = self.digits[dim]
        if radix == 1:
            return lax.index_in_dim(source, 0, axis, keepdims=False)
        here = self.place(dim)
        total = lax.dynamic_index_in_dim(source, here, axis, keepdims=False)
        for offset in self.offsets(dim):
            owner = self.there(here, dim, offset, False)
            part = lax.dynamic_index_in_dim(source, owner, axis, keepdims=False).astype(LOW)
            total = total + self.send(part, dim, offset).astype(F32)
        return total

    def all_sum(self, source):
        for dim in (2, 1, 0):
            radix = self.digits[dim]
            if radix & (radix - 1) == 0:
                offset = 1
                while offset < radix:
                    source = source + self.send(source, dim, offset)
                    offset *= 2
            else:
                source = source + sum(
                    self.send(source, dim, offset) for offset in self.offsets(dim)
                )
        return source


def cut_of(columns):
    return (columns // 256) * 128


def gather_rows(ring, source):
    rows, columns = source.shape
    cut = cut_of(columns)
    whole = ring.gather(source, 0)
    left, right = whole[..., :cut], whole[..., cut:]
    left = ring.gather(ring.gather(left, 2), 1)
    right = ring.gather(ring.gather(right, 1), 2)
    left = jnp.transpose(left, (2, 0, 1, 3, 4))
    right = jnp.transpose(right, (2, 1, 0, 3, 4))
    return jnp.concatenate([left, right], axis=4).reshape(ring.count * rows, columns)


def scatter_rows(ring, source):
    rows, columns = source.shape
    cut = cut_of(columns)
    blocks = source.reshape(*ring.digits, rows // ring.count, columns)
    left, right = blocks[..., :cut], blocks[..., cut:]
    left = ring.reduce(ring.reduce(left, 1, 1), 1, 2)
    right = ring.reduce(ring.reduce(right, 2, 2), 1, 1)
    return ring.reduce(jnp.concatenate([left, right], axis=2), 0, 0)


def swap(source):
    return lax.ppermute(source, "tensor", [(0, 1), (1, 0)])


def ordered(mine, other, axis):
    core = lax.axis_index("tensor")
    return jnp.where(
        core == 0,
        jnp.concatenate([mine, other], axis=axis),
        jnp.concatenate([other, mine], axis=axis),
    )


def half(source, axis, which):
    size = source.shape[axis] // 2
    return lax.dynamic_slice_in_dim(source, which * size, size, axis)


def norm_stats(source):
    width = source.shape[1]
    centred = source - jnp.sum(source, axis=1, keepdims=True) / width
    inv_std = lax.rsqrt(jnp.sum(centred * centred, axis=1, keepdims=True) / width + EPS_NORM)
    return centred * inv_std, inv_std


def norm_backward(grad_out, normed, inv_std, gain_row):
    width = normed.shape[1]
    scaled = grad_out * gain_row
    sum_plain = jnp.sum(scaled, axis=1, keepdims=True) / width
    sum_cross = jnp.sum(scaled * normed, axis=1, keepdims=True) / width
    return inv_std * (scaled - sum_plain - normed * sum_cross)


def norm_sums(grad_out, normed):
    return jnp.stack([jnp.sum(grad_out * normed, axis=0), jnp.sum(grad_out, axis=0)])


def adam_moments(grad, first, second):
    new_first = BETA_ONE * first + (1.0 - BETA_ONE) * grad
    new_second = BETA_TWO * second + (1.0 - BETA_TWO) * grad * grad
    step_dir = (
        new_first
        / (1.0 - BETA_ONE**STEP)
        / (jnp.sqrt(new_second / (1.0 - BETA_TWO**STEP)) + EPS_ADAM)
    )
    return (new_first, new_second, step_dir)


def dot(left, right, dims):
    return lax.dot_general(left, right, (dims, ((), ())), preferred_element_type=F32)


NN = ((1,), (0,))
NT = ((1,), (1,))
TN = ((0,), (0,))


def shards(
    ring,
    tokens,
    cotangent,
    seq_lengths,
    attn_in,
    attn_out,
    ffn_up,
    ffn_down,
    first_attn_in,
    second_attn_in,
    first_attn_out,
    second_attn_out,
    first_ffn_up,
    second_ffn_up,
    first_ffn_down,
    second_ffn_down,
    width_norm_params,
    first_width_norms,
    second_width_norms,
    hidden_norm_params,
    first_hidden_norms,
    second_hidden_norms,
):
    core = lax.axis_index("tensor")
    tok_rows, half_width = tokens.shape
    heads_local = half_width // HD
    half_hidden = ffn_up.shape[1]
    block_rows = min(512, tok_rows)
    block_count = tok_rows // block_rows
    head_scale = HD ** (-0.5)

    shard_in = jnp.transpose(attn_in, (1, 0, 2)).reshape(attn_in.shape[1], -1).astype(LOW)
    shard_mid = jnp.concatenate([ffn_up, attn_out.T], axis=1).astype(LOW)
    shard_down = ffn_down.T.astype(LOW)
    half_in = gather_rows(ring, shard_in)
    half_mid = gather_rows(ring, shard_mid)
    half_down = gather_rows(ring, shard_down)

    tokens_all = ordered(tokens, swap(tokens), 1)
    cotangent_all = ordered(cotangent, swap(cotangent), 1)
    width_params = ordered(width_norm_params, swap(width_norm_params), 1)
    hidden_params = ordered(hidden_norm_params, swap(hidden_norm_params), 1)

    seq_ends = jnp.cumsum(seq_lengths[0])
    position = jnp.arange(tok_rows, dtype=jnp.int32)
    segment = jnp.sum((position[:, None] >= seq_ends[None, :]).astype(jnp.int32), axis=1)
    seg_blocks = segment.reshape(block_count, block_rows)
    pos_blocks = position.reshape(block_count, block_rows)

    input_rows = tokens_all.astype(F32)
    normed_one, inv_one = norm_stats(input_rows)
    feat_one = (normed_one * width_params[0] + width_params[1]).astype(LOW)
    mixed = dot(feat_one, half_in, NN).astype(LOW)
    query_heads = mixed[:, :half_width].reshape(tok_rows, heads_local, HD)
    key_heads = mixed[:, half_width : 2 * half_width].reshape(tok_rows, heads_local, HD)
    value_heads = mixed[:, 2 * half_width :].reshape(tok_rows, heads_local, HD)
    query_blocks = query_heads.reshape(block_count, block_rows, heads_local, HD)

    def masked_scores(query, seg_rows, pos_rows):
        scores = (
            jnp.einsum("qhd,khd->hqk", query, key_heads, preferred_element_type=F32) * head_scale
        )
        allowed = (seg_rows[:, None] == segment[None, :]) & (position[None, :] <= pos_rows[:, None])
        return jnp.where(allowed[None], scores, MASKED)

    def forward_block(items):
        query, seg_rows, pos_rows = items
        scores = masked_scores(query, seg_rows, pos_rows)
        row_max = jnp.max(scores, axis=2, keepdims=True)
        log_total = row_max + jnp.log(jnp.sum(jnp.exp(scores - row_max), axis=2, keepdims=True))
        attn_probs = jnp.exp(scores - log_total)
        result = jnp.einsum(
            "hqk,khd->qhd", attn_probs.astype(LOW), value_heads, preferred_element_type=F32
        )
        return (result, log_total[..., 0])

    attn_blocks, log_totals = lax.map(forward_block, (query_blocks, seg_blocks, pos_blocks))
    attended_heads = attn_blocks.reshape(tok_rows, half_width)

    attended = ordered(half(attended_heads, 0, core), swap(half(attended_heads, 0, 1 - core)), 1)
    out_t = ordered(half_mid[:, half_hidden:], swap(half_mid[:, half_hidden:]), 1)
    up_all = ordered(half_mid[:, :half_hidden], swap(half_mid[:, :half_hidden]), 1)
    down_t = ordered(half_down, swap(half_down), 1)

    normed_att, inv_att = norm_stats(attended)
    inner_low = (normed_att * width_params[2] + width_params[3]).astype(LOW)
    token_rows = half(input_rows, 0, core)
    residual = token_rows + dot(inner_low, out_t, NT)
    normed_two, inv_two = norm_stats(residual)
    feat_two = (normed_two * width_params[4] + width_params[5]).astype(LOW)
    raised = dot(feat_two, up_all, NN)
    active, gelu_pull = jax.vjp(lambda source: jax.nn.gelu(source, approximate=False), raised)
    normed_hid, inv_hid = norm_stats(active)
    hidden_low = (normed_hid * hidden_params[0] + hidden_params[1]).astype(LOW)
    output_rows = residual + dot(hidden_low, down_t, NT)
    block_output = ordered(
        half(output_rows, 1, core), swap(half(output_rows, 1, 1 - core)), 0
    )

    cot_rows = half(cotangent_all, 0, core)
    hidden_both = ordered(half(hidden_low, 1, core), swap(half(hidden_low, 1, 1 - core)), 0)
    grad_down_t = dot(cotangent_all, hidden_both, TN)
    red_down_t = scatter_rows(ring, grad_down_t)

    grad_hidden = dot(cot_rows, down_t, NN)
    sums_hidden = norm_sums(grad_hidden, normed_hid)
    grad_active = norm_backward(grad_hidden, normed_hid, inv_hid, hidden_params[0])
    grad_raised = gelu_pull(grad_active)[0].astype(LOW)
    grad_mid = dot(grad_raised, up_all, NT)
    sums_two = norm_sums(grad_mid, normed_two)
    grad_residual = cot_rows.astype(F32) + norm_backward(
        grad_mid, normed_two, inv_two, width_params[4]
    )
    grad_res_low = grad_residual.astype(LOW)
    grad_inner = dot(grad_res_low, out_t, NN)
    sums_att = norm_sums(grad_inner, normed_att)
    grad_attended = norm_backward(grad_inner, normed_att, inv_att, width_params[2]).astype(LOW)

    feat_two_both = ordered(feat_two, swap(feat_two), 0)
    raised_both = ordered(half(grad_raised, 1, core), swap(half(grad_raised, 1, 1 - core)), 0)
    inner_both = ordered(half(inner_low, 1, core), swap(half(inner_low, 1, 1 - core)), 0)
    grad_res_both = ordered(grad_res_low, swap(grad_res_low), 0)
    grad_mid_w = jnp.concatenate(
        [dot(feat_two_both, raised_both, TN), dot(grad_res_both, inner_both, TN)], axis=1
    )
    red_mid = scatter_rows(ring, grad_mid_w)

    grad_att_heads = ordered(
        half(grad_attended, 1, core), swap(half(grad_attended, 1, 1 - core)), 0
    )
    grad_att_blocks = grad_att_heads.reshape(block_count, block_rows, heads_local, HD)

    def back_block(carry, items):
        grad_keys, grad_values = carry
        query, grad_o, log_total, seg_rows, pos_rows = items
        scores = masked_scores(query, seg_rows, pos_rows)
        attn_probs = jnp.exp(scores - log_total[..., None])
        probs_low = attn_probs.astype(LOW)
        grad_p = jnp.einsum("qhd,khd->hqk", grad_o, value_heads, preferred_element_type=F32)
        grad_scores = attn_probs * (grad_p - jnp.sum(attn_probs * grad_p, axis=2, keepdims=True))
        grad_scores_low = grad_scores.astype(LOW)
        grad_query = (
            jnp.einsum("hqk,khd->qhd", grad_scores_low, key_heads, preferred_element_type=F32)
            * head_scale
        )
        grad_keys = (
            grad_keys
            + jnp.einsum("hqk,qhd->khd", grad_scores_low, query, preferred_element_type=F32)
            * head_scale
        )
        grad_values = grad_values + jnp.einsum(
            "hqk,qhd->khd", probs_low, grad_o, preferred_element_type=F32
        )
        return ((grad_keys, grad_values), grad_query)

    zero_heads = jnp.zeros((tok_rows, heads_local, HD), F32)
    (grad_keys, grad_values), grad_queries = lax.scan(
        back_block,
        (zero_heads, zero_heads),
        (query_blocks, grad_att_blocks, log_totals, seg_blocks, pos_blocks),
    )
    grad_mixed = jnp.concatenate(
        [
            grad_queries.reshape(tok_rows, half_width),
            grad_keys.reshape(tok_rows, half_width),
            grad_values.reshape(tok_rows, half_width),
        ],
        axis=1,
    ).astype(LOW)
    red_in_rows = scatter_rows(ring, dot(feat_one, grad_mixed, TN))
    grad_first = dot(grad_mixed, half_in, NT)
    sums_one = norm_sums(grad_first, normed_one)
    grad_first_rows = half(grad_first, 0, core) + swap(half(grad_first, 0, 1 - core))
    grad_token_rows = grad_residual + norm_backward(
        grad_first_rows, half(normed_one, 0, core), half(inv_one, 0, core), width_params[0]
    )
    grad_tokens = ordered(
        half(grad_token_rows, 1, core), swap(half(grad_token_rows, 1, 1 - core)), 0
    )

    sums_width = jnp.concatenate([sums_one, sums_att, sums_two])
    sums_width = half(sums_width, 1, core) + swap(half(sums_width, 1, 1 - core))
    sums_hid = half(sums_hidden, 1, core) + swap(half(sums_hidden, 1, 1 - core))
    packed = jnp.concatenate([sums_width.reshape(-1, 128), sums_hid.reshape(-1, 128)])
    packed = ring.all_sum(packed)
    width_rows = sums_width.size // 128
    red_width = packed[:width_rows].reshape(sums_width.shape)
    red_hidden = packed[width_rows:].reshape(sums_hid.shape)

    red_in = jnp.transpose(red_in_rows.reshape(-1, 3, half_width), (1, 0, 2))
    red_up = red_mid[:, :half_hidden]
    red_out = red_mid[:, half_hidden:].T
    red_down = red_down_t.T

    masters = (attn_in, attn_out, ffn_up, ffn_down)
    reduced = (red_in, red_out, red_up, red_down)
    firsts = (first_attn_in, first_attn_out, first_ffn_up, first_ffn_down)
    seconds = (second_attn_in, second_attn_out, second_ffn_up, second_ffn_down)
    states = [adam_moments(reduced[index], firsts[index], seconds[index]) for index in range(4)]
    updates = [states[index][2] + DECAY * masters[index] for index in range(4)]
    width_state = adam_moments(red_width, first_width_norms, second_width_norms)
    hidden_state = adam_moments(red_hidden, first_hidden_norms, second_hidden_norms)
    matrix_squares = jnp.stack(
        [jnp.sum(matrix * matrix) for matrix in masters]
        + [jnp.sum(matrix * matrix) for matrix in updates]
    )
    norm_squares = jnp.concatenate(
        [
            jnp.sum(width_norm_params * width_norm_params, axis=1),
            jnp.sum(hidden_norm_params * hidden_norm_params, axis=1),
            jnp.sum(width_state[2] * width_state[2], axis=1),
            jnp.sum(hidden_state[2] * hidden_state[2], axis=1),
        ]
    )
    matrix_squares = ring.all_sum(matrix_squares)
    squares = jnp.concatenate([matrix_squares, norm_squares])
    squares = squares + swap(squares)
    ratio = jnp.sqrt(squares[0:4] / (squares[4:8] + 1e-06))
    norm_ratio = jnp.sqrt(squares[8:16] / (squares[16:24] + 1e-06))
    new_masters = [masters[index] - RATE * ratio[index] * updates[index] for index in range(4)]
    new_width = width_norm_params - RATE * norm_ratio[0:6][:, None] * width_state[2]
    new_hidden = hidden_norm_params - RATE * norm_ratio[6:8][:, None] * hidden_state[2]
    return (
        block_output,
        grad_tokens,
        new_masters[0],
        new_masters[1],
        new_masters[2],
        new_masters[3],
        states[0][0],
        states[1][0],
        states[2][0],
        states[3][0],
        states[0][1],
        states[1][1],
        states[2][1],
        states[3][1],
        new_width,
        width_state[0],
        width_state[1],
        new_hidden,
        hidden_state[0],
        hidden_state[1],
    )


def solution(mesh):
    rows = P("dp", "tensor")
    stacked = P(None, "dp", "tensor")
    turned = P("tensor", "dp")
    narrow = P(None, "tensor")
    in_specs = (
        (rows, rows, P("dp", None), stacked, turned, rows, turned)
        + (stacked, stacked, turned, turned, rows, rows, turned, turned)
        + (narrow,) * 6
    )
    out_specs = (rows, rows) + (stacked, turned, rows, turned) * 3 + (narrow,) * 6
    ring = Ring(mesh.shape["dp"])

    def body(*arrays):
        return shards(ring, *arrays)

    return jax.shard_map(
        body, mesh=mesh, in_specs=in_specs, out_specs=out_specs, check_vma=False
    )
```

```python
import functools

import jax
import jax.numpy as jnp
from jax import lax
from jax.experimental import pallas as pl
from jax.experimental.pallas import tpu as pltpu
from jax.sharding import PartitionSpec as P

HD = 64
STEP = 10
EPS_NORM = 1e-05
BETA_ONE = 0.9
BETA_TWO = 0.999
EPS_ADAM = 1e-06
DECAY = 0.01
RATE = 0.25
MASKED = -1e30
ROOT_HALF = 0.7071067811865476
ROOT_TURN = 0.3989422804014327
LOW = jnp.bfloat16
F32 = jnp.float32
MIB = 2**20
RATE_FLOPS = 1_150_000_000

NN = ((1,), (0,))
NT = ((1,), (1,))
TN = ((0,), (0,))


def dot(left, right, dims):
    return lax.dot_general(left, right, (dims, ((), ())), preferred_element_type=F32)


def dp_digits(count):
    if count == 16:
        return (4, 2, 2)
    if count == 128:
        return (4, 4, 8)
    raise ValueError("dp size")


class Ring:
    def __init__(self, count):
        self.digits = dp_digits(count)
        self.strides = (self.digits[1] * self.digits[2], self.digits[2], 1)
        self.count = count

    def place(self, dim):
        return (lax.axis_index("dp") // self.strides[dim]) % self.digits[dim]

    def offsets(self, dim):
        return range(1, self.digits[dim])

    def send(self, source, dim, offset):
        radix, stride = self.digits[dim], self.strides[dim]
        pairs = []
        for device in range(self.count):
            digit = (device // stride) % radix
            pairs.append((device, device + ((digit ^ offset) - digit) * stride))
        return lax.ppermute(source, "dp", pairs)

    def spread(self, source, dim):
        return [source] + [self.send(source, dim, offset) for offset in self.offsets(dim)]

    def all_sum(self, source):
        for dim in (2, 1, 0):
            offset = 1
            while offset < self.digits[dim]:
                source = source + self.send(source, dim, offset)
                offset *= 2
        return source


def put(whole, block, *places):
    index = tuple(places) + (0,) * (whole.ndim - len(places))
    return lax.dynamic_update_slice(whole, block, index)


def pick(source, place, axis):
    return lax.dynamic_index_in_dim(source, place, axis, keepdims=False)


def tie(*values):
    return lax.optimization_barrier(values)


class Gather:
    def __init__(self, ring, cut, flip):
        self.ring, self.cut, self.flip = ring, cut, flip

    def along_first(self, source):
        ring = self.ring
        whole = jnp.zeros((ring.digits[0],) + source.shape, source.dtype)
        here = ring.place(0) ^ self.flip
        for offset, block in enumerate(ring.spread(source, 0)):
            whole = put(whole, block[None], here ^ offset)
        return whole

    def step_one(self, line):
        parts = (line[..., : self.cut], line[..., self.cut :])
        return [
            jnp.stack(self.ring.spread(part, dim)) for part, dim in zip(parts, (2, 1))
        ]

    def step_two(self, stacks):
        return [self.ring.spread(stack, dim) for stack, dim in zip(stacks, (1, 2))]

    def finish(self, arrived):
        return [self.ordered(part, dim) for part, dim in zip(arrived, (2, 1))]

    def ordered(self, arrived, first):
        ring, second = self.ring, 3 - first
        here = {1: ring.place(1), 2: ring.place(2)}
        inner_count, depth, rows, columns = arrived[0].shape
        whole = jnp.zeros(
            (depth, ring.digits[1], ring.digits[2], rows, columns), arrived[0].dtype
        )
        for offset, blocks in enumerate(arrived):
            for inner in range(inner_count):
                at = {first: here[first] ^ inner, second: here[second] ^ offset}
                whole = put(whole, blocks[inner][:, None, None], 0, at[1], at[2])
        return whole.reshape(ring.count * rows, columns)


class Scatter:
    def __init__(self, ring, cut, flip):
        self.ring, self.cut, self.flip = ring, cut, flip

    def parts(self, source, axis, dim, flip=0):
        here = self.ring.place(dim) ^ flip
        own = pick(source, here, axis).astype(F32)
        sends = [pick(source, here ^ offset, axis).astype(LOW) for offset in self.ring.offsets(dim)]
        return own, sends

    def reduce(self, source, axis, dim, flip=0):
        own, sends = self.parts(source, axis, dim, flip)
        for offset, part in zip(self.ring.offsets(dim), sends):
            own = own + self.ring.send(part, dim, offset).astype(F32)
        return own

    def step_one(self, source):
        rows, columns = source.shape
        blocks = source.reshape(*self.ring.digits, rows // self.ring.count, columns)
        left = self.reduce(blocks[..., : self.cut], 1, 1)
        right = self.reduce(blocks[..., self.cut :], 2, 2)
        return left, right

    def step_two(self, sums):
        left, right = sums
        return jnp.concatenate([self.reduce(left, 1, 2), self.reduce(right, 1, 1)], axis=2)

    def along_first(self, line):
        return self.reduce(line, 0, 0, self.flip)


def swap(source):
    return lax.ppermute(source, "tensor", [(0, 1), (1, 0)])


def in_token_order(mine, other):
    whole = jnp.zeros((2,) + mine.shape, mine.dtype)
    core = lax.axis_index("tensor")
    return put(put(whole, mine[None], core), other[None], 1 - core).reshape(-1, mine.shape[1])


def norm_of(source):
    width = source.shape[1]
    centred = source - jnp.sum(source, axis=1, keepdims=True) * (1.0 / width)
    variance = jnp.sum(centred * centred, axis=1, keepdims=True) * (1.0 / width)
    inv_std = lax.rsqrt(variance + EPS_NORM)
    return centred * inv_std, inv_std


def norm_back(grad_out, normed, inv_std, gain_row):
    width = normed.shape[1]
    scaled = grad_out * gain_row
    mean_plain = jnp.sum(scaled, axis=1, keepdims=True) * (1.0 / width)
    mean_cross = jnp.sum(scaled * normed, axis=1, keepdims=True) * (1.0 / width)
    return inv_std * (scaled - mean_plain - normed * mean_cross)


def joined(mine_ref, other_ref):
    return jnp.concatenate([mine_ref[...], other_ref[...]], axis=1)


def whole_block(array):
    zeros = (0,) * array.ndim
    return pl.BlockSpec(array.shape, lambda *_: zeros, pipeline_mode=pl.Buffered(1))


def cost(micros):
    return pl.CostEstimate(flops=micros * RATE_FLOPS, bytes_accessed=0, transcendentals=0)


def like(*shape, dtype=F32):
    return jax.ShapeDtypeStruct(shape, dtype)


def rows_of(block, columns, shift=None):
    if shift is None:
        return pl.BlockSpec((block, columns), lambda i, core: (i, 0))
    return pl.BlockSpec((block, columns), lambda i, core: (i + core[0] * shift, 0))


def qkv_body(core, mine_ref, other_ref, norms_ref, left_ref, right_ref, mixed_ref, feat_ref):
    normed, _ = norm_of(joined(mine_ref, other_ref).astype(F32))
    feat = (normed * norms_ref[0:1, :] + norms_ref[1:2, :]).astype(LOW)
    feat_ref[...] = feat
    result = jnp.concatenate(
        [dot(feat, left_ref[...], NN).astype(LOW), dot(feat, right_ref[...], NN).astype(LOW)],
        axis=1,
    )
    width = mixed_ref.shape[2]
    for part in range(3):
        mixed_ref[part] = result[:, part * width : (part + 1) * width]


def qkv_forward(core, mine, other, norms, left, right):
    rows, width = mine.shape
    block = min(256, rows)
    return pl.pallas_call(
        qkv_body,
        grid_spec=pltpu.PrefetchScalarGridSpec(
            num_scalar_prefetch=1,
            grid=(rows // block,),
            in_specs=[
                rows_of(block, width),
                rows_of(block, width),
                whole_block(norms),
                whole_block(left),
                whole_block(right),
            ],
            out_specs=[
                pl.BlockSpec((3, block, width), lambda i, core: (0, i, 0)),
                rows_of(block, 2 * width),
            ],
        ),
        out_shape=[like(3, rows, width, dtype=LOW), like(rows, 2 * width, dtype=LOW)],
        compiler_params=pltpu.CompilerParams(vmem_limit_bytes=24 * MIB),
        cost_estimate=cost(5),
        name="qkv_forward",
    )(core, mine, other, norms, left, right)


def write_bias(ends_ref, bias_ref, block):
    for at in range(0, bias_ref.shape[1], block):
        keys = at + block
        place = at + lax.broadcasted_iota(jnp.int32, (1, block), 1)
        start = jnp.zeros_like(place)
        for slot in range(ends_ref.shape[0]):
            end = ends_ref[slot]
            start = jnp.maximum(start, jnp.where(end <= place, end, 0))
        key_place = lax.broadcasted_iota(jnp.int32, (keys, block), 0)
        visible = (key_place >= start) & (key_place <= place)
        bias_ref[0:keys, at : at + block] = jnp.where(visible, 0.0, MASKED)


def per_head(source):
    lane = lax.broadcasted_iota(jnp.int32, source.shape, 1)
    zero = jnp.zeros_like(source)
    return jnp.where(lane < HD, source, zero), jnp.where(lane < HD, zero, source)


def attn_forward_body(block, core, ends_ref, mixed_ref, own_ref, send_ref, log_ref, bias_ref):
    rows = mixed_ref.shape[1]

    @pl.when(pl.program_id(0) == 0)
    def _():
        write_bias(ends_ref, bias_ref, block)

    for at in range(0, rows, block):
        keys = at + block
        query = mixed_ref[0, at : at + block, :] * jnp.asarray(HD**-0.5, LOW)
        key = mixed_ref[1, 0:keys, :]
        value = mixed_ref[2, 0:keys, :]
        bias = bias_ref[0:keys, at : at + block]
        total, logs = None, []
        for query_head, value_head in zip(per_head(query), per_head(value)):
            scores = dot(key, query_head, NT) + bias
            top = jnp.max(scores, axis=0, keepdims=True)
            weight = jnp.exp(scores - top)
            norm = jnp.sum(weight, axis=0, keepdims=True)
            logs.append(top + jnp.log(norm))
            part = dot((weight * (1.0 / norm)).astype(LOW), value_head, TN)
            total = part if total is None else total + part
        log_ref[0, :, at : at + block] = jnp.concatenate(logs, axis=0)
        side = (2 * at) // rows
        inner = at - side * (rows // 2)

        @pl.when(core[0] == side)
        def _():
            own_ref[inner : inner + block, :] = total

        @pl.when(core[0] != side)
        def _():
            send_ref[inner : inner + block, :] = total


def attn_forward(core, ends, mixed):
    _, rows, width = mixed.shape
    block = 256
    pairs = width // 128
    return pl.pallas_call(
        functools.partial(attn_forward_body, block),
        grid_spec=pltpu.PrefetchScalarGridSpec(
            num_scalar_prefetch=2,
            grid=(pairs,),
            in_specs=[pl.BlockSpec((3, rows, 128), lambda i, *_: (0, 0, i))],
            out_specs=[
                pl.BlockSpec((rows // 2, 128), lambda i, *_: (0, i)),
                pl.BlockSpec((rows // 2, 128), lambda i, *_: (0, i)),
                pl.BlockSpec((1, 2, rows), lambda i, *_: (i, 0, 0)),
            ],
            scratch_shapes=[pltpu.VMEM((rows, rows), F32)],
        ),
        out_shape=[like(rows // 2, width), like(rows // 2, width), like(pairs, 2, rows)],
        compiler_params=pltpu.CompilerParams(vmem_limit_bytes=40 * MIB),
        cost_estimate=cost(12),
        name="attn_forward",
    )(core, ends, mixed)


def attn_backward_body(
    block, core, ends_ref, mixed_ref, own_ref, other_ref, log_ref, out_ref, bias_ref, key_sum, value_sum
):
    rows = mixed_ref.shape[1]

    @pl.when(pl.program_id(0) == 0)
    def _():
        write_bias(ends_ref, bias_ref, block)

    scale = jnp.asarray(HD**-0.5, LOW)
    for at in reversed(range(0, rows, block)):
        keys = at + block
        side = (2 * at) // rows
        inner = at - side * (rows // 2)
        query = mixed_ref[0, at : at + block, :] * scale
        grad = jnp.where(
            core[0] == side, own_ref[inner : inner + block, :], other_ref[inner : inner + block, :]
        )
        key = mixed_ref[1, 0:keys, :]
        value = mixed_ref[2, 0:keys, :]
        bias = bias_ref[0:keys, at : at + block]
        sums = None
        heads = zip(per_head(query), per_head(grad), per_head(key))
        for head, (query_head, grad_head, key_head) in enumerate(heads):
            log_total = log_ref[0, head : head + 1, at : at + block]
            probs = jnp.exp(dot(key, query_head, NT) + bias - log_total)
            grad_p = dot(value, grad_head, NT)
            row_sum = jnp.sum(probs * grad_p, axis=0, keepdims=True)
            grad_scores = (probs * (grad_p - row_sum)).astype(LOW)
            parts = (
                dot(grad_scores, key_head, TN),
                dot(grad_scores, query_head, NN),
                dot(probs.astype(LOW), grad_head, NN),
            )
            sums = parts if sums is None else [one + two for one, two in zip(sums, parts)]
        out_ref[0, at : at + block, :] = (sums[0] * HD**-0.5).astype(LOW)
        if keys == rows:
            key_sum[...] = sums[1]
            value_sum[...] = sums[2]
        else:
            key_sum[0:keys, :] += sums[1]
            value_sum[0:keys, :] += sums[2]
    out_ref[1] = key_sum[...].astype(LOW)
    out_ref[2] = value_sum[...].astype(LOW)


def attn_backward(core, ends, mixed, own, other, logs):
    _, rows, width = mixed.shape
    block = 256
    return pl.pallas_call(
        functools.partial(attn_backward_body, block),
        grid_spec=pltpu.PrefetchScalarGridSpec(
            num_scalar_prefetch=2,
            grid=(width // 128,),
            in_specs=[
                pl.BlockSpec((3, rows, 128), lambda i, *_: (0, 0, i)),
                pl.BlockSpec((rows // 2, 128), lambda i, *_: (0, i)),
                pl.BlockSpec((rows // 2, 128), lambda i, *_: (0, i)),
                pl.BlockSpec((1, 2, rows), lambda i, *_: (i, 0, 0)),
            ],
            out_specs=pl.BlockSpec((3, rows, 128), lambda i, *_: (0, 0, i)),
            scratch_shapes=[
                pltpu.VMEM((rows, rows), F32),
                pltpu.VMEM((rows, 128), F32),
                pltpu.VMEM((rows, 128), F32),
            ],
        ),
        out_shape=like(3, rows, width, dtype=LOW),
        compiler_params=pltpu.CompilerParams(vmem_limit_bytes=40 * MIB),
        cost_estimate=cost(16),
        name="attn_backward",
    )(core, ends, mixed, own, other, logs)


def turned(source):
    half = source.shape[1] // 2
    return jnp.concatenate([source[:, half:], source[:, :half]], axis=1)


def columns_of(refs, width, step):
    found = []
    for ref in refs:
        for at in range(0, ref.shape[1], step):
            if len(found) < width // step:
                found.append((ref, at))
    return found


def up_body(
    core,
    att_own_ref,
    att_other_ref,
    tok_own_ref,
    tok_other_ref,
    norms_ref,
    gains_ref,
    mid_own_left_ref,
    mid_own_right_ref,
    mid_other_left_ref,
    mid_other_right_ref,
    inner_own_ref,
    inner_send_ref,
    residual_ref,
    feat_ref,
    hidden_own_ref,
    hidden_send_ref,
    normed_ref,
    slope_ref,
    inv_ref,
):
    half = att_own_ref.shape[1]
    units = hidden_own_ref.shape[1]
    step = 512
    out_at = units - mid_own_left_ref.shape[1]
    normed, _ = norm_of(joined(att_own_ref, att_other_ref))
    inner = (normed * norms_ref[2:3, :] + norms_ref[3:4, :]).astype(LOW)
    inner_own_ref[...] = inner[:, :half]
    inner_send_ref[...] = inner[:, half:]
    residual = (
        joined(tok_own_ref, tok_other_ref).astype(F32)
        + dot(inner[:, :half], mid_own_right_ref[:, out_at:], NT)
        + turned(dot(inner[:, half:], mid_other_right_ref[:, out_at:], NT))
    )
    residual_ref[...] = residual
    normed, _ = norm_of(residual)
    feat = (normed * norms_ref[4:5, :] + norms_ref[5:6, :]).astype(LOW)
    feat_ref[...] = feat
    feat_turned = turned(feat)
    own = columns_of((mid_own_left_ref, mid_own_right_ref), units, step)
    other = columns_of((mid_other_left_ref, mid_other_right_ref), units, step)
    total = None
    for number, (ref, at) in enumerate(own + other):
        raised = dot(feat if number < len(own) else feat_turned, ref[:, at : at + step], NN)
        lower = 0.5 + 0.5 * lax.erf(raised * ROOT_HALF)
        active = raised * lower
        to = slice(number * step, (number + 1) * step)
        slope_ref[:, to] = lower + raised * (jnp.exp(raised * raised * -0.5) * ROOT_TURN)
        normed_ref[:, to] = active
        part = jnp.sum(active, axis=1, keepdims=True)
        total = part if total is None else total + part
    mean = total * (1.0 / (2 * units))
    total = None
    for at in range(0, 2 * units, step):
        centred = normed_ref[:, at : at + step] - mean
        part = jnp.sum(centred * centred, axis=1, keepdims=True)
        total = part if total is None else total + part
    inv_std = lax.rsqrt(total * (1.0 / (2 * units)) + EPS_NORM)
    inv_ref[...] = jnp.broadcast_to(inv_std, inv_ref.shape)
    for at in range(0, 2 * units, step):
        normed = (normed_ref[:, at : at + step] - mean) * inv_std
        normed_ref[:, at : at + step] = normed
        hidden = (normed * gains_ref[0:1, at : at + step] + gains_ref[1:2, at : at + step]).astype(LOW)
        if at < units:
            hidden_own_ref[:, at : at + step] = hidden
        else:
            hidden_send_ref[:, at - units : at - units + step] = hidden


def up_forward(core, att_own, att_other, tok_mine, tok_other, norms, gains, *weights):
    rows, half = att_own.shape
    units = gains.shape[1] // 2
    block = min(256, rows)
    shift = rows // block
    return pl.pallas_call(
        up_body,
        grid_spec=pltpu.PrefetchScalarGridSpec(
            num_scalar_prefetch=1,
            grid=(rows // block,),
            in_specs=[
                rows_of(block, half),
                rows_of(block, half),
                rows_of(block, half, shift),
                rows_of(block, half, shift),
                whole_block(norms),
                whole_block(gains),
            ]
            + [whole_block(weight) for weight in weights],
            out_specs=[
                rows_of(block, half),
                rows_of(block, half),
                rows_of(block, 2 * half),
                rows_of(block, 2 * half),
                rows_of(block, units),
                rows_of(block, units),
                rows_of(block, 2 * units),
                rows_of(block, 2 * units),
                rows_of(block, 128),
            ],
        ),
        out_shape=[
            like(rows, half, dtype=LOW),
            like(rows, half, dtype=LOW),
            like(rows, 2 * half),
            like(rows, 2 * half, dtype=LOW),
            like(rows, units, dtype=LOW),
            like(rows, units, dtype=LOW),
            like(rows, 2 * units),
            like(rows, 2 * units),
            like(rows, 128),
        ],
        compiler_params=pltpu.CompilerParams(vmem_limit_bytes=48 * MIB),
        cost_estimate=cost(15),
        name="up_forward",
    )(core, att_own, att_other, tok_mine, tok_other, norms, gains, *weights)


def down_body(
    core,
    hidden_own_ref,
    hidden_send_ref,
    normed_ref,
    slope_ref,
    inv_ref,
    residual_ref,
    cot_mine_ref,
    cot_other_ref,
    att_own_ref,
    att_other_ref,
    norms_ref,
    gains_ref,
    mid_own_left_ref,
    mid_own_right_ref,
    mid_other_left_ref,
    mid_other_right_ref,
    down_own_left_ref,
    down_own_right_ref,
    down_other_left_ref,
    down_other_right_ref,
    output_own_ref,
    output_send_ref,
    raised_own_ref,
    raised_send_ref,
    residual_grad_ref,
    residual_low_ref,
    att_grad_own_ref,
    att_grad_send_ref,
    width_sum_ref,
    hidden_sum_ref,
    scaled_ref,
):
    first = pl.program_id(0) == 0
    half = att_own_ref.shape[1]
    units = hidden_own_ref.shape[1]
    out_at = units - mid_own_left_ref.shape[1]

    def add(ref, row, at, columns, value):
        held = jnp.where(first, 0.0, ref[row : row + 1, at : at + columns])
        ref[row : row + 1, at : at + columns] = held + jnp.sum(value, axis=0, keepdims=True)

    cot = joined(cot_mine_ref, cot_other_ref)
    residual = residual_ref[...]
    inv_std = inv_ref[:, 0:1]
    cut = down_own_left_ref.shape[1]
    output = (
        residual
        + dot(hidden_own_ref[:, :cut], down_own_left_ref[...], NT)
        + dot(hidden_own_ref[:, cut:], down_own_right_ref[...], NT)
        + turned(
            dot(hidden_send_ref[:, :cut], down_other_left_ref[...], NT)
            + dot(hidden_send_ref[:, cut:], down_other_right_ref[...], NT)
        )
    )
    output_own_ref[...] = output[:, :half]
    output_send_ref[...] = output[:, half:]
    sum_plain, sum_cross = None, None
    step = 384
    own = columns_of((down_own_left_ref, down_own_right_ref), units, step)
    other = columns_of((down_other_left_ref, down_other_right_ref), units, step)
    cot_turned = turned(cot)
    for number, (ref, start) in enumerate(own + other):
        at = number * step
        grad = dot(cot if number < len(own) else cot_turned, ref[:, start : start + step], NN)
        cross = grad * normed_ref[:, at : at + step]
        add(hidden_sum_ref, 0, at, step, cross)
        add(hidden_sum_ref, 1, at, step, grad)
        gain = gains_ref[0:1, at : at + step]
        scaled = grad * gain
        scaled_ref[:, at : at + step] = scaled
        plain = jnp.sum(scaled, axis=1, keepdims=True)
        crossed = jnp.sum(cross * gain, axis=1, keepdims=True)
        sum_plain = plain if sum_plain is None else sum_plain + plain
        sum_cross = crossed if sum_cross is None else sum_cross + crossed
    mean_plain = sum_plain * (1.0 / (2 * units))
    mean_cross = sum_cross * (1.0 / (2 * units))
    step = 512
    own = columns_of((mid_own_left_ref, mid_own_right_ref), units, step)
    other = columns_of((mid_other_left_ref, mid_other_right_ref), units, step)
    sums = []
    for side, store in ((own, raised_own_ref), (other, raised_send_ref)):
        total = None
        for number, (ref, start) in enumerate(side):
            to = slice(number * step, (number + 1) * step)
            at = number * step + (0 if side is own else units)
            active = inv_std * (
                scaled_ref[:, at : at + step] - mean_plain - normed_ref[:, at : at + step] * mean_cross
            )
            raised = (active * slope_ref[:, at : at + step]).astype(LOW)
            store[:, to] = raised
            part = dot(raised, ref[:, start : start + step], NT)
            total = part if total is None else total + part
        sums.append(total)
    middle = sums[0] + turned(sums[1])
    normed, inv_std = norm_of(residual)
    add(width_sum_ref, 4, 0, 2 * half, middle * normed)
    add(width_sum_ref, 5, 0, 2 * half, middle)
    residual_grad = cot.astype(F32) + norm_back(middle, normed, inv_std, norms_ref[4:5, :])
    residual_grad_ref[...] = residual_grad
    low = residual_grad.astype(LOW)
    residual_low_ref[...] = low
    inner = jnp.concatenate(
        [
            dot(low, mid_own_right_ref[:, out_at:], NN),
            dot(turned(low), mid_other_right_ref[:, out_at:], NN),
        ],
        axis=1,
    )
    normed, inv_std = norm_of(joined(att_own_ref, att_other_ref))
    add(width_sum_ref, 2, 0, 2 * half, inner * normed)
    add(width_sum_ref, 3, 0, 2 * half, inner)
    att_grad = norm_back(inner, normed, inv_std, norms_ref[2:3, :]).astype(LOW)
    att_grad_own_ref[...] = att_grad[:, :half]
    att_grad_send_ref[...] = att_grad[:, half:]


def down_backward(
    core, hidden_own, hidden_send, normed, slope, inv_std, residual, cot_mine, cot_other, att_own, att_other, *weights
):
    rows, half = att_own.shape
    units = hidden_own.shape[1]
    block = min(256, rows)
    shift = rows // block
    return pl.pallas_call(
        down_body,
        grid_spec=pltpu.PrefetchScalarGridSpec(
            num_scalar_prefetch=1,
            grid=(rows // block,),
            in_specs=[
                rows_of(block, units),
                rows_of(block, units),
                rows_of(block, 2 * units),
                rows_of(block, 2 * units),
                rows_of(block, 128),
                rows_of(block, 2 * half),
                rows_of(block, half, shift),
                rows_of(block, half, shift),
                rows_of(block, half),
                rows_of(block, half),
            ]
            + [whole_block(weight) for weight in weights],
            out_specs=[
                rows_of(block, half),
                rows_of(block, half),
                rows_of(block, units),
                rows_of(block, units),
                rows_of(block, 2 * half),
                rows_of(block, 2 * half),
                rows_of(block, half),
                rows_of(block, half),
                pl.BlockSpec((8, 2 * half), lambda i, core: (0, 0)),
                pl.BlockSpec((8, 2 * units), lambda i, core: (0, 0)),
            ],
            scratch_shapes=[pltpu.VMEM((block, 2 * units), F32)],
        ),
        out_shape=[
            like(rows, half),
            like(rows, half),
            like(rows, units, dtype=LOW),
            like(rows, units, dtype=LOW),
            like(rows, 2 * half),
            like(rows, 2 * half, dtype=LOW),
            like(rows, half, dtype=LOW),
            like(rows, half, dtype=LOW),
            like(8, 2 * half),
            like(8, 2 * units),
        ],
        compiler_params=pltpu.CompilerParams(vmem_limit_bytes=56 * MIB),
        cost_estimate=cost(23),
        name="down_backward",
    )(
        core, hidden_own, hidden_send, normed, slope, inv_std, residual, cot_mine, cot_other, att_own, att_other, *weights
    )


def adam_moments(grad, first, second):
    new_first = BETA_ONE * first + (1.0 - BETA_ONE) * grad
    new_second = BETA_TWO * second + (1.0 - BETA_TWO) * grad * grad
    step_dir = (
        new_first
        / (1.0 - BETA_ONE**STEP)
        / (jnp.sqrt(new_second / (1.0 - BETA_TWO**STEP)) + EPS_ADAM)
    )
    return (new_first, new_second, step_dir)


def shards(
    ring,
    tokens,
    cotangent,
    seq_lengths,
    attn_in,
    attn_out,
    ffn_up,
    ffn_down,
    first_attn_in,
    second_attn_in,
    first_attn_out,
    second_attn_out,
    first_ffn_up,
    second_ffn_up,
    first_ffn_down,
    second_ffn_down,
    width_norm_params,
    first_width_norms,
    second_width_norms,
    hidden_norm_params,
    first_hidden_norms,
    second_hidden_norms,
):
    core = lax.axis_index("tensor")
    core_row = jnp.reshape(core, (1,)).astype(jnp.int32)
    flip = core * (ring.digits[0] // 2)
    tok_rows, half = tokens.shape
    own_rows = tok_rows // 2
    units = ffn_up.shape[1]

    shard_in = jnp.transpose(attn_in, (1, 0, 2)).reshape(attn_in.shape[1], -1).astype(LOW)
    shard_mid = jnp.concatenate([ffn_up, attn_out.T], axis=1).astype(LOW)
    shard_down = ffn_down.T.astype(LOW)
    cut_in, cut_mid, cut_down = 512, 1024, units // 2
    get_in, get_mid, get_down = [Gather(ring, cut, flip) for cut in (cut_in, cut_mid, cut_down)]
    sum_in, sum_mid, sum_down = [Scatter(ring, cut, flip) for cut in (cut_in, cut_mid, cut_down)]

    tok_other = swap(tokens)
    cot_other = swap(cotangent)
    norms = jnp.concatenate([width_norm_params, swap(width_norm_params)], axis=1)
    gains = jnp.concatenate([hidden_norm_params, swap(hidden_norm_params)], axis=1)
    ends = jnp.cumsum(seq_lengths[0])

    line_in = get_in.along_first(shard_in)
    shard_mid, line_in = tie(shard_mid, line_in)
    line_mid = get_mid.along_first(shard_mid)
    arrived_in = get_in.step_two(get_in.step_one(line_in))
    shard_down, line_mid, arrived_in = tie(shard_down, line_mid, arrived_in)
    line_down = get_down.along_first(shard_down)
    stacks_mid = get_mid.step_one(line_mid)
    in_left, in_right = get_in.finish(arrived_in)
    mixed, feat_one = qkv_forward(core_row, tokens, tok_other, norms, in_left, in_right)
    mixed, feat_one, stacks_mid, line_down = tie(mixed, feat_one, stacks_mid, line_down)
    arrived_mid = get_mid.step_two(stacks_mid)
    att_own, att_send, logs = attn_forward(core_row, ends, mixed)
    att_other = swap(att_send)
    arrived_mid, line_down, att_own, att_other = tie(arrived_mid, line_down, att_own, att_other)
    mid_own = get_mid.finish(arrived_mid)
    mid_other = [swap(part) for part in mid_own]
    stacks_down = get_down.step_one(line_down)
    mid_own, mid_other, stacks_down = tie(mid_own, mid_other, stacks_down)
    arrived_down = get_down.step_two(stacks_down)
    (
        inner_own,
        inner_send,
        residual,
        feat_two,
        hidden_own,
        hidden_send,
        hidden_normed,
        slope,
        hidden_inv,
    ) = up_forward(
        core_row,
        att_own,
        att_other,
        tokens,
        tok_other,
        norms,
        gains,
        *mid_own,
        *mid_other,
    )
    arrived_down, hidden_own, hidden_send = tie(arrived_down, hidden_own, hidden_send)
    down_own = get_down.finish(arrived_down)
    down_other = [swap(part) for part in down_own]

    def token_half(source, which):
        return lax.dynamic_slice_in_dim(source, which * own_rows, own_rows, 0)

    cot_all = jnp.concatenate([cotangent, cot_other], axis=1)
    hidden_there = swap(hidden_send)
    feat_two_there = swap(feat_two)
    inner_there = swap(inner_send)
    grad_down = dot(token_half(cot_all, core), hidden_own, TN) + dot(
        token_half(cot_all, 1 - core), hidden_there, TN
    )
    grad_down = grad_down.astype(LOW)
    grad_down, down_own, down_other = tie(grad_down, down_own, down_other)
    sums_down = sum_down.step_one(grad_down)
    (
        output_own,
        output_send,
        raised_own,
        raised_send,
        residual_grad,
        residual_low,
        att_grad_own,
        att_grad_send,
        width_sum,
        hidden_sum,
    ) = down_backward(
        core_row,
        hidden_own,
        hidden_send,
        hidden_normed,
        slope,
        hidden_inv,
        residual,
        cotangent,
        cot_other,
        att_own,
        att_other,
        norms,
        gains,
        *mid_own,
        *mid_other,
        *down_own,
        *down_other,
    )
    block_output = in_token_order(output_own, swap(output_send))
    att_grad_other = swap(att_grad_send)

    def halves_turned(source):
        return jnp.concatenate([source[:, half:], source[:, :half]], axis=1)

    sums_down, feat_two, raised_own, residual_low, att_grad_other = tie(
        sums_down, feat_two, raised_own, residual_low, att_grad_other
    )
    raised_there = swap(raised_send)
    residual_there = swap(residual_low)
    line_sum_down = sum_down.step_two(sums_down)
    grad_mid = jnp.concatenate(
        [
            dot(feat_two, raised_own, TN) + dot(halves_turned(feat_two_there), raised_there, TN),
            dot(residual_low, inner_own, TN) + dot(halves_turned(residual_there), inner_there, TN),
        ],
        axis=1,
    ).astype(LOW)
    grad_mid, line_sum_down, att_grad_other = tie(grad_mid, line_sum_down, att_grad_other)
    sums_mid = sum_mid.step_one(grad_mid)
    red_down_t = sum_down.along_first(line_sum_down)
    grad_mixed = attn_backward(core_row, ends, mixed, att_grad_own, att_grad_other, logs)
    grad_mixed, sums_mid, red_down_t = tie(grad_mixed, sums_mid, red_down_t)
    line_sum_mid = sum_mid.step_two(sums_mid)
    grad_in = jnp.concatenate(
        [dot(feat_one, grad_mixed[part], TN) for part in range(3)], axis=1
    ).astype(LOW)
    grad_in, line_sum_mid, grad_mixed = tie(grad_in, line_sum_mid, grad_mixed)
    sums_in = sum_in.step_one(grad_in)
    red_mid = sum_mid.along_first(line_sum_mid)
    red_in_rows = sum_in.along_first(sum_in.step_two(sums_in))

    weights_in = jnp.concatenate([in_left, in_right], axis=1)
    grad_first = sum(
        dot(grad_mixed[part], weights_in[:, part * half : (part + 1) * half], NT) for part in range(3)
    )
    tok_all = jnp.concatenate([tokens, tok_other], axis=1).astype(F32)
    normed_one, inv_one = norm_of(tok_all)
    sums_one = jnp.stack([jnp.sum(grad_first * normed_one, axis=0), jnp.sum(grad_first, axis=0)])
    first_rows = token_half(grad_first, core) + halves_turned(swap(token_half(grad_first, 1 - core)))
    token_grads = residual_grad + norm_back(
        first_rows, token_half(normed_one, core), token_half(inv_one, core), norms[0:1]
    )
    grad_tokens = in_token_order(token_grads[:, :half], swap(token_grads[:, half:]))

    sums_width = jnp.concatenate([sums_one, width_sum[2:6]])
    sums_width = sums_width[:, :half] + swap(sums_width[:, half:])
    sums_hidden = hidden_sum[0:2, :units] + swap(hidden_sum[0:2, units:])
    packed = jnp.concatenate([sums_width.reshape(-1, 128), sums_hidden.reshape(-1, 128)])
    packed = ring.all_sum(packed)
    width_rows = sums_width.size // 128
    red_width = packed[:width_rows].reshape(sums_width.shape)
    red_hidden = packed[width_rows:].reshape(sums_hidden.shape)

    red_in = jnp.transpose(red_in_rows.reshape(-1, 3, half), (1, 0, 2))
    red_up = red_mid[:, :units]
    red_out = red_mid[:, units:].T
    red_down = red_down_t.T

    masters = (attn_in, attn_out, ffn_up, ffn_down)
    reduced = (red_in, red_out, red_up, red_down)
    firsts = (first_attn_in, first_attn_out, first_ffn_up, first_ffn_down)
    seconds = (second_attn_in, second_attn_out, second_ffn_up, second_ffn_down)
    states = [adam_moments(reduced[index], firsts[index], seconds[index]) for index in range(4)]
    updates = [states[index][2] + DECAY * masters[index] for index in range(4)]
    width_state = adam_moments(red_width, first_width_norms, second_width_norms)
    hidden_state = adam_moments(red_hidden, first_hidden_norms, second_hidden_norms)
    matrix_squares = jnp.stack(
        [jnp.sum(matrix * matrix) for matrix in masters]
        + [jnp.sum(matrix * matrix) for matrix in updates]
    )
    norm_squares = jnp.concatenate(
        [
            jnp.sum(width_norm_params * width_norm_params, axis=1),
            jnp.sum(hidden_norm_params * hidden_norm_params, axis=1),
            jnp.sum(width_state[2] * width_state[2], axis=1),
            jnp.sum(hidden_state[2] * hidden_state[2], axis=1),
        ]
    )
    matrix_squares = ring.all_sum(matrix_squares)
    squares = jnp.concatenate([matrix_squares, norm_squares])
    squares = squares + swap(squares)
    ratio = jnp.sqrt(squares[0:4] / (squares[4:8] + 1e-06))
    norm_ratio = jnp.sqrt(squares[8:16] / (squares[16:24] + 1e-06))
    new_masters = [masters[index] - RATE * ratio[index] * updates[index] for index in range(4)]
    new_width = width_norm_params - RATE * norm_ratio[0:6][:, None] * width_state[2]
    new_hidden = hidden_norm_params - RATE * norm_ratio[6:8][:, None] * hidden_state[2]
    return (
        block_output,
        grad_tokens,
        new_masters[0],
        new_masters[1],
        new_masters[2],
        new_masters[3],
        states[0][0],
        states[1][0],
        states[2][0],
        states[3][0],
        states[0][1],
        states[1][1],
        states[2][1],
        states[3][1],
        new_width,
        width_state[0],
        width_state[1],
        new_hidden,
        hidden_state[0],
        hidden_state[1],
    )


def solution(mesh):
    rows = P("dp", "tensor")
    stacked = P(None, "dp", "tensor")
    turned = P("tensor", "dp")
    narrow = P(None, "tensor")
    in_specs = (
        (rows, rows, P("dp", None), stacked, turned, rows, turned)
        + (stacked, stacked, turned, turned, rows, rows, turned, turned)
        + (narrow,) * 6
    )
    out_specs = (rows, rows) + (stacked, turned, rows, turned) * 3 + (narrow,) * 6
    ring = Ring(mesh.shape["dp"])

    def body(*arrays):
        return shards(ring, *arrays)

    return jax.shard_map(
        body, mesh=mesh, in_specs=in_specs, out_specs=out_specs, check_vma=False
    )
```

```python
import functools

import jax
import jax.numpy as jnp
import numpy as np
from jax import lax
from jax.experimental import pallas as pl
from jax.experimental.pallas import tpu as pltpu
from jax.sharding import PartitionSpec as P

HD = 64
STEP = 10
EPS_NORM = 1e-05
BETA_ONE = 0.9
BETA_TWO = 0.999
EPS_ADAM = 1e-06
DECAY = 0.01
RATE = 0.25
MASKED = -1e30
ROOT_HALF = 0.7071067811865476
ROOT_TURN = 0.3989422804014327
LOW = jnp.bfloat16
F32 = jnp.float32
MIB = 2**20
RATE_FLOPS = 1_150_000_000
PACKED_ROWS = 16

NN = ((1,), (0,))
NT = ((1,), (1,))
TN = ((0,), (0,))


def dot(left, right, dims):
    return lax.dot_general(left, right, (dims, ((), ())), preferred_element_type=F32)


def tie(*values):
    return lax.optimization_barrier(values)


class Paths:
    def __init__(self, count):
        self.count = count
        if count == 16:
            self.shared, self.one, self.two = (8, 4), (1,), (2,)
        elif count == 128:
            self.shared, self.one, self.two = (64, 32), (4, 2, 1), (16, 8)
        else:
            raise ValueError("dp size")
        self.left = self.shared + self.one + self.two
        self.right = self.shared + self.two + self.one

    def send(self, source, mask):
        pairs = [(device, device ^ mask) for device in range(self.count)]
        return lax.ppermute(source, "dp", pairs)

    def owners(self, masks):
        found = [0]
        for mask in masks:
            found = found + [owner ^ mask for owner in found]
        return np.array(found, np.int32)

    def all_sum(self, source):
        for mask in reversed(self.left):
            source = source + self.send(source, mask)
        return source


class Gather:
    def __init__(self, paths, cut):
        self.paths, self.cut = paths, cut

    def shared(self, source, step, mine):
        mask = self.paths.shared[step]
        arrived = self.paths.send(source, mask)
        low = (mine & mask) == 0
        pair = [jnp.where(low, source, arrived), jnp.where(low, arrived, source)]
        return jnp.stack(pair, axis=step)

    def step_one(self, line):
        line = line.reshape(1, -1, *line.shape[2:])
        return [
            self.grow(line[..., : self.cut], self.paths.one),
            self.grow(line[..., self.cut :], self.paths.two),
        ]

    def grow(self, stack, masks):
        for mask in masks:
            stack = jnp.concatenate([stack, self.paths.send(stack, mask)])
        return stack

    def step_two(self, stacks):
        left, right = stacks
        left = self.grow(left, self.paths.two[:-1])
        right = self.grow(right, self.paths.one[:-1])
        return [
            left,
            self.paths.send(left, self.paths.two[-1]),
            right,
            self.paths.send(right, self.paths.one[-1]),
        ]


class Scatter:
    def __init__(self, paths):
        self.paths = paths

    def halve(self, keep, send, mask):
        arrived = self.paths.send(send, mask)
        size = keep.shape[0] // 2
        kept = keep[:size].astype(F32) + arrived[:size].astype(F32)
        sent = (keep[size:].astype(F32) + arrived[size:].astype(F32)).astype(LOW)
        return kept, sent

    def step_one(self, blocks):
        left, right = blocks[:2], blocks[2:]
        for mask in reversed(self.paths.two):
            left = self.halve(*left, mask)
        for mask in reversed(self.paths.one):
            right = self.halve(*right, mask)
        return left, right

    def step_two(self, sums):
        left, right = sums
        for mask in reversed(self.paths.one):
            left = self.halve(*left, mask)
        for mask in reversed(self.paths.two):
            right = self.halve(*right, mask)
        return [jnp.concatenate(pair, axis=2) for pair in zip(left, right)]

    def shared(self, pair):
        for mask in reversed(self.paths.shared[1:]):
            pair = self.halve(*pair, mask)
        return pair

    def last(self, pair):
        keep, send = pair
        return keep[0], self.paths.send(send, self.paths.shared[0])[0]


def swap(source):
    return lax.ppermute(source, "tensor", [(0, 1), (1, 0)])


def own_first(place_ref):
    return place_ref[2]


class Layout:
    def __init__(self, paths, rows):
        self.paths, self.rows = paths, rows
        self.direct = rows % PACKED_ROWS == 0
        self.left, self.right = paths.owners(paths.left), paths.owners(paths.right)
        self.wide = 2 ** len(paths.shared)
        self.left_lines = paths.owners(paths.one + paths.two)
        self.right_lines = paths.owners(paths.two + paths.one)

    def prepare(self, pieces, mine, there=False):
        if self.direct:
            return list(pieces)
        whole = []
        lines = self.paths.count // self.wide
        for part, owners in ((pieces[:2], self.left_lines), (pieces[2:], self.right_lines)):
            stack = jnp.concatenate(part)
            inverse = np.argsort(owners).astype(np.int32)
            order = jnp.take(jnp.asarray(inverse), jnp.arange(lines) ^ (mine % lines))
            stack = jnp.swapaxes(jnp.take(stack, order, axis=0), 0, 1)
            if there:
                stack = jnp.roll(stack, self.wide // 2, axis=0)
            whole.append(stack.reshape(-1, stack.shape[3]))
        return whole

    def count(self):
        return 4 if self.direct else 2

    def columns(self, refs):
        return refs[0].shape[-1], refs[-1].shape[-1]

    def scratch(self, columns):
        rows = self.rows * self.paths.count
        if not self.direct:
            return pltpu.VMEM((rows, columns), LOW)
        return pltpu.VMEM((self.wide, self.paths.count // self.wide, self.rows, columns), LOW)

    def read(self, ref, start=0, stop=None):
        value = ref[..., start : ref.shape[-1] if stop is None else stop]
        return value.reshape(-1, value.shape[-1])

    def copies(self, refs, place_ref, spans, there=False):
        found = []
        cut = refs[0].shape[-1]
        lines = self.paths.count // self.wide
        groups = (
            (0, refs[: len(refs) // 2], self.left_lines),
            (cut, refs[len(refs) // 2 :], self.right_lines),
        )
        for base, part, owners in groups:
            width = part[0].shape[-1]
            for start, stop, target, column in spans:
                low, high = max(start, base), min(stop, base + width)
                if low >= high:
                    continue
                source = pl.ds(low - base, high - low)
                to = pl.ds(column + low - start, high - low)
                if not self.direct:
                    found.append((part[0].at[:, source], target.at[:, to]))
                    continue
                number = 0
                for ref in part:
                    for line in range(ref.shape[0]):
                        owner = (own_first(place_ref) % lines) ^ int(owners[number])
                        size = self.wide // 2 if there else self.wide
                        for at in range(0, self.wide, size):
                            past = self.wide - size - at if there else at
                            found.append(
                                (
                                    ref.at[line, pl.ds(at, size), :, source],
                                    target.at[pl.ds(past, size), owner, :, to],
                                )
                            )
                        number += 1
        return found

    def order_rows(self, source_ref, target_ref, place_ref):
        if not self.direct:
            target_ref[...] = source_ref[...]
            return
        for number, owner in enumerate(self.left):
            row = pl.multiple_of((own_first(place_ref) ^ int(owner)) * self.rows, PACKED_ROWS)
            target_ref[number * self.rows : (number + 1) * self.rows, :] = source_ref[
                pl.ds(row, self.rows), :
            ]

    def right_rows(self):
        if not self.direct:
            size = self.rows * self.paths.count // 2
            return [(0, 0, size), (size, size, size)]
        line = self.rows * 2 ** len(self.paths.shared)
        ones, twos = 2 ** len(self.paths.one), 2 ** len(self.paths.two)
        return [
            ((two * ones + one) * line, (one * twos + two) * line, line)
            for two in range(twos)
            for one in range(ones)
        ]

    def finish(self, blocks, mine):
        if self.direct:
            return [block.reshape(-1, self.rows, block.shape[1]) for block in blocks]
        found = []
        for part, owners in ((blocks[:2], self.left), (blocks[2:], self.right)):
            whole = jnp.concatenate(part).reshape(-1, self.rows, part[0].shape[1])
            whole = jnp.take(whole, jnp.asarray(owners) ^ mine, axis=0)
            found += [whole[: self.paths.count // 2], whole[self.paths.count // 2 :]]
        return found


def start_all(copies, sems):
    started = [
        pltpu.make_async_copy(source, target, sems.at[number])
        for number, (source, target) in enumerate(copies)
    ]
    for copy in started:
        copy.start()
    return started


def wait_all(copies):
    for copy in copies:
        copy.wait()


def norm_of(source):
    width = source.shape[1]
    centred = source - jnp.sum(source, axis=1, keepdims=True) * (1.0 / width)
    variance = jnp.sum(centred * centred, axis=1, keepdims=True) * (1.0 / width)
    inv_std = lax.rsqrt(variance + EPS_NORM)
    return centred * inv_std, inv_std


def norm_back(grad_out, normed, inv_std, gain_row):
    width = normed.shape[1]
    scaled = grad_out * gain_row
    mean_plain = jnp.sum(scaled, axis=1, keepdims=True) * (1.0 / width)
    mean_cross = jnp.sum(scaled * normed, axis=1, keepdims=True) * (1.0 / width)
    return inv_std * (scaled - mean_plain - normed * mean_cross)


def add_rows(ref, row, first, at, value):
    columns = value.shape[1]
    held = jnp.where(first, 0.0, ref[row : row + 1, at : at + columns])
    ref[row : row + 1, at : at + columns] = held + jnp.sum(value, axis=0, keepdims=True)


def joined(mine_ref, other_ref):
    return jnp.concatenate([mine_ref[...], other_ref[...]], axis=1)


def whole_block(array):
    zeros = (0,) * array.ndim
    return pl.BlockSpec(array.shape, lambda *_: zeros, pipeline_mode=pl.Buffered(1))


ANYWHERE = pl.BlockSpec(memory_space=pl.ANY)


def like(*shape, dtype=F32):
    return jax.ShapeDtypeStruct(shape, dtype)


def rows_of(block, columns, shift=None):
    if shift is None:
        return pl.BlockSpec((block, columns), lambda i, place: (i, 0))
    return pl.BlockSpec((block, columns), lambda i, place: (i + place[0] * shift, 0))


def cost(micros):
    return pl.CostEstimate(flops=micros * RATE_FLOPS, bytes_accessed=0, transcendentals=0)


def params(mib):
    return pltpu.CompilerParams(vmem_limit_bytes=mib * MIB)


def qkv_body(layout, place, mine_ref, other_ref, norms_ref, *refs):
    weights, (mixed_ref, feat_ref, scratch, sems) = refs[:-4], refs[-4:]
    first = pl.program_id(0) == 0
    copies = layout.copies(weights, place, [(0, scratch.shape[-1], scratch, 0)])

    @pl.when(first)
    def _():
        start_all(copies, sems)

    normed, _ = norm_of(joined(mine_ref, other_ref).astype(F32))
    feat = (normed * norms_ref[0:1, :] + norms_ref[1:2, :]).astype(LOW)
    feat_ref[...] = feat

    @pl.when(first)
    def _():
        wait_all([pltpu.make_async_copy(*copy, sems.at[n]) for n, copy in enumerate(copies)])

    result = dot(feat, layout.read(scratch), NN).astype(LOW)
    width = mixed_ref.shape[2]
    for part in range(3):
        mixed_ref[part] = result[:, part * width : (part + 1) * width]


def qkv_forward(layout, place, mine, other, norms, weights):
    rows, width = mine.shape
    block = min(256, rows)
    return pl.pallas_call(
        functools.partial(qkv_body, layout),
        grid_spec=pltpu.PrefetchScalarGridSpec(
            num_scalar_prefetch=1,
            grid=(rows // block,),
            in_specs=[rows_of(block, width), rows_of(block, width), whole_block(norms)]
            + [ANYWHERE] * len(weights),
            out_specs=[
                pl.BlockSpec((3, block, width), lambda i, place: (0, i, 0)),
                rows_of(block, 2 * width),
            ],
            scratch_shapes=[
                layout.scratch(3 * width),
                pltpu.SemaphoreType.DMA((64,)),
            ],
        ),
        out_shape=[like(3, rows, width, dtype=LOW), like(rows, 2 * width, dtype=LOW)],
        compiler_params=params(24),
        cost_estimate=cost(5),
        name="qkv_forward",
    )(place, mine, other, norms, *weights)


def write_bias(ends_ref, bias_ref, block):
    for at in range(0, bias_ref.shape[1], block):
        keys = at + block
        place = at + lax.broadcasted_iota(jnp.int32, (1, block), 1)
        start = jnp.zeros_like(place)
        for slot in range(ends_ref.shape[0]):
            end = ends_ref[slot]
            start = jnp.maximum(start, jnp.where(end <= place, end, 0))
        key_place = lax.broadcasted_iota(jnp.int32, (keys, block), 0)
        visible = (key_place >= start) & (key_place <= place)
        bias_ref[0:keys, at : at + block] = jnp.where(visible, 0.0, MASKED)


def per_head(source):
    lane = lax.broadcasted_iota(jnp.int32, source.shape, 1)
    zero = jnp.zeros_like(source)
    return jnp.where(lane < HD, source, zero), jnp.where(lane < HD, zero, source)


def attn_forward_body(block, place, ends_ref, mixed_ref, own_ref, send_ref, log_ref, bias_ref):
    rows = mixed_ref.shape[1]

    @pl.when(pl.program_id(0) == 0)
    def _():
        write_bias(ends_ref, bias_ref, block)

    for at in range(0, rows, block):
        keys = at + block
        query = mixed_ref[0, at : at + block, :] * jnp.asarray(HD**-0.5, LOW)
        key = mixed_ref[1, 0:keys, :]
        value = mixed_ref[2, 0:keys, :]
        bias = bias_ref[0:keys, at : at + block]
        total, logs = None, []
        for query_head, value_head in zip(per_head(query), per_head(value)):
            scores = dot(key, query_head, NT) + bias
            top = jnp.max(scores, axis=0, keepdims=True)
            weight = jnp.exp(scores - top)
            norm = jnp.sum(weight, axis=0, keepdims=True)
            logs.append(top + jnp.log(norm))
            part = dot((weight * (1.0 / norm)).astype(LOW), value_head, TN)
            total = part if total is None else total + part
        log_ref[0, :, at : at + block] = jnp.concatenate(logs, axis=0)
        side = (2 * at) // rows
        inner = at - side * (rows // 2)

        @pl.when(place[0] == side)
        def _():
            own_ref[inner : inner + block, :] = total

        @pl.when(place[0] != side)
        def _():
            send_ref[inner : inner + block, :] = total


def attn_forward(place, ends, mixed):
    _, rows, width = mixed.shape
    block = 256
    pairs = width // 128
    return pl.pallas_call(
        functools.partial(attn_forward_body, block),
        grid_spec=pltpu.PrefetchScalarGridSpec(
            num_scalar_prefetch=2,
            grid=(pairs,),
            in_specs=[pl.BlockSpec((3, rows, 128), lambda i, *_: (0, 0, i))],
            out_specs=[
                pl.BlockSpec((rows // 2, 128), lambda i, *_: (0, i)),
                pl.BlockSpec((rows // 2, 128), lambda i, *_: (0, i)),
                pl.BlockSpec((1, 2, rows), lambda i, *_: (i, 0, 0)),
            ],
            scratch_shapes=[pltpu.VMEM((rows, rows), F32)],
        ),
        out_shape=[like(rows // 2, width), like(rows // 2, width), like(pairs, 2, rows)],
        compiler_params=params(40),
        cost_estimate=cost(12),
        name="attn_forward",
    )(place, ends, mixed)


def attn_backward_body(
    block, place, ends_ref, mixed_ref, own_ref, other_ref, log_ref, out_ref, bias_ref, key_sum, value_sum
):
    rows = mixed_ref.shape[1]

    @pl.when(pl.program_id(0) == 0)
    def _():
        write_bias(ends_ref, bias_ref, block)

    scale = jnp.asarray(HD**-0.5, LOW)
    for at in reversed(range(0, rows, block)):
        keys = at + block
        side = (2 * at) // rows
        inner = at - side * (rows // 2)
        query = mixed_ref[0, at : at + block, :] * scale
        grad = jnp.where(
            place[0] == side, own_ref[inner : inner + block, :], other_ref[inner : inner + block, :]
        )
        key = mixed_ref[1, 0:keys, :]
        value = mixed_ref[2, 0:keys, :]
        bias = bias_ref[0:keys, at : at + block]
        sums = None
        heads = zip(per_head(query), per_head(grad), per_head(key))
        for head, (query_head, grad_head, key_head) in enumerate(heads):
            log_total = log_ref[0, head : head + 1, at : at + block]
            probs = jnp.exp(dot(key, query_head, NT) + bias - log_total)
            grad_p = dot(value, grad_head, NT)
            row_sum = jnp.sum(probs * grad_p, axis=0, keepdims=True)
            grad_scores = (probs * (grad_p - row_sum)).astype(LOW)
            parts = (
                dot(grad_scores, key_head, TN),
                dot(grad_scores, query_head, NN),
                dot(probs.astype(LOW), grad_head, NN),
            )
            sums = parts if sums is None else [one + two for one, two in zip(sums, parts)]
        out_ref[0, at : at + block, :] = (sums[0] * HD**-0.5).astype(LOW)
        if keys == rows:
            key_sum[...] = sums[1]
            value_sum[...] = sums[2]
        else:
            key_sum[0:keys, :] += sums[1]
            value_sum[0:keys, :] += sums[2]
    out_ref[1] = key_sum[...].astype(LOW)
    out_ref[2] = value_sum[...].astype(LOW)


def attn_backward(place, ends, mixed, own, other, logs):
    _, rows, width = mixed.shape
    block = 256
    return pl.pallas_call(
        functools.partial(attn_backward_body, block),
        grid_spec=pltpu.PrefetchScalarGridSpec(
            num_scalar_prefetch=2,
            grid=(width // 128,),
            in_specs=[
                pl.BlockSpec((3, rows, 128), lambda i, *_: (0, 0, i)),
                pl.BlockSpec((rows // 2, 128), lambda i, *_: (0, i)),
                pl.BlockSpec((rows // 2, 128), lambda i, *_: (0, i)),
                pl.BlockSpec((1, 2, rows), lambda i, *_: (i, 0, 0)),
            ],
            out_specs=pl.BlockSpec((3, rows, 128), lambda i, *_: (0, 0, i)),
            scratch_shapes=[
                pltpu.VMEM((rows, rows), F32),
                pltpu.VMEM((rows, 128), F32),
                pltpu.VMEM((rows, 128), F32),
            ],
        ),
        out_shape=like(3, rows, width, dtype=LOW),
        compiler_params=params(40),
        cost_estimate=cost(16),
        name="attn_backward",
    )(place, ends, mixed, own, other, logs)


def turned(source):
    half = source.shape[1] // 2
    return jnp.concatenate([source[:, half:], source[:, :half]], axis=1)


def mid_spans(up_scratch, out_scratch, side):
    units, half = up_scratch.shape[-1] // 2, out_scratch.shape[-1] // 2
    return [
        (0, units, up_scratch, side * units),
        (units, units + half, out_scratch, side * half),
    ]


def part_copies(layout, place, groups):
    found = []
    for side, (refs, spans) in enumerate(groups):
        found += layout.copies(refs, place, spans, side == 1)
    return found


def up_body(layout, place, *refs):
    (
        att_own_ref,
        att_other_ref,
        tok_own_ref,
        tok_other_ref,
        norms_ref,
        gains_ref,
    ) = refs[:6]
    count = layout.count()
    own_weights, other_weights = refs[6 : 6 + count], refs[6 + count : 6 + 2 * count]
    (
        inner_own_ref,
        inner_send_ref,
        residual_ref,
        feat_ref,
        hidden_own_ref,
        hidden_send_ref,
        normed_ref,
        slope_ref,
        inv_ref,
        up_ref,
        out_ref,
        sems,
    ) = refs[6 + 2 * count :]
    half = att_own_ref.shape[1]
    units = hidden_own_ref.shape[1]
    step = 512
    first = pl.program_id(0) == 0
    spans = [mid_spans(up_ref, out_ref, side) for side in range(2)]
    out_copies = part_copies(
        layout, place, [(own_weights, spans[0][1:]), (other_weights, spans[1][1:])]
    )
    up_copies = part_copies(
        layout, place, [(own_weights, spans[0][:1]), (other_weights, spans[1][:1])]
    )
    copies = [
        pltpu.make_async_copy(*copy, sems.at[n]) for n, copy in enumerate(out_copies + up_copies)
    ]

    @pl.when(first)
    def _():
        for copy in copies:
            copy.start()

    normed, _ = norm_of(joined(att_own_ref, att_other_ref))
    inner = (normed * norms_ref[2:3, :] + norms_ref[3:4, :]).astype(LOW)
    inner_own_ref[...] = inner[:, :half]
    inner_send_ref[...] = inner[:, half:]

    @pl.when(first)
    def _():
        wait_all(copies[: len(out_copies)])

    residual = joined(tok_own_ref, tok_other_ref).astype(F32) + dot(inner, layout.read(out_ref), NT)
    residual_ref[...] = residual
    normed, _ = norm_of(residual)
    feat = (normed * norms_ref[4:5, :] + norms_ref[5:6, :]).astype(LOW)
    feat_ref[...] = feat

    @pl.when(first)
    def _():
        wait_all(copies[len(out_copies) :])

    total = None
    for at in range(0, 2 * units, step):
        raised = dot(feat, layout.read(up_ref, at, at + step), NN)
        lower = 0.5 + 0.5 * lax.erf(raised * ROOT_HALF)
        active = raised * lower
        slope_ref[:, at : at + step] = lower + raised * (
            jnp.exp(raised * raised * -0.5) * ROOT_TURN
        )
        normed_ref[:, at : at + step] = active
        part = jnp.sum(active, axis=1, keepdims=True)
        total = part if total is None else total + part
    mean = total * (1.0 / (2 * units))
    total = None
    for at in range(0, 2 * units, step):
        centred = normed_ref[:, at : at + step] - mean
        part = jnp.sum(centred * centred, axis=1, keepdims=True)
        total = part if total is None else total + part
    inv_std = lax.rsqrt(total * (1.0 / (2 * units)) + EPS_NORM)
    inv_ref[...] = jnp.broadcast_to(inv_std, inv_ref.shape)
    for at in range(0, 2 * units, step):
        normed = (normed_ref[:, at : at + step] - mean) * inv_std
        normed_ref[:, at : at + step] = normed
        hidden = (normed * gains_ref[0:1, at : at + step] + gains_ref[1:2, at : at + step]).astype(LOW)
        if at < units:
            hidden_own_ref[:, at : at + step] = hidden
        else:
            hidden_send_ref[:, at - units : at - units + step] = hidden


def up_forward(layout, place, att_own, att_other, tok_mine, tok_other, norms, gains, weights):
    rows, half = att_own.shape
    units = gains.shape[1] // 2
    block = min(256, rows)
    shift = rows // block
    return pl.pallas_call(
        functools.partial(up_body, layout),
        grid_spec=pltpu.PrefetchScalarGridSpec(
            num_scalar_prefetch=1,
            grid=(rows // block,),
            in_specs=[
                rows_of(block, half),
                rows_of(block, half),
                rows_of(block, half, shift),
                rows_of(block, half, shift),
                whole_block(norms),
                whole_block(gains),
            ]
            + [ANYWHERE] * len(weights),
            out_specs=[
                rows_of(block, half),
                rows_of(block, half),
                rows_of(block, 2 * half),
                rows_of(block, 2 * half),
                rows_of(block, units),
                rows_of(block, units),
                rows_of(block, 2 * units),
                rows_of(block, 2 * units),
                rows_of(block, 128),
            ],
            scratch_shapes=[
                layout.scratch(2 * units),
                layout.scratch(2 * half),
                pltpu.SemaphoreType.DMA((128,)),
            ],
        ),
        out_shape=[
            like(rows, half, dtype=LOW),
            like(rows, half, dtype=LOW),
            like(rows, 2 * half),
            like(rows, 2 * half, dtype=LOW),
            like(rows, units, dtype=LOW),
            like(rows, units, dtype=LOW),
            like(rows, 2 * units),
            like(rows, 2 * units),
            like(rows, 128),
        ],
        compiler_params=params(48),
        cost_estimate=cost(15),
        name="up_forward",
    )(place, att_own, att_other, tok_mine, tok_other, norms, gains, *weights)


def down_body(layout, place, *refs):
    (
        hidden_own_ref,
        hidden_send_ref,
        normed_ref,
        slope_ref,
        inv_ref,
        residual_ref,
        cot_mine_ref,
        cot_other_ref,
        att_own_ref,
        att_other_ref,
        norms_ref,
        gains_ref,
    ) = refs[:12]
    count = layout.count()
    weights = [refs[12 + number * count : 12 + (number + 1) * count] for number in range(4)]
    (
        output_own_ref,
        output_send_ref,
        raised_own_ref,
        raised_send_ref,
        residual_grad_ref,
        residual_low_ref,
        att_grad_own_ref,
        att_grad_send_ref,
        width_sum_ref,
        hidden_sum_ref,
        scaled_ref,
        up_ref,
        out_ref,
        down_ref,
        sems,
    ) = refs[12 + 4 * count :]
    first = pl.program_id(0) == 0
    half = att_own_ref.shape[1]
    units = hidden_own_ref.shape[1]
    spans = [mid_spans(up_ref, out_ref, side) for side in range(2)]
    down_copies = part_copies(
        layout,
        place,
        [(weights[2 + side], [(0, units, down_ref, side * units)]) for side in range(2)],
    )
    up_copies = part_copies(layout, place, [(weights[side], spans[side][:1]) for side in range(2)])
    out_copies = part_copies(layout, place, [(weights[side], spans[side][1:]) for side in range(2)])
    copies = [
        pltpu.make_async_copy(*copy, sems.at[n])
        for n, copy in enumerate(down_copies + up_copies + out_copies)
    ]
    marks = (0, len(down_copies), len(down_copies) + len(up_copies), len(copies))

    @pl.when(first)
    def _():
        for copy in copies:
            copy.start()
        width_sum_ref[...] = jnp.zeros_like(width_sum_ref)
        hidden_sum_ref[...] = jnp.zeros_like(hidden_sum_ref)
        wait_all(copies[marks[0] : marks[1]])

    cot = joined(cot_mine_ref, cot_other_ref)
    residual = residual_ref[...]
    inv_std = inv_ref[:, 0:1]
    output = (
        residual
        + dot(hidden_own_ref[...], layout.read(down_ref, 0, units), NT)
        + dot(hidden_send_ref[...], layout.read(down_ref, units), NT)
    )
    output_own_ref[...] = output[:, :half]
    output_send_ref[...] = output[:, half:]
    sum_plain, sum_cross = None, None
    step = 512
    for at in range(0, 2 * units, step):
        grad = dot(cot, layout.read(down_ref, at, at + step), NN)
        cross = grad * normed_ref[:, at : at + step]
        add_rows(hidden_sum_ref, 0, first, at, cross)
        add_rows(hidden_sum_ref, 1, first, at, grad)
        gain = gains_ref[0:1, at : at + step]
        scaled = grad * gain
        scaled_ref[:, at : at + step] = scaled
        plain = jnp.sum(scaled, axis=1, keepdims=True)
        crossed = jnp.sum(cross * gain, axis=1, keepdims=True)
        sum_plain = plain if sum_plain is None else sum_plain + plain
        sum_cross = crossed if sum_cross is None else sum_cross + crossed
    mean_plain = sum_plain * (1.0 / (2 * units))
    mean_cross = sum_cross * (1.0 / (2 * units))

    @pl.when(first)
    def _():
        wait_all(copies[marks[1] : marks[2]])

    middle = None
    for at in range(0, 2 * units, step):
        active = inv_std * (
            scaled_ref[:, at : at + step] - mean_plain - normed_ref[:, at : at + step] * mean_cross
        )
        raised = (active * slope_ref[:, at : at + step]).astype(LOW)
        if at < units:
            raised_own_ref[:, at : at + step] = raised
        else:
            raised_send_ref[:, at - units : at - units + step] = raised
        part = dot(raised, layout.read(up_ref, at, at + step), NT)
        middle = part if middle is None else middle + part
    normed, inv_std = norm_of(residual)
    add_rows(width_sum_ref, 4, first, 0, middle * normed)
    add_rows(width_sum_ref, 5, first, 0, middle)
    residual_grad = cot.astype(F32) + norm_back(middle, normed, inv_std, norms_ref[4:5, :])
    residual_grad_ref[...] = residual_grad
    low = residual_grad.astype(LOW)
    residual_low_ref[...] = low

    @pl.when(first)
    def _():
        wait_all(copies[marks[2] : marks[3]])

    inner = dot(low, layout.read(out_ref), NN)
    normed, inv_std = norm_of(joined(att_own_ref, att_other_ref))
    add_rows(width_sum_ref, 2, first, 0, inner * normed)
    add_rows(width_sum_ref, 3, first, 0, inner)
    att_grad = norm_back(inner, normed, inv_std, norms_ref[2:3, :]).astype(LOW)
    att_grad_own_ref[...] = att_grad[:, :half]
    att_grad_send_ref[...] = att_grad[:, half:]


def down_backward(layout, place, rowwise, norms, gains, weights):
    hidden_own, _, _, _, _, _, _, _, att_own, _ = rowwise
    rows, half = att_own.shape
    units = hidden_own.shape[1]
    block = min(256, rows)
    shift = rows // block
    return pl.pallas_call(
        functools.partial(down_body, layout),
        grid_spec=pltpu.PrefetchScalarGridSpec(
            num_scalar_prefetch=1,
            grid=(rows // block,),
            in_specs=[
                rows_of(block, units),
                rows_of(block, units),
                rows_of(block, 2 * units),
                rows_of(block, 2 * units),
                rows_of(block, 128),
                rows_of(block, 2 * half),
                rows_of(block, half, shift),
                rows_of(block, half, shift),
                rows_of(block, half),
                rows_of(block, half),
                whole_block(norms),
                whole_block(gains),
            ]
            + [ANYWHERE] * len(weights),
            out_specs=[
                rows_of(block, half),
                rows_of(block, half),
                rows_of(block, units),
                rows_of(block, units),
                rows_of(block, 2 * half),
                rows_of(block, 2 * half),
                rows_of(block, half),
                rows_of(block, half),
                pl.BlockSpec((8, 2 * half), lambda i, place: (0, 0)),
                pl.BlockSpec((8, 2 * units), lambda i, place: (0, 0)),
            ],
            scratch_shapes=[
                pltpu.VMEM((block, 2 * units), F32),
                layout.scratch(2 * units),
                layout.scratch(2 * half),
                layout.scratch(2 * units),
                pltpu.SemaphoreType.DMA((192,)),
            ],
        ),
        out_shape=[
            like(rows, half),
            like(rows, half),
            like(rows, units, dtype=LOW),
            like(rows, units, dtype=LOW),
            like(rows, 2 * half),
            like(rows, 2 * half, dtype=LOW),
            like(rows, half, dtype=LOW),
            like(rows, half, dtype=LOW),
            like(8, 2 * half),
            like(8, 2 * units),
        ],
        compiler_params=params(56),
        cost_estimate=cost(23),
        name="down_backward",
    )(place, *rowwise, norms, gains, *weights)


def emit(layout, ordered_ref, columns, cut, blocks):
    keep_left, send_left, keep_right, send_right = blocks
    middle = keep_left.shape[0]
    rows = ordered_ref[...]
    for value, start in columns:
        result = dot(rows, value, NN).astype(LOW)
        width = value.shape[1]
        if start < cut:
            to = slice(start, start + width)
            keep_left[:, to] = result[:middle]
            send_left[:, to] = result[middle:]
            continue
        to = slice(start - cut, start - cut + width)
        for at, where, size in layout.right_rows():
            target, where = (keep_right, where) if where < middle else (send_right, where - middle)
            target[where : where + size, to] = result[at : at + size]


def column_cuts(width, base, cut, step):
    found, at = [], 0
    while at < width:
        stop = min(at + step, width)
        if base + at < cut < base + stop:
            stop = cut - base
        found.append((at, stop))
        at = stop
    return found


def stacked(own_ref, there_ref, base, cut):
    return [
        (jnp.concatenate([own_ref[:, at:stop], there_ref[:, at:stop]], axis=0), base + at)
        for at, stop in column_cuts(own_ref.shape[1], base, cut, 512)
    ]


def down_grad_body(layout, cut, place, mine_ref, other_ref, own_ref, there_ref, *refs):
    blocks, (columns_ref, ordered_ref) = refs[:4], refs[4:]
    half, tokens = mine_ref.shape[1], own_ref.shape[0]
    for side in range(2):
        row = pl.multiple_of(jnp.bitwise_xor(place[0], side) * tokens, PACKED_ROWS)
        to = slice(side * tokens, (side + 1) * tokens)
        columns_ref[:half, to] = mine_ref[pl.ds(row, tokens), :].T
        columns_ref[half:, to] = other_ref[pl.ds(row, tokens), :].T
    layout.order_rows(columns_ref, ordered_ref, place)
    emit(layout, ordered_ref, stacked(own_ref, there_ref, 0, cut), cut, blocks)


def mid_grad_body(layout, cut, place, *refs):
    pairs, blocks, (columns_ref, ordered_ref) = refs[:8], refs[8:12], refs[12:]
    base = 0
    for number in range(2):
        feat_ref, feat_there_ref, own_ref, there_ref = pairs[4 * number : 4 * number + 4]
        tokens, half = feat_ref.shape[0], feat_ref.shape[1] // 2
        columns_ref[:, :tokens] = feat_ref[...].T
        columns_ref[:half, tokens:] = feat_there_ref[:, half:].T
        columns_ref[half:, tokens:] = feat_there_ref[:, :half].T
        layout.order_rows(columns_ref, ordered_ref, place)
        emit(layout, ordered_ref, stacked(own_ref, there_ref, base, cut), cut, blocks)
        base += own_ref.shape[1]


def in_grad_body(layout, cut, place, feat_ref, mixed_ref, *refs):
    blocks, (columns_ref, ordered_ref) = refs[:4], refs[4:]
    columns_ref[...] = feat_ref[...].T
    layout.order_rows(columns_ref, ordered_ref, place)
    width = mixed_ref.shape[2]
    columns = [
        (mixed_ref[part, :, at:stop], part * width + at)
        for part in range(3)
        for at, stop in column_cuts(width, part * width, cut, width)
    ]
    emit(layout, ordered_ref, columns, cut, blocks)


def weight_grad(layout, body, name, place, cut, width, tokens, arrays, micros):
    rows = layout.rows * layout.paths.count
    columns = (cut, cut, width - cut, width - cut)
    found = pl.pallas_call(
        functools.partial(body, layout, cut),
        grid_spec=pltpu.PrefetchScalarGridSpec(
            num_scalar_prefetch=1,
            grid=(1,),
            in_specs=[whole_block(array) for array in arrays],
            out_specs=[pl.BlockSpec((rows // 2, size), lambda i, place: (0, 0)) for size in columns],
            scratch_shapes=[pltpu.VMEM((rows, tokens), LOW), pltpu.VMEM((rows, tokens), LOW)],
        ),
        out_shape=[like(rows // 2, size, dtype=LOW) for size in columns],
        compiler_params=params(40),
        cost_estimate=cost(micros),
        name=name,
    )(place, *arrays)
    return layout.finish(found, place[2])


def first_body(layout, place, mixed_ref, mine_ref, other_ref, *refs):
    weights, (own_ref, send_ref, sum_ref, scratch, sems) = refs[:-5], refs[-5:]
    first = pl.program_id(0) == 0
    own_blocks = pl.num_programs(0) // 2
    copies = [
        pltpu.make_async_copy(*copy, sems.at[n])
        for n, copy in enumerate(layout.copies(weights, place, [(0, scratch.shape[-1], scratch, 0)]))
    ]

    @pl.when(first)
    def _():
        for copy in copies:
            copy.start()
        sum_ref[...] = jnp.zeros_like(sum_ref)

    normed, _ = norm_of(joined(mine_ref, other_ref).astype(F32))
    grad_mixed = jnp.concatenate([mixed_ref[part] for part in range(3)], axis=1)

    @pl.when(first)
    def _():
        wait_all(copies)

    grad = dot(grad_mixed, layout.read(scratch), NT)
    add_rows(sum_ref, 0, first, 0, grad * normed)
    add_rows(sum_ref, 1, first, 0, grad)

    @pl.when(pl.program_id(0) < own_blocks)
    def _():
        own_ref[...] = grad

    @pl.when(pl.program_id(0) >= own_blocks)
    def _():
        send_ref[...] = grad


def first_backward(layout, place, grad_mixed, mine, other, weights):
    rows, half = mine.shape
    block = min(256, rows // 2)
    count = rows // block

    def own_rows_first(i, place):
        return (i + place[0] * (count // 2)) % count

    return pl.pallas_call(
        functools.partial(first_body, layout),
        grid_spec=pltpu.PrefetchScalarGridSpec(
            num_scalar_prefetch=1,
            grid=(count,),
            in_specs=[
                pl.BlockSpec((3, block, half), lambda i, place: (0, own_rows_first(i, place), 0)),
                pl.BlockSpec((block, half), lambda i, place: (own_rows_first(i, place), 0)),
                pl.BlockSpec((block, half), lambda i, place: (own_rows_first(i, place), 0)),
            ]
            + [ANYWHERE] * len(weights),
            out_specs=[
                pl.BlockSpec((block, 2 * half), lambda i, place: (jnp.minimum(i, count // 2 - 1), 0)),
                pl.BlockSpec((block, 2 * half), lambda i, place: (jnp.maximum(i - count // 2, 0), 0)),
                pl.BlockSpec((8, 2 * half), lambda i, place: (0, 0)),
            ],
            scratch_shapes=[
                layout.scratch(3 * half),
                pltpu.SemaphoreType.DMA((64,)),
            ],
        ),
        out_shape=[like(rows // 2, 2 * half), like(rows // 2, 2 * half), like(8, 2 * half)],
        compiler_params=params(32),
        cost_estimate=cost(6),
        name="first_backward",
    )(place, grad_mixed, mine, other, *weights)


def token_body(place, own_ref, there_ref, mine_ref, other_ref, norms_ref, residual_ref, keep_ref, send_ref):
    half = mine_ref.shape[1]
    normed, inv_std = norm_of(joined(mine_ref, other_ref).astype(F32))
    grad = own_ref[...] + turned(there_ref[...])
    result = residual_ref[...] + norm_back(grad, normed, inv_std, norms_ref[0:1, :])
    keep_ref[...] = result[:, :half]
    send_ref[...] = result[:, half:]


def token_backward(place, own, there, mine, other, norms, residual):
    rows, half = own.shape[0], mine.shape[1]
    block = min(256, rows)
    shift = rows // block
    return pl.pallas_call(
        token_body,
        grid_spec=pltpu.PrefetchScalarGridSpec(
            num_scalar_prefetch=1,
            grid=(rows // block,),
            in_specs=[
                rows_of(block, 2 * half),
                rows_of(block, 2 * half),
                rows_of(block, half, shift),
                rows_of(block, half, shift),
                whole_block(norms),
                rows_of(block, 2 * half),
            ],
            out_specs=[rows_of(block, half), rows_of(block, half)],
        ),
        out_shape=[like(rows, half), like(rows, half)],
        compiler_params=params(24),
        cost_estimate=cost(3),
        name="token_backward",
    )(place, own, there, mine, other, norms, residual)


def in_order_body(place, own_ref, there_ref, out_ref):
    side = pl.program_id(0) // (pl.num_programs(0) // 2)

    @pl.when(side == place[0])
    def _():
        out_ref[...] = own_ref[...]

    @pl.when(side != place[0])
    def _():
        out_ref[...] = there_ref[...]


def in_token_order(place, own, there):
    rows, columns = own.shape
    block = min(256, rows)
    count = rows // block
    source = pl.BlockSpec((block, columns), lambda i, place: (i % count, 0))
    return pl.pallas_call(
        in_order_body,
        grid_spec=pltpu.PrefetchScalarGridSpec(
            num_scalar_prefetch=1,
            grid=(2 * count,),
            in_specs=[source, source],
            out_specs=pl.BlockSpec((block, columns), lambda i, place: (i, 0)),
        ),
        out_shape=like(2 * rows, columns),
        cost_estimate=cost(2),
        name="in_token_order",
    )(place, own, there)


def adam_moments(grad, first, second):
    new_first = BETA_ONE * first + (1.0 - BETA_ONE) * grad
    new_second = BETA_TWO * second + (1.0 - BETA_TWO) * grad * grad
    step_dir = (
        new_first
        / (1.0 - BETA_ONE**STEP)
        / (jnp.sqrt(new_second / (1.0 - BETA_TWO**STEP)) + EPS_ADAM)
    )
    return (new_first, new_second, step_dir)


def at_lane(row, lane, value):
    rows = lax.broadcasted_iota(jnp.int32, (8, 128), 0)
    lanes = lax.broadcasted_iota(jnp.int32, (8, 128), 1)
    return jnp.where((rows == row) & (lanes == lane), value, 0.0)


def sum_of(source):
    return jnp.sum(jnp.sum(source * source, axis=1, keepdims=True), axis=0, keepdims=True)


def moments_body(numbers, cuts, keep_ref, arrived_ref, *refs):
    count = len(numbers)
    states, outs, squares_ref = refs[: 3 * count], refs[3 * count : 6 * count], refs[6 * count]
    squares = jnp.zeros((8, 128), F32)
    for number in range(count):
        master_ref, first_ref, second_ref = states[3 * number : 3 * number + 3]
        new_first_ref, new_second_ref, update_ref = outs[3 * number : 3 * number + 3]
        start, stop = cuts[number]
        grad = keep_ref[:, start:stop] + arrived_ref[:, start:stop].astype(F32)
        parts = master_ref.shape[0] if master_ref.ndim == 3 else 1
        width = (stop - start) // parts
        for part in range(parts):
            pick = (lambda ref: ref.at[part]) if master_ref.ndim == 3 else (lambda ref: ref)
            part_grad = grad[:, part * width : (part + 1) * width] if parts > 1 else grad
            master = pick(master_ref)[...]
            new_first, new_second, step_dir = adam_moments(
                part_grad, pick(first_ref)[...], pick(second_ref)[...]
            )
            update = step_dir + DECAY * master
            pick(new_first_ref)[...] = new_first
            pick(new_second_ref)[...] = new_second
            pick(update_ref)[...] = update
            squares = squares + at_lane(0, numbers[number], sum_of(master))
            squares = squares + at_lane(1, numbers[number], sum_of(update))
    squares_ref[...] = squares


def moments(numbers, cuts, keep, arrived, states, name):
    in_vmem = pl.BlockSpec(memory_space=pltpu.VMEM)
    outs = [like(*state.shape) for state in states]
    return pl.pallas_call(
        functools.partial(moments_body, numbers, cuts),
        in_specs=[in_vmem] * (2 + len(states)),
        out_specs=[in_vmem] * (len(states) + 1),
        out_shape=outs + [like(8, 128)],
        compiler_params=params(40),
        cost_estimate=cost(3),
        name=name,
    )(keep, arrived, *states)


def norm_moments_body(share, packed_ref, *refs):
    states, outs, squares_ref = refs[:6], refs[6:12], refs[12]
    units = states[3].shape[1]
    squares = jnp.zeros((8, 128), F32)
    lane = 4
    for number, (rows, start) in enumerate(((6, units), (2, 0))):
        master_ref, first_ref, second_ref = states[3 * number : 3 * number + 3]
        grad = packed_ref[0:rows, start : start + master_ref.shape[1]]
        master = master_ref[...]
        results = adam_moments(grad, first_ref[...], second_ref[...])
        for ref, result in zip(outs[3 * number : 3 * number + 3], results):
            ref[...] = result
        for row in range(rows):
            squares = squares + at_lane(0, lane, sum_of(master[row : row + 1]) * share)
            squares = squares + at_lane(1, lane, sum_of(results[2][row : row + 1]) * share)
            lane += 1
    squares_ref[...] = squares


def norm_moments(share, packed, states):
    in_vmem = pl.BlockSpec(memory_space=pltpu.VMEM)
    return pl.pallas_call(
        functools.partial(norm_moments_body, share),
        in_specs=[in_vmem] * 7,
        out_specs=[in_vmem] * 7,
        out_shape=[like(*state.shape) for state in states] + [like(8, 128)],
        cost_estimate=cost(1),
        name="norm_moments",
    )(packed, *states)


def apply_body(squares_ref, *refs):
    masters, updates, outs = refs[:6], refs[6:12], refs[12:]
    squares = squares_ref[...]
    ratio = jnp.sqrt(squares[0:1, :] / (squares[1:2, :] + 1e-06)) * RATE
    lanes = lax.broadcasted_iota(jnp.int32, ratio.shape, 1)

    def scale(lane):
        return jnp.sum(jnp.where(lanes == lane, ratio, 0.0), axis=1, keepdims=True)

    lane = 0
    for master_ref, update_ref, out_ref in zip(masters, updates, outs):
        if out_ref.ndim == 3:
            for part in range(out_ref.shape[0]):
                out_ref[part] = master_ref[part] - scale(lane) * update_ref[part]
            lane += 1
        elif lane < 4:
            out_ref[...] = master_ref[...] - scale(lane) * update_ref[...]
            lane += 1
        else:
            rows = out_ref.shape[0]
            factors = jnp.concatenate([scale(lane + row) for row in range(rows)], axis=0)
            out_ref[...] = master_ref[...] - factors * update_ref[...]
            lane += rows


def apply_updates(squares, masters, updates):
    in_vmem = pl.BlockSpec(memory_space=pltpu.VMEM)
    return pl.pallas_call(
        apply_body,
        in_specs=[in_vmem] * 13,
        out_specs=[in_vmem] * 6,
        out_shape=[like(*master.shape) for master in masters],
        compiler_params=params(40),
        cost_estimate=cost(3),
        name="apply_updates",
    )(squares, *masters, *updates)


def shards(
    paths,
    tokens,
    cotangent,
    seq_lengths,
    attn_in,
    attn_out,
    ffn_up,
    ffn_down,
    first_attn_in,
    second_attn_in,
    first_attn_out,
    second_attn_out,
    first_ffn_up,
    second_ffn_up,
    first_ffn_down,
    second_ffn_down,
    width_norm_params,
    first_width_norms,
    second_width_norms,
    hidden_norm_params,
    first_hidden_norms,
    second_hidden_norms,
):
    core = lax.axis_index("tensor")
    index = lax.axis_index("dp")
    mine = index ^ (core * (paths.count // 2))
    place = jnp.stack([core, index, mine]).astype(jnp.int32)
    tok_rows, half = tokens.shape
    units = ffn_up.shape[1]
    layout = Layout(paths, ffn_up.shape[0])

    shard_in = jnp.transpose(attn_in, (1, 0, 2)).reshape(attn_in.shape[1], -1).astype(LOW)
    shard_mid = jnp.concatenate([ffn_up, attn_out.T], axis=1).astype(LOW)
    shard_down = ffn_down.T.astype(LOW)
    cut_in, cut_mid, cut_down = 512, 1024, units // 2
    get_in, get_mid, get_down = [Gather(paths, cut) for cut in (cut_in, cut_mid, cut_down)]
    scatter = Scatter(paths)

    line_in = get_in.shared(get_in.shared(shard_in, 0, mine), 1, mine)
    tok_other = swap(tokens)
    cot_other = swap(cotangent)
    norms = jnp.concatenate([width_norm_params, swap(width_norm_params)], axis=1)
    gains = jnp.concatenate([hidden_norm_params, swap(hidden_norm_params)], axis=1)
    ends = jnp.cumsum(seq_lengths[0])
    line_in, shard_mid, shard_down, tok_other, cot_other, norms, gains, ends = tie(
        line_in, shard_mid, shard_down, tok_other, cot_other, norms, gains, ends
    )
    stacks_in = get_in.step_one(line_in)
    pair_mid = get_mid.shared(shard_mid, 0, mine)
    stacks_in, pair_mid = tie(stacks_in, pair_mid)
    pieces_in = get_in.step_two(stacks_in)
    line_mid = get_mid.shared(pair_mid, 1, mine)
    pieces_in, line_mid, shard_down = tie(pieces_in, line_mid, shard_down)
    weights_in = layout.prepare(pieces_in, mine)
    stacks_mid = get_mid.step_one(line_mid)
    pair_down = get_down.shared(shard_down, 0, mine)
    mixed, feat_one = qkv_forward(layout, place, tokens, tok_other, norms, weights_in)
    mixed, feat_one, stacks_mid, pair_down = tie(mixed, feat_one, stacks_mid, pair_down)
    line_down = get_down.shared(pair_down, 1, mine)
    pieces_mid = get_mid.step_two(stacks_mid)
    early_mid = [swap(pieces_mid[0]), swap(pieces_mid[2])]
    att_own, att_send, logs = attn_forward(place, ends, mixed)
    att_own, att_send, line_down, pieces_mid, early_mid = tie(
        att_own, att_send, line_down, pieces_mid, early_mid
    )
    att_other = swap(att_send)
    late_mid = [swap(pieces_mid[1]), swap(pieces_mid[3])]
    stacks_down = get_down.step_one(line_down)
    att_other, late_mid, stacks_down = tie(att_other, late_mid, stacks_down)
    weights_mid = layout.prepare(pieces_mid, mine) + layout.prepare(
        [early_mid[0], late_mid[0], early_mid[1], late_mid[1]], mine, True
    )
    pieces_down = get_down.step_two(stacks_down)
    early_down = [swap(pieces_down[0]), swap(pieces_down[2])]
    (
        inner_own,
        inner_send,
        residual,
        feat_two,
        hidden_own,
        hidden_send,
        hidden_normed,
        slope,
        hidden_inv,
    ) = up_forward(
        layout, place, att_own, att_other, tokens, tok_other, norms, gains, weights_mid
    )
    pieces_down, early_down, hidden_send, feat_two, inner_send = tie(
        pieces_down, early_down, hidden_send, feat_two, inner_send
    )
    hidden_there = swap(hidden_send)
    late_down = [swap(pieces_down[1]), swap(pieces_down[3])]
    hidden_there, late_down, hidden_own = tie(hidden_there, late_down, hidden_own)
    weights_down = layout.prepare(pieces_down, mine) + layout.prepare(
        [early_down[0], late_down[0], early_down[1], late_down[1]], mine, True
    )
    grad_down = weight_grad(
        layout,
        down_grad_body,
        "down_grad",
        place,
        cut_down,
        units,
        tok_rows,
        (cotangent, cot_other, hidden_own, hidden_there),
        4,
    )
    grad_down, hidden_own, feat_two, inner_send = tie(grad_down, hidden_own, feat_two, inner_send)
    feat_two_there, inner_there = swap(feat_two), swap(inner_send)
    sums_down = scatter.step_one(grad_down)
    (
        output_own,
        output_send,
        raised_own,
        raised_send,
        residual_grad,
        residual_low,
        att_grad_own,
        att_grad_send,
        width_sum,
        hidden_sum,
    ) = down_backward(
        layout,
        place,
        (
            hidden_own,
            hidden_send,
            hidden_normed,
            slope,
            hidden_inv,
            residual,
            cotangent,
            cot_other,
            att_own,
            att_other,
        ),
        norms,
        gains,
        weights_mid + weights_down,
    )
    sums_down, raised_send, residual_low, att_grad_send, feat_two_there, inner_there, output_send = tie(
        sums_down, raised_send, residual_low, att_grad_send, feat_two_there, inner_there, output_send
    )
    raised_there, residual_there = swap(raised_send), swap(residual_low)
    att_grad_other = swap(att_grad_send)
    sums_down, raised_there, residual_there, att_grad_other = tie(
        sums_down, raised_there, residual_there, att_grad_other
    )
    line_sum_down = scatter.step_two(sums_down)
    grad_mid = weight_grad(
        layout,
        mid_grad_body,
        "mid_grad",
        place,
        cut_mid,
        units + half,
        tok_rows,
        (
            feat_two,
            feat_two_there,
            raised_own,
            raised_there,
            residual_low,
            residual_there,
            inner_own,
            inner_there,
        ),
        6,
    )
    grad_mid, line_sum_down, att_grad_other, output_send = tie(
        grad_mid, line_sum_down, att_grad_other, output_send
    )
    output_there = swap(output_send)
    sums_mid = scatter.step_one(grad_mid)
    pair_sum_down = scatter.shared(line_sum_down)
    grad_mixed = attn_backward(place, ends, mixed, att_grad_own, att_grad_other, logs)
    grad_mixed, sums_mid, pair_sum_down, output_there = tie(
        grad_mixed, sums_mid, pair_sum_down, output_there
    )
    line_sum_mid = scatter.step_two(sums_mid)
    keep_down, arrived_down = scatter.last(pair_sum_down)
    grad_in = weight_grad(
        layout, in_grad_body, "in_grad", place, cut_in, 3 * half, tok_rows, (feat_one, grad_mixed), 5
    )
    grad_in, grad_mixed, output_own, output_there = tie(
        grad_in, grad_mixed, output_own, output_there
    )
    sums_in = scatter.step_one(grad_in)
    first_own, first_send, first_sum = first_backward(
        layout, place, grad_mixed, tokens, tok_other, weights_in
    )
    block_output = in_token_order(place, output_own, output_there)
    sums_in, first_own, first_send, first_sum, line_sum_mid, arrived_down, block_output = tie(
        sums_in, first_own, first_send, first_sum, line_sum_mid, arrived_down, block_output
    )
    line_sum_in = scatter.step_two(sums_in)
    pair_sum_mid = scatter.shared(line_sum_mid)
    first_there = swap(first_send)
    width_sum = width_sum + first_sum
    packed = jnp.concatenate([hidden_sum[:, :units], width_sum[:, :half]], axis=1) + swap(
        jnp.concatenate([hidden_sum[:, units:], width_sum[:, half:]], axis=1)
    )

    down_state = moments(
        (3,),
        ((0, units),),
        keep_down,
        arrived_down,
        (ffn_down.T, first_ffn_down.T, second_ffn_down.T),
        "down_moments",
    )
    line_sum_in, pair_sum_mid, first_there, packed, down_state = tie(
        line_sum_in, pair_sum_mid, first_there, packed, down_state
    )
    keep_mid, arrived_mid = scatter.last(pair_sum_mid)
    pair_sum_in = scatter.shared(line_sum_in)
    packed = paths.all_sum(packed)
    keep_in, arrived_in = scatter.last(pair_sum_in)
    mid_state = moments(
        (2, 1),
        ((0, units), (units, units + half)),
        keep_mid,
        arrived_mid,
        (ffn_up, first_ffn_up, second_ffn_up, attn_out.T, first_attn_out.T, second_attn_out.T),
        "mid_moments",
    )
    token_own, token_send = token_backward(
        place, first_own, first_there, tokens, tok_other, norms, residual_grad
    )
    grad_tokens = in_token_order(place, token_own, swap(token_send))
    norm_state = norm_moments(
        1.0 / paths.count,
        packed,
        (
            width_norm_params,
            first_width_norms,
            second_width_norms,
            hidden_norm_params,
            first_hidden_norms,
            second_hidden_norms,
        ),
    )
    in_state = moments(
        (0,),
        ((0, 3 * half),),
        keep_in,
        arrived_in,
        (attn_in, first_attn_in, second_attn_in),
        "in_moments",
    )
    squares = in_state[3] + (mid_state[6] + down_state[3] + norm_state[6])
    squares = paths.all_sum(squares)
    squares = squares + swap(squares)
    new_in, new_out, new_up, new_down, new_width, new_hidden = apply_updates(
        squares,
        (attn_in, attn_out.T, ffn_up, ffn_down.T, width_norm_params, hidden_norm_params),
        (in_state[2], mid_state[5], mid_state[2], down_state[2], norm_state[2], norm_state[5]),
    )
    return (
        block_output,
        grad_tokens,
        new_in,
        new_out.T,
        new_up,
        new_down.T,
        in_state[0],
        mid_state[3].T,
        mid_state[0],
        down_state[0].T,
        in_state[1],
        mid_state[4].T,
        mid_state[1],
        down_state[1].T,
        new_width,
        norm_state[0],
        norm_state[1],
        new_hidden,
        norm_state[3],
        norm_state[4],
    )


def solution(mesh):
    rows = P("dp", "tensor")
    stacked_rows = P(None, "dp", "tensor")
    upright_rows = P("tensor", "dp")
    narrow = P(None, "tensor")
    in_specs = (
        (rows, rows, P("dp", None), stacked_rows, upright_rows, rows, upright_rows)
        + (stacked_rows, stacked_rows, upright_rows, upright_rows)
        + (rows, rows, upright_rows, upright_rows)
        + (narrow,) * 6
    )
    out_specs = (rows, rows) + (stacked_rows, upright_rows, rows, upright_rows) * 3 + (narrow,) * 6
    paths = Paths(mesh.shape["dp"])

    def body(*arrays):
        return shards(paths, *arrays)

    return jax.shard_map(
        body, mesh=mesh, in_specs=in_specs, out_specs=out_specs, check_vma=False
    )
```

```python
import functools

import jax
import jax.numpy as jnp
import numpy as np
from jax import lax
from jax.experimental import pallas as pl
from jax.experimental.pallas import tpu as pltpu
from jax.sharding import PartitionSpec as P

HD = 64
STEP = 10
EPS_NORM = 1e-05
BETA_ONE = 0.9
BETA_TWO = 0.999
EPS_ADAM = 1e-06
DECAY = 0.01
RATE = 0.25
MASKED = -1e30
ROOT_HALF = 0.7071067811865476
ROOT_TURN = 0.3989422804014327
LOW = jnp.bfloat16
F32 = jnp.float32
MIB = 2**20
RATE_FLOPS = 1_000_000
PACKED_ROWS = 16

NN = ((1,), (0,))
NT = ((1,), (1,))
TN = ((0,), (0,))


def dot(left, right, dims):
    return lax.dot_general(left, right, (dims, ((), ())), preferred_element_type=F32)


def tie(*values):
    return lax.optimization_barrier(values)


class Paths:
    def __init__(self, count):
        self.count = count
        if count == 16:
            self.shared, self.one, self.two = (8, 4), (1,), (2,)
        elif count == 128:
            self.shared, self.one, self.two = (64, 32), (4, 2, 1), (16, 8)
        else:
            raise ValueError("dp size")
        self.left = self.shared + self.one + self.two
        self.right = self.shared + self.two + self.one
        self.inner_left = self.one + self.shared + self.two
        self.inner_right = self.two + self.shared + self.one

    def send(self, source, mask):
        pairs = [(device, device ^ mask) for device in range(self.count)]
        return lax.ppermute(source, "dp", pairs)

    def owners(self, masks):
        found = [0]
        for mask in masks:
            found = found + [owner ^ mask for owner in found]
        return np.array(found, np.int32)

    def steps(self):
        return len(self.left)

    def sum_send(self, source, step):
        return source, self.send(source, self.left[-1 - step])

    def all_sum(self, source):
        for step in range(self.steps()):
            source = sum(self.sum_send(source, step))
        return source


class Gather:
    def __init__(self, paths, cut, mine):
        self.paths, self.cut, self.mine = paths, cut, mine

    def send_shared(self, source, step):
        return self.paths.send(source, self.paths.shared[step])

    def join_shared(self, source, arrived, step):
        low = (self.mine & self.paths.shared[step]) == 0
        pair = [jnp.where(low, source, arrived), jnp.where(low, arrived, source)]
        return jnp.stack(pair, axis=step)

    def grow(self, stack, masks):
        for mask in masks:
            stack = jnp.concatenate([stack, self.paths.send(stack, mask)])
        return stack

    def send_one(self, line):
        found = []
        for part, masks in (
            (line[..., : self.cut], self.paths.one),
            (line[..., self.cut :], self.paths.two),
        ):
            part = self.grow(part, masks[:-1])
            found.append((part, self.paths.send(part, masks[-1])))
        return found

    def join_one(self, pairs):
        return [jnp.concatenate(pair) for pair in pairs]

    def send_two(self, stacks):
        found = []
        for stack, masks in zip(stacks, (self.paths.two, self.paths.one)):
            stack = self.grow(stack, masks[:-1])
            found += [stack, self.paths.send(stack, masks[-1])]
        return found

    def even(self):
        return len(self.paths.one) == len(self.paths.two)


class Scatter:
    def __init__(self, paths):
        self.paths = paths

    def settle(self, pair):
        keep, arrived = pair
        size = keep.shape[0] // 2
        kept = keep[:size].astype(F32) + arrived[:size].astype(F32)
        sent = (keep[size:].astype(F32) + arrived[size:].astype(F32)).astype(LOW)
        return kept, sent

    def exchange(self, pair, masks):
        for mask in reversed(masks[1:]):
            pair = self.settle((pair[0], self.paths.send(pair[1], mask)))
        return pair[0], self.paths.send(pair[1], masks[0])

    def send_one(self, blocks):
        return self.exchange(blocks[:2], self.paths.two), self.exchange(blocks[2:], self.paths.one)

    def send_two(self, held):
        return self.send_settled([self.settle(pair) for pair in held])

    def send_settled(self, settled):
        left, right = settled
        return self.exchange(left, self.paths.one), self.exchange(right, self.paths.two)

    def join(self, held):
        left, right = [self.settle(pair) for pair in held]
        return [jnp.concatenate(pair, axis=2) for pair in zip(left, right)]

    def send_shared(self, pair):
        return self.exchange(pair, self.paths.shared[1:])

    def send_shared_at_once(self, held):
        top, low = self.paths.shared
        parts = [
            keep.astype(F32) + arrived.astype(F32) for keep, arrived in held
        ]
        total = jnp.concatenate(parts, axis=2)
        sends = total[1:].astype(LOW)
        return total[0], [
            self.paths.send(sends[number], mask) for number, mask in enumerate((top, low, top ^ low))
        ]

    def send_inner(self, held):
        return self.exchange(self.join(held), self.paths.shared[1:])

    def send_inner_last(self, held):
        return self.exchange(self.settle(held), self.paths.shared[:1])

    def send_ends(self, held, cut):
        keep, send = self.settle(held)
        left = self.exchange((keep[..., :cut], send[..., :cut]), self.paths.one)
        right = self.exchange((keep[..., cut:], send[..., cut:]), self.paths.two)
        return [part[0][0] for part in (left, right)], [part[1][0] for part in (left, right)]

    def send_last(self, held):
        keep, send = self.settle(held)
        return keep[0], self.paths.send(send, self.paths.shared[0])[0]


def swap(source):
    return lax.ppermute(source, "tensor", [(0, 1), (1, 0)])


def own_first(place_ref):
    return place_ref[2]


class Layout:
    def __init__(self, paths, rows):
        self.paths, self.rows = paths, rows
        self.direct = rows % PACKED_ROWS == 0
        self.outer = paths.owners(paths.left), paths.owners(paths.right)
        self.inner = paths.owners(paths.inner_left), paths.owners(paths.inner_right)
        self.wide = 2 ** len(paths.shared)
        self.left_lines = paths.owners(paths.one + paths.two)
        self.right_lines = paths.owners(paths.two + paths.one)

    def prepare(self, pieces, mine, there=False):
        if self.direct:
            return list(pieces)
        whole = []
        lines = self.paths.count // self.wide
        for part, owners in ((pieces[:2], self.left_lines), (pieces[2:], self.right_lines)):
            stack = jnp.concatenate(part)
            inverse = np.argsort(owners).astype(np.int32)
            order = jnp.take(jnp.asarray(inverse), jnp.arange(lines) ^ (mine % lines))
            stack = jnp.swapaxes(jnp.take(stack, order, axis=0), 0, 1)
            if there:
                stack = jnp.roll(stack, self.wide // 2, axis=0)
            whole.append(stack.reshape(-1, stack.shape[3]))
        return whole

    def count(self):
        return 4 if self.direct else 2

    def columns(self, refs):
        return refs[0].shape[-1], refs[-1].shape[-1]

    def scratch(self, columns):
        rows = self.rows * self.paths.count
        if not self.direct:
            return pltpu.VMEM((rows, columns), LOW)
        return pltpu.VMEM((self.wide, self.paths.count // self.wide, self.rows, columns), LOW)

    def read(self, ref, start=0, stop=None):
        value = ref[..., start : ref.shape[-1] if stop is None else stop]
        return value.reshape(-1, value.shape[-1])

    def copies(self, refs, place_ref, spans, there=False, shared_first=False):
        found = []
        cut = refs[0].shape[-1]
        lines = self.paths.count // self.wide
        groups = (
            (0, refs[: len(refs) // 2], self.left_lines),
            (cut, refs[len(refs) // 2 :], self.right_lines),
        )
        for base, part, owners in groups:
            width = part[0].shape[-1]
            for start, stop, target, column in spans:
                low, high = max(start, base), min(stop, base + width)
                if low >= high:
                    continue
                source = pl.ds(low - base, high - low)
                to = pl.ds(column + low - start, high - low)
                if not self.direct:
                    found.append((part[0].at[:, source], target.at[:, to]))
                    continue
                number = 0
                for ref in part:
                    for line in range(ref.shape[1 if shared_first else 0]):
                        owner = (own_first(place_ref) % lines) ^ int(owners[number])
                        size = self.wide // 2 if there else self.wide
                        for at in range(0, self.wide, size):
                            past = self.wide - size - at if there else at
                            block = (pl.ds(at, size), line) if shared_first else (line, pl.ds(at, size))
                            found.append(
                                (ref.at[(*block, slice(None), source)], target.at[pl.ds(past, size), owner, :, to])
                            )
                        number += 1
        return found

    def order_rows(self, source_ref, target_ref, place_ref, owners):
        if not self.direct:
            target_ref[...] = source_ref[...]
            return
        for number, owner in enumerate(owners):
            row = pl.multiple_of((own_first(place_ref) ^ int(owner)) * self.rows, PACKED_ROWS)
            target_ref[number * self.rows : (number + 1) * self.rows, :] = source_ref[
                pl.ds(row, self.rows), :
            ]

    def right_rows(self, order):
        if not self.direct:
            size = self.rows * self.paths.count // 2
            return [(0, 0, size), (size, size, size)]
        left, right = order
        place = {int(owner): number for number, owner in enumerate(right)}
        return [
            (number * self.rows, place[int(owner)] * self.rows, self.rows)
            for number, owner in enumerate(left)
        ]

    def finish(self, blocks, mine, order):
        if self.direct:
            return [block.reshape(-1, self.rows, block.shape[1]) for block in blocks]
        found = []
        for part, owners in zip((blocks[:2], blocks[2:]), order):
            whole = jnp.concatenate(part).reshape(-1, self.rows, part[0].shape[1])
            whole = jnp.take(whole, jnp.asarray(owners) ^ mine, axis=0)
            found += [whole[: self.paths.count // 2], whole[self.paths.count // 2 :]]
        return found


def start_all(copies, sems):
    started = [
        pltpu.make_async_copy(source, target, sems.at[number])
        for number, (source, target) in enumerate(copies)
    ]
    for copy in started:
        copy.start()
    return started


def wait_all(copies):
    for copy in copies:
        copy.wait()


def norm_of(source):
    width = source.shape[1]
    centred = source - jnp.sum(source, axis=1, keepdims=True) * (1.0 / width)
    variance = jnp.sum(centred * centred, axis=1, keepdims=True) * (1.0 / width)
    inv_std = lax.rsqrt(variance + EPS_NORM)
    return centred * inv_std, inv_std


def norm_back(grad_out, normed, inv_std, gain_row):
    width = normed.shape[1]
    scaled = grad_out * gain_row
    mean_plain = jnp.sum(scaled, axis=1, keepdims=True) * (1.0 / width)
    mean_cross = jnp.sum(scaled * normed, axis=1, keepdims=True) * (1.0 / width)
    return inv_std * (scaled - mean_plain - normed * mean_cross)


def add_rows(ref, row, first, at, value):
    columns = value.shape[1]
    held = jnp.where(first, 0.0, ref[row : row + 1, at : at + columns])
    ref[row : row + 1, at : at + columns] = held + jnp.sum(value, axis=0, keepdims=True)


def joined(mine_ref, other_ref):
    return jnp.concatenate([mine_ref[...], other_ref[...]], axis=1)


def whole_block(array):
    zeros = (0,) * array.ndim
    return pl.BlockSpec(array.shape, lambda *_: zeros, pipeline_mode=pl.Buffered(1))


ANYWHERE = pl.BlockSpec(memory_space=pl.ANY)


def like(*shape, dtype=F32):
    return jax.ShapeDtypeStruct(shape, dtype)


def rows_of(block, columns, shift=None):
    if shift is None:
        return pl.BlockSpec((block, columns), lambda i, place: (i, 0))
    return pl.BlockSpec((block, columns), lambda i, place: (i + place[0] * shift, 0))


def cost(micros):
    return pl.CostEstimate(flops=micros * RATE_FLOPS, bytes_accessed=0, transcendentals=0)


def params(mib):
    return pltpu.CompilerParams(vmem_limit_bytes=mib * MIB)


def qkv_body(layout, place, mine_ref, other_ref, norms_ref, *refs):
    weights, (mixed_ref, feat_ref, scratch, sems) = refs[:-4], refs[-4:]
    first = pl.program_id(0) == 0
    copies = layout.copies(weights, place, [(0, scratch.shape[-1], scratch, 0)])

    @pl.when(first)
    def _():
        start_all(copies, sems)

    normed, _ = norm_of(joined(mine_ref, other_ref).astype(F32))
    feat = (normed * norms_ref[0:1, :] + norms_ref[1:2, :]).astype(LOW)
    feat_ref[...] = feat

    @pl.when(first)
    def _():
        wait_all([pltpu.make_async_copy(*copy, sems.at[n]) for n, copy in enumerate(copies)])

    result = dot(feat, layout.read(scratch), NN).astype(LOW)
    width = mixed_ref.shape[2]
    for part in range(3):
        mixed_ref[part] = result[:, part * width : (part + 1) * width]


def qkv_forward(layout, place, mine, other, norms, weights):
    rows, width = mine.shape
    block = min(256, rows)
    return pl.pallas_call(
        functools.partial(qkv_body, layout),
        grid_spec=pltpu.PrefetchScalarGridSpec(
            num_scalar_prefetch=1,
            grid=(rows // block,),
            in_specs=[rows_of(block, width), rows_of(block, width), whole_block(norms)]
            + [ANYWHERE] * len(weights),
            out_specs=[
                pl.BlockSpec((3, block, width), lambda i, place: (0, i, 0)),
                rows_of(block, 2 * width),
            ],
            scratch_shapes=[
                layout.scratch(3 * width),
                pltpu.SemaphoreType.DMA((64,)),
            ],
        ),
        out_shape=[like(3, rows, width, dtype=LOW), like(rows, 2 * width, dtype=LOW)],
        compiler_params=params(24),
        cost_estimate=cost(5),
        name="qkv_forward",
    )(place, mine, other, norms, *weights)


def write_bias(ends_ref, bias_ref, block):
    for at in range(0, bias_ref.shape[1], block):
        keys = at + block
        place = at + lax.broadcasted_iota(jnp.int32, (1, block), 1)
        start = jnp.zeros_like(place)
        for slot in range(ends_ref.shape[0]):
            end = ends_ref[slot]
            start = jnp.maximum(start, jnp.where(end <= place, end, 0))
        key_place = lax.broadcasted_iota(jnp.int32, (keys, block), 0)
        visible = (key_place >= start) & (key_place <= place)
        bias_ref[0:keys, at : at + block] = jnp.where(visible, 0.0, MASKED)


def per_head(source):
    lane = lax.broadcasted_iota(jnp.int32, source.shape, 1)
    zero = jnp.zeros_like(source)
    return jnp.where(lane < HD, source, zero), jnp.where(lane < HD, zero, source)


def attn_forward_body(block, place, ends_ref, mixed_ref, own_ref, send_ref, log_ref, bias_ref):
    rows = mixed_ref.shape[1]

    @pl.when(pl.program_id(0) == 0)
    def _():
        write_bias(ends_ref, bias_ref, block)

    for at in range(0, rows, block):
        keys = at + block
        query = mixed_ref[0, at : at + block, :] * jnp.asarray(HD**-0.5, LOW)
        key = mixed_ref[1, 0:keys, :]
        value = mixed_ref[2, 0:keys, :]
        bias = bias_ref[0:keys, at : at + block]
        total, logs = None, []
        for query_head, value_head in zip(per_head(query), per_head(value)):
            scores = dot(key, query_head, NT) + bias
            top = jnp.max(scores, axis=0, keepdims=True)
            weight = jnp.exp(scores - top)
            norm = jnp.sum(weight, axis=0, keepdims=True)
            logs.append(top + jnp.log(norm))
            part = dot((weight * (1.0 / norm)).astype(LOW), value_head, TN)
            total = part if total is None else total + part
        log_ref[0, :, at : at + block] = jnp.concatenate(logs, axis=0)
        side = (2 * at) // rows
        inner = at - side * (rows // 2)

        @pl.when(place[0] == side)
        def _():
            own_ref[inner : inner + block, :] = total

        @pl.when(place[0] != side)
        def _():
            send_ref[inner : inner + block, :] = total


def attn_forward(place, ends, mixed):
    _, rows, width = mixed.shape
    block = 256
    pairs = width // 128
    return pl.pallas_call(
        functools.partial(attn_forward_body, block),
        grid_spec=pltpu.PrefetchScalarGridSpec(
            num_scalar_prefetch=2,
            grid=(pairs,),
            in_specs=[pl.BlockSpec((3, rows, 128), lambda i, *_: (0, 0, i))],
            out_specs=[
                pl.BlockSpec((rows // 2, 128), lambda i, *_: (0, i)),
                pl.BlockSpec((rows // 2, 128), lambda i, *_: (0, i)),
                pl.BlockSpec((1, 2, rows), lambda i, *_: (i, 0, 0)),
            ],
            scratch_shapes=[pltpu.VMEM((rows, rows), F32)],
        ),
        out_shape=[like(rows // 2, width), like(rows // 2, width), like(pairs, 2, rows)],
        compiler_params=params(40),
        cost_estimate=cost(12),
        name="attn_forward",
    )(place, ends, mixed)


def attn_backward_body(
    block, place, ends_ref, mixed_ref, own_ref, other_ref, log_ref, out_ref, bias_ref, key_sum, value_sum
):
    rows = mixed_ref.shape[1]

    @pl.when(pl.program_id(0) == 0)
    def _():
        write_bias(ends_ref, bias_ref, block)

    scale = jnp.asarray(HD**-0.5, LOW)
    for at in reversed(range(0, rows, block)):
        keys = at + block
        side = (2 * at) // rows
        inner = at - side * (rows // 2)
        query = mixed_ref[0, at : at + block, :] * scale
        grad = jnp.where(
            place[0] == side, own_ref[inner : inner + block, :], other_ref[inner : inner + block, :]
        )
        key = mixed_ref[1, 0:keys, :]
        value = mixed_ref[2, 0:keys, :]
        bias = bias_ref[0:keys, at : at + block]
        sums = None
        heads = zip(per_head(query), per_head(grad), per_head(key))
        for head, (query_head, grad_head, key_head) in enumerate(heads):
            log_total = log_ref[0, head : head + 1, at : at + block]
            probs = jnp.exp(dot(key, query_head, NT) + bias - log_total)
            grad_p = dot(value, grad_head, NT)
            row_sum = jnp.sum(probs * grad_p, axis=0, keepdims=True)
            grad_scores = (probs * (grad_p - row_sum)).astype(LOW)
            parts = (
                dot(grad_scores, key_head, TN),
                dot(grad_scores, query_head, NN),
                dot(probs.astype(LOW), grad_head, NN),
            )
            sums = parts if sums is None else [one + two for one, two in zip(sums, parts)]
        out_ref[0, at : at + block, :] = (sums[0] * HD**-0.5).astype(LOW)
        if keys == rows:
            key_sum[...] = sums[1]
            value_sum[...] = sums[2]
        else:
            key_sum[0:keys, :] += sums[1]
            value_sum[0:keys, :] += sums[2]
    out_ref[1] = key_sum[...].astype(LOW)
    out_ref[2] = value_sum[...].astype(LOW)


def attn_backward(place, ends, mixed, own, other, logs):
    _, rows, width = mixed.shape
    block = 256
    return pl.pallas_call(
        functools.partial(attn_backward_body, block),
        grid_spec=pltpu.PrefetchScalarGridSpec(
            num_scalar_prefetch=2,
            grid=(width // 128,),
            in_specs=[
                pl.BlockSpec((3, rows, 128), lambda i, *_: (0, 0, i)),
                pl.BlockSpec((rows // 2, 128), lambda i, *_: (0, i)),
                pl.BlockSpec((rows // 2, 128), lambda i, *_: (0, i)),
                pl.BlockSpec((1, 2, rows), lambda i, *_: (i, 0, 0)),
            ],
            out_specs=pl.BlockSpec((3, rows, 128), lambda i, *_: (0, 0, i)),
            scratch_shapes=[
                pltpu.VMEM((rows, rows), F32),
                pltpu.VMEM((rows, 128), F32),
                pltpu.VMEM((rows, 128), F32),
            ],
        ),
        out_shape=like(3, rows, width, dtype=LOW),
        compiler_params=params(40),
        cost_estimate=cost(16),
        name="attn_backward",
    )(place, ends, mixed, own, other, logs)


def turned(source):
    half = source.shape[1] // 2
    return jnp.concatenate([source[:, half:], source[:, :half]], axis=1)


def mid_spans(up_scratch, out_scratch, side):
    units, half = up_scratch.shape[-1] // 2, out_scratch.shape[-1] // 2
    return [
        (0, units, up_scratch, side * units),
        (units, units + half, out_scratch, side * half),
    ]


def part_copies(layout, place, groups, shared_first=False):
    found = []
    for side, (refs, spans) in enumerate(groups):
        found += layout.copies(refs, place, spans, side == 1, shared_first)
    return found


def up_body(layout, place, *refs):
    (
        att_own_ref,
        att_other_ref,
        tok_own_ref,
        tok_other_ref,
        norms_ref,
        gains_ref,
    ) = refs[:6]
    count = layout.count()
    own_weights, other_weights = refs[6 : 6 + count], refs[6 + count : 6 + 2 * count]
    (
        inner_own_ref,
        inner_send_ref,
        residual_ref,
        feat_ref,
        hidden_own_ref,
        hidden_send_ref,
        normed_ref,
        slope_ref,
        inv_ref,
        up_ref,
        out_ref,
        sems,
    ) = refs[6 + 2 * count :]
    half = att_own_ref.shape[1]
    units = hidden_own_ref.shape[1]
    step = 512
    first = pl.program_id(0) == 0
    spans = [mid_spans(up_ref, out_ref, side) for side in range(2)]
    out_copies = part_copies(
        layout, place, [(own_weights, spans[0][1:]), (other_weights, spans[1][1:])]
    )
    up_copies = part_copies(
        layout, place, [(own_weights, spans[0][:1]), (other_weights, spans[1][:1])]
    )
    copies = [
        pltpu.make_async_copy(*copy, sems.at[n]) for n, copy in enumerate(out_copies + up_copies)
    ]

    @pl.when(first)
    def _():
        for copy in copies:
            copy.start()

    normed, _ = norm_of(joined(att_own_ref, att_other_ref))
    inner = (normed * norms_ref[2:3, :] + norms_ref[3:4, :]).astype(LOW)
    inner_own_ref[...] = inner[:, :half]
    inner_send_ref[...] = inner[:, half:]

    @pl.when(first)
    def _():
        wait_all(copies[: len(out_copies)])

    residual = joined(tok_own_ref, tok_other_ref).astype(F32) + dot(inner, layout.read(out_ref), NT)
    residual_ref[...] = residual
    normed, _ = norm_of(residual)
    feat = (normed * norms_ref[4:5, :] + norms_ref[5:6, :]).astype(LOW)
    feat_ref[...] = feat

    @pl.when(first)
    def _():
        wait_all(copies[len(out_copies) :])

    total = None
    for at in range(0, 2 * units, step):
        raised = dot(feat, layout.read(up_ref, at, at + step), NN)
        lower = 0.5 + 0.5 * lax.erf(raised * ROOT_HALF)
        active = raised * lower
        slope_ref[:, at : at + step] = lower + raised * (
            jnp.exp(raised * raised * -0.5) * ROOT_TURN
        )
        normed_ref[:, at : at + step] = active
        part = jnp.sum(active, axis=1, keepdims=True)
        total = part if total is None else total + part
    mean = total * (1.0 / (2 * units))
    total = None
    for at in range(0, 2 * units, step):
        centred = normed_ref[:, at : at + step] - mean
        part = jnp.sum(centred * centred, axis=1, keepdims=True)
        total = part if total is None else total + part
    inv_std = lax.rsqrt(total * (1.0 / (2 * units)) + EPS_NORM)
    inv_ref[...] = jnp.broadcast_to(inv_std, inv_ref.shape)
    for at in range(0, 2 * units, step):
        normed = (normed_ref[:, at : at + step] - mean) * inv_std
        normed_ref[:, at : at + step] = normed
        hidden = (normed * gains_ref[0:1, at : at + step] + gains_ref[1:2, at : at + step]).astype(LOW)
        if at < units:
            hidden_own_ref[:, at : at + step] = hidden
        else:
            hidden_send_ref[:, at - units : at - units + step] = hidden


def up_forward(layout, place, att_own, att_other, tok_mine, tok_other, norms, gains, weights):
    rows, half = att_own.shape
    units = gains.shape[1] // 2
    block = min(256, rows)
    shift = rows // block
    return pl.pallas_call(
        functools.partial(up_body, layout),
        grid_spec=pltpu.PrefetchScalarGridSpec(
            num_scalar_prefetch=1,
            grid=(rows // block,),
            in_specs=[
                rows_of(block, half),
                rows_of(block, half),
                rows_of(block, half, shift),
                rows_of(block, half, shift),
                whole_block(norms),
                whole_block(gains),
            ]
            + [ANYWHERE] * len(weights),
            out_specs=[
                rows_of(block, half),
                rows_of(block, half),
                rows_of(block, 2 * half),
                rows_of(block, 2 * half),
                rows_of(block, units),
                rows_of(block, units),
                rows_of(block, 2 * units),
                rows_of(block, 2 * units),
                rows_of(block, 128),
            ],
            scratch_shapes=[
                layout.scratch(2 * units),
                layout.scratch(2 * half),
                pltpu.SemaphoreType.DMA((128,)),
            ],
        ),
        out_shape=[
            like(rows, half, dtype=LOW),
            like(rows, half, dtype=LOW),
            like(rows, 2 * half),
            like(rows, 2 * half, dtype=LOW),
            like(rows, units, dtype=LOW),
            like(rows, units, dtype=LOW),
            like(rows, 2 * units),
            like(rows, 2 * units),
            like(rows, 128),
        ],
        compiler_params=params(48),
        cost_estimate=cost(15),
        name="up_forward",
    )(place, att_own, att_other, tok_mine, tok_other, norms, gains, *weights)


def down_body(layout, place, *refs):
    (
        normed_ref,
        slope_ref,
        inv_ref,
        residual_ref,
        cot_mine_ref,
        cot_other_ref,
        att_own_ref,
        att_other_ref,
        norms_ref,
        gains_ref,
    ) = refs[:10]
    count = layout.count()
    weights = [refs[10 + number * count : 10 + (number + 1) * count] for number in range(4)]
    (
        raised_own_ref,
        raised_send_ref,
        residual_grad_ref,
        residual_low_ref,
        att_grad_own_ref,
        att_grad_send_ref,
        width_sum_ref,
        hidden_sum_ref,
        scaled_ref,
        up_ref,
        out_ref,
        down_ref,
        sems,
    ) = refs[10 + 4 * count :]
    first = pl.program_id(0) == 0
    half = att_own_ref.shape[1]
    units = normed_ref.shape[1] // 2
    spans = [mid_spans(up_ref, out_ref, side) for side in range(2)]
    down_copies = part_copies(
        layout,
        place,
        [(weights[2 + side], [(0, units, down_ref, side * units)]) for side in range(2)],
        shared_first=True,
    )
    up_copies = part_copies(layout, place, [(weights[side], spans[side][:1]) for side in range(2)])
    out_copies = part_copies(layout, place, [(weights[side], spans[side][1:]) for side in range(2)])
    copies = [
        pltpu.make_async_copy(*copy, sems.at[n])
        for n, copy in enumerate(down_copies + up_copies + out_copies)
    ]
    marks = (0, len(down_copies), len(down_copies) + len(up_copies), len(copies))

    @pl.when(first)
    def _():
        for copy in copies:
            copy.start()
        width_sum_ref[...] = jnp.zeros_like(width_sum_ref)
        hidden_sum_ref[...] = jnp.zeros_like(hidden_sum_ref)
        wait_all(copies[marks[0] : marks[1]])

    cot = joined(cot_mine_ref, cot_other_ref)
    residual = residual_ref[...]
    inv_std = inv_ref[:, 0:1]
    sum_plain, sum_cross = None, None
    step = 512
    for at in range(0, 2 * units, step):
        grad = dot(cot, layout.read(down_ref, at, at + step), NN)
        cross = grad * normed_ref[:, at : at + step]
        add_rows(hidden_sum_ref, 0, first, at, cross)
        add_rows(hidden_sum_ref, 1, first, at, grad)
        gain = gains_ref[0:1, at : at + step]
        scaled = grad * gain
        scaled_ref[:, at : at + step] = scaled
        plain = jnp.sum(scaled, axis=1, keepdims=True)
        crossed = jnp.sum(cross * gain, axis=1, keepdims=True)
        sum_plain = plain if sum_plain is None else sum_plain + plain
        sum_cross = crossed if sum_cross is None else sum_cross + crossed
    mean_plain = sum_plain * (1.0 / (2 * units))
    mean_cross = sum_cross * (1.0 / (2 * units))

    @pl.when(first)
    def _():
        wait_all(copies[marks[1] : marks[2]])

    middle = None
    for at in range(0, 2 * units, step):
        active = inv_std * (
            scaled_ref[:, at : at + step] - mean_plain - normed_ref[:, at : at + step] * mean_cross
        )
        raised = (active * slope_ref[:, at : at + step]).astype(LOW)
        if at < units:
            raised_own_ref[:, at : at + step] = raised
        else:
            raised_send_ref[:, at - units : at - units + step] = raised
        part = dot(raised, layout.read(up_ref, at, at + step), NT)
        middle = part if middle is None else middle + part
    normed, inv_std = norm_of(residual)
    add_rows(width_sum_ref, 4, first, 0, middle * normed)
    add_rows(width_sum_ref, 5, first, 0, middle)
    residual_grad = cot.astype(F32) + norm_back(middle, normed, inv_std, norms_ref[4:5, :])
    residual_grad_ref[...] = residual_grad
    low = residual_grad.astype(LOW)
    residual_low_ref[...] = low

    @pl.when(first)
    def _():
        wait_all(copies[marks[2] : marks[3]])

    inner = dot(low, layout.read(out_ref), NN)
    normed, inv_std = norm_of(joined(att_own_ref, att_other_ref))
    add_rows(width_sum_ref, 2, first, 0, inner * normed)
    add_rows(width_sum_ref, 3, first, 0, inner)
    att_grad = norm_back(inner, normed, inv_std, norms_ref[2:3, :]).astype(LOW)
    att_grad_own_ref[...] = att_grad[:, :half]
    att_grad_send_ref[...] = att_grad[:, half:]


def down_backward(layout, place, rowwise, norms, gains, weights):
    hidden_normed, att_own = rowwise[0], rowwise[6]
    rows, half = att_own.shape
    units = hidden_normed.shape[1] // 2
    block = min(256, rows)
    shift = rows // block
    return pl.pallas_call(
        functools.partial(down_body, layout),
        grid_spec=pltpu.PrefetchScalarGridSpec(
            num_scalar_prefetch=1,
            grid=(rows // block,),
            in_specs=[
                rows_of(block, 2 * units),
                rows_of(block, 2 * units),
                rows_of(block, 128),
                rows_of(block, 2 * half),
                rows_of(block, half, shift),
                rows_of(block, half, shift),
                rows_of(block, half),
                rows_of(block, half),
                whole_block(norms),
                whole_block(gains),
            ]
            + [ANYWHERE] * len(weights),
            out_specs=[
                rows_of(block, units),
                rows_of(block, units),
                rows_of(block, 2 * half),
                rows_of(block, 2 * half),
                rows_of(block, half),
                rows_of(block, half),
                pl.BlockSpec((8, 2 * half), lambda i, place: (0, 0)),
                pl.BlockSpec((8, 2 * units), lambda i, place: (0, 0)),
            ],
            scratch_shapes=[
                pltpu.VMEM((block, 2 * units), F32),
                layout.scratch(2 * units),
                layout.scratch(2 * half),
                layout.scratch(2 * units),
                pltpu.SemaphoreType.DMA((192,)),
            ],
        ),
        out_shape=[
            like(rows, units, dtype=LOW),
            like(rows, units, dtype=LOW),
            like(rows, 2 * half),
            like(rows, 2 * half, dtype=LOW),
            like(rows, half, dtype=LOW),
            like(rows, half, dtype=LOW),
            like(8, 2 * half),
            like(8, 2 * units),
        ],
        compiler_params=params(56),
        cost_estimate=cost(23),
        name="down_backward",
    )(place, *rowwise, norms, gains, *weights)


def emit(layout, order, ordered_ref, columns, cut, blocks):
    keep_left, send_left, keep_right, send_right = blocks
    middle = keep_left.shape[0]
    rows = ordered_ref[...]
    for value, start in columns:
        result = dot(rows, value, NN).astype(LOW)
        width = value.shape[1]
        if start < cut:
            to = slice(start, start + width)
            keep_left[:, to] = result[:middle]
            send_left[:, to] = result[middle:]
            continue
        to = slice(start - cut, start - cut + width)
        for at, where, size in layout.right_rows(order):
            target, where = (keep_right, where) if where < middle else (send_right, where - middle)
            target[where : where + size, to] = result[at : at + size]


def column_cuts(width, base, cut, step):
    found, at = [], 0
    while at < width:
        stop = min(at + step, width)
        if base + at < cut < base + stop:
            stop = cut - base
        found.append((at, stop))
        at = stop
    return found


def stacked(own_ref, there_ref, base, cut):
    return [
        (jnp.concatenate([own_ref[:, at:stop], there_ref[:, at:stop]], axis=0), base + at)
        for at, stop in column_cuts(own_ref.shape[1], base, cut, 512)
    ]


def down_grad_body(layout, order, cut, place, mine_ref, other_ref, own_ref, there_ref, *refs):
    blocks, (columns_ref, ordered_ref) = refs[:4], refs[4:]
    half, tokens = mine_ref.shape[1], own_ref.shape[0]
    for side in range(2):
        row = pl.multiple_of(jnp.bitwise_xor(place[0], side) * tokens, PACKED_ROWS)
        to = slice(side * tokens, (side + 1) * tokens)
        columns_ref[:half, to] = mine_ref[pl.ds(row, tokens), :].T
        columns_ref[half:, to] = other_ref[pl.ds(row, tokens), :].T
    layout.order_rows(columns_ref, ordered_ref, place, order[0])
    emit(layout, order, ordered_ref, stacked(own_ref, there_ref, 0, cut), cut, blocks)


def mid_grad_body(layout, order, cut, place, *refs):
    pairs, blocks, (columns_ref, ordered_ref) = refs[:8], refs[8:12], refs[12:]
    base = 0
    for number in range(2):
        feat_ref, feat_there_ref, own_ref, there_ref = pairs[4 * number : 4 * number + 4]
        tokens, half = feat_ref.shape[0], feat_ref.shape[1] // 2
        columns_ref[:, :tokens] = feat_ref[...].T
        columns_ref[:half, tokens:] = feat_there_ref[:, half:].T
        columns_ref[half:, tokens:] = feat_there_ref[:, :half].T
        layout.order_rows(columns_ref, ordered_ref, place, order[0])
        emit(layout, order, ordered_ref, stacked(own_ref, there_ref, base, cut), cut, blocks)
        base += own_ref.shape[1]


def in_grad_body(layout, order, cut, place, feat_ref, mixed_ref, *refs):
    blocks, (columns_ref, ordered_ref) = refs[:4], refs[4:]
    columns_ref[...] = feat_ref[...].T
    layout.order_rows(columns_ref, ordered_ref, place, order[0])
    width = mixed_ref.shape[2]
    columns = [
        (mixed_ref[part, :, at:stop], part * width + at)
        for part in range(3)
        for at, stop in column_cuts(width, part * width, cut, width)
    ]
    emit(layout, order, ordered_ref, columns, cut, blocks)


def weight_grad(layout, order, body, name, place, cut, width, tokens, arrays, micros):
    rows = layout.rows * layout.paths.count
    columns = (cut, cut, width - cut, width - cut)
    found = pl.pallas_call(
        functools.partial(body, layout, order, cut),
        grid_spec=pltpu.PrefetchScalarGridSpec(
            num_scalar_prefetch=1,
            grid=(1,),
            in_specs=[whole_block(array) for array in arrays],
            out_specs=[pl.BlockSpec((rows // 2, size), lambda i, place: (0, 0)) for size in columns],
            scratch_shapes=[pltpu.VMEM((rows, tokens), LOW), pltpu.VMEM((rows, tokens), LOW)],
        ),
        out_shape=[like(rows // 2, size, dtype=LOW) for size in columns],
        compiler_params=params(40),
        cost_estimate=cost(micros),
        name=name,
    )(place, *arrays)
    return layout.finish(found, place[2], order)


def first_body(layout, place, mixed_ref, mine_ref, other_ref, hidden_own_ref, hidden_send_ref, residual_ref, *refs):
    count = layout.count()
    in_refs, down_own_refs, down_other_refs = refs[:count], refs[count : 2 * count], refs[2 * count : 3 * count]
    own_ref, send_ref, sum_ref, output_own_ref, output_send_ref, in_ref, down_ref, sems = refs[3 * count :]
    first = pl.program_id(0) == 0
    own_blocks = pl.num_programs(0) // 2
    half, units = output_send_ref.shape[1], hidden_own_ref.shape[1]
    in_copies = layout.copies(in_refs, place, [(0, in_ref.shape[-1], in_ref, 0)])
    down_copies = part_copies(
        layout,
        place,
        [
            (down_own_refs, [(0, units, down_ref, 0)]),
            (down_other_refs, [(0, units, down_ref, units)]),
        ],
        shared_first=True,
    )
    copies = [
        pltpu.make_async_copy(*copy, sems.at[n]) for n, copy in enumerate(in_copies + down_copies)
    ]

    @pl.when(first)
    def _():
        for copy in copies:
            copy.start()
        sum_ref[...] = jnp.zeros_like(sum_ref)

    normed, _ = norm_of(joined(mine_ref, other_ref).astype(F32))
    grad_mixed = jnp.concatenate([mixed_ref[part] for part in range(3)], axis=1)

    @pl.when(first)
    def _():
        wait_all(copies[: len(in_copies)])

    grad = dot(grad_mixed, layout.read(in_ref), NT)
    add_rows(sum_ref, 0, first, 0, grad * normed)
    add_rows(sum_ref, 1, first, 0, grad)

    @pl.when(first)
    def _():
        wait_all(copies[len(in_copies) :])

    @pl.when(pl.program_id(0) < own_blocks)
    def _():
        own_ref[...] = grad
        output = (
            residual_ref[...]
            + dot(hidden_own_ref[...], layout.read(down_ref, 0, units), NT)
            + dot(hidden_send_ref[...], layout.read(down_ref, units), NT)
        )
        output_own_ref[...] = output[:, :half]
        output_send_ref[...] = output[:, half:]

    @pl.when(pl.program_id(0) >= own_blocks)
    def _():
        send_ref[...] = grad


def first_backward(layout, place, grad_mixed, mine, other, hidden_own, hidden_send, residual, weights):
    rows, half = mine.shape
    units = hidden_own.shape[1]
    block = min(256, rows // 2)
    count = rows // block
    owned = count // 2

    def own_rows_first(i, place):
        return (i + place[0] * owned) % count

    def own_rows(columns):
        return pl.BlockSpec((block, columns), lambda i, place: (jnp.minimum(i, owned - 1), 0))

    return pl.pallas_call(
        functools.partial(first_body, layout),
        grid_spec=pltpu.PrefetchScalarGridSpec(
            num_scalar_prefetch=1,
            grid=(count,),
            in_specs=[
                pl.BlockSpec((3, block, half), lambda i, place: (0, own_rows_first(i, place), 0)),
                pl.BlockSpec((block, half), lambda i, place: (own_rows_first(i, place), 0)),
                pl.BlockSpec((block, half), lambda i, place: (own_rows_first(i, place), 0)),
                own_rows(units),
                own_rows(units),
                own_rows(2 * half),
            ]
            + [ANYWHERE] * len(weights),
            out_specs=[
                own_rows(2 * half),
                pl.BlockSpec((block, 2 * half), lambda i, place: (jnp.maximum(i - owned, 0), 0)),
                pl.BlockSpec((8, 2 * half), lambda i, place: (0, 0)),
                pl.BlockSpec(
                    (block, half),
                    lambda i, place: (jnp.minimum(i, owned - 1) + place[0] * owned, 0),
                ),
                own_rows(half),
            ],
            scratch_shapes=[
                layout.scratch(3 * half),
                layout.scratch(2 * units),
                pltpu.SemaphoreType.DMA((96,)),
            ],
        ),
        out_shape=[
            like(rows // 2, 2 * half),
            like(rows // 2, 2 * half),
            like(8, 2 * half),
            like(rows, half),
            like(rows // 2, half),
        ],
        compiler_params=params(40),
        cost_estimate=cost(11),
        name="first_backward",
    )(place, grad_mixed, mine, other, hidden_own, hidden_send, residual, *weights)


def token_body(place, own_ref, there_ref, mine_ref, other_ref, norms_ref, residual_ref, keep_ref, send_ref):
    half = mine_ref.shape[1]
    normed, inv_std = norm_of(joined(mine_ref, other_ref).astype(F32))
    grad = own_ref[...] + turned(there_ref[...])
    result = residual_ref[...] + norm_back(grad, normed, inv_std, norms_ref[0:1, :])
    keep_ref[...] = result[:, :half]
    send_ref[...] = result[:, half:]


def token_backward(place, own, there, mine, other, norms, residual):
    rows, half = own.shape[0], mine.shape[1]
    block = min(256, rows)
    shift = rows // block
    return pl.pallas_call(
        token_body,
        grid_spec=pltpu.PrefetchScalarGridSpec(
            num_scalar_prefetch=1,
            grid=(rows // block,),
            in_specs=[
                rows_of(block, 2 * half),
                rows_of(block, 2 * half),
                rows_of(block, half, shift),
                rows_of(block, half, shift),
                whole_block(norms),
                rows_of(block, 2 * half),
            ],
            out_specs=[rows_of(block, half, shift), rows_of(block, half)],
        ),
        out_shape=[like(2 * rows, half), like(rows, half)],
        compiler_params=params(24),
        cost_estimate=cost(3),
        name="token_backward",
    )(place, own, there, mine, other, norms, residual)


def fill_body(place, there_ref, whole_ref, out_ref):
    out_ref[...] = there_ref[...]


def fill_there(place, whole, there):
    rows, columns = there.shape
    return pl.pallas_call(
        fill_body,
        grid_spec=pltpu.PrefetchScalarGridSpec(
            num_scalar_prefetch=1,
            grid=(1,),
            in_specs=[pl.BlockSpec((rows, columns), lambda i, place: (0, 0)), ANYWHERE],
            out_specs=pl.BlockSpec((rows, columns), lambda i, place: (1 - place[0], 0)),
        ),
        out_shape=like(2 * rows, columns),
        input_output_aliases={2: 0},
        cost_estimate=cost(2),
        name="fill_there",
    )(place, there, whole)


def adam_moments(grad, first, second):
    new_first = BETA_ONE * first + (1.0 - BETA_ONE) * grad
    new_second = BETA_TWO * second + (1.0 - BETA_TWO) * grad * grad
    step_dir = (
        new_first
        / (1.0 - BETA_ONE**STEP)
        / (jnp.sqrt(new_second / (1.0 - BETA_TWO**STEP)) + EPS_ADAM)
    )
    return (new_first, new_second, step_dir)


def at_lane(row, lane, value):
    rows = lax.broadcasted_iota(jnp.int32, (8, 128), 0)
    lanes = lax.broadcasted_iota(jnp.int32, (8, 128), 1)
    return jnp.where((rows == row) & (lanes == lane), value, 0.0)


def sum_of(source):
    return jnp.sum(jnp.sum(source * source, axis=1, keepdims=True), axis=0, keepdims=True)


def moments_body(numbers, cuts, counts, *refs):
    kept, arrived, refs = refs[: counts[0]], refs[counts[0] : sum(counts)], refs[sum(counts) :]
    count = len(numbers)
    states, outs, squares_ref = refs[: 3 * count], refs[3 * count : 6 * count], refs[6 * count]
    whole = []
    for at, keep_ref in enumerate(kept):
        total = keep_ref[...]
        for ref in arrived[at :: len(kept)]:
            total = total + ref[...].astype(F32)
        whole.append(total)
    whole = jnp.concatenate(whole, axis=1) if len(whole) > 1 else whole[0]
    squares = jnp.zeros((8, 128), F32)
    for number in range(count):
        master_ref, first_ref, second_ref = states[3 * number : 3 * number + 3]
        new_first_ref, new_second_ref, update_ref = outs[3 * number : 3 * number + 3]
        start, stop = cuts[number]
        parts = master_ref.shape[0] if master_ref.ndim == 3 else 1
        width = (stop - start) // parts
        for part in range(parts):
            pick = (lambda ref: ref.at[part]) if master_ref.ndim == 3 else (lambda ref: ref)
            master = pick(master_ref)[...]
            new_first, new_second, step_dir = adam_moments(
                whole[:, start + part * width : start + (part + 1) * width],
                pick(first_ref)[...],
                pick(second_ref)[...],
            )
            update = step_dir + DECAY * master
            pick(new_first_ref)[...] = new_first
            pick(new_second_ref)[...] = new_second
            pick(update_ref)[...] = update
            squares = squares + at_lane(0, numbers[number], sum_of(master))
            squares = squares + at_lane(1, numbers[number], sum_of(update))
    squares_ref[...] = squares


def moments(numbers, cuts, kept, arrived, states, name):
    in_vmem = pl.BlockSpec(memory_space=pltpu.VMEM)
    outs = [like(*state.shape) for state in states]
    counts = (len(kept), len(arrived))
    return pl.pallas_call(
        functools.partial(moments_body, numbers, cuts, counts),
        in_specs=[in_vmem] * (sum(counts) + len(states)),
        out_specs=[in_vmem] * (len(states) + 1),
        out_shape=outs + [like(8, 128)],
        compiler_params=params(40),
        cost_estimate=cost(3),
        name=name,
    )(*kept, *arrived, *states)


def norm_moments_body(packed_ref, *refs):
    states, outs, squares_ref = refs[:6], refs[6:12], refs[12]
    units = states[3].shape[1]
    squares = jnp.zeros((8, 128), F32)
    lane = 4
    for number, (rows, start) in enumerate(((6, units), (2, 0))):
        master_ref, first_ref, second_ref = states[3 * number : 3 * number + 3]
        grad = packed_ref[0:rows, start : start + master_ref.shape[1]]
        master = master_ref[...]
        results = adam_moments(grad, first_ref[...], second_ref[...])
        for ref, result in zip(outs[3 * number : 3 * number + 3], results):
            ref[...] = result
        for row in range(rows):
            squares = squares + at_lane(0, lane, sum_of(master[row : row + 1]))
            squares = squares + at_lane(1, lane, sum_of(results[2][row : row + 1]))
            lane += 1
    squares_ref[...] = squares


def norm_moments(packed, states):
    in_vmem = pl.BlockSpec(memory_space=pltpu.VMEM)
    return pl.pallas_call(
        norm_moments_body,
        in_specs=[in_vmem] * 7,
        out_specs=[in_vmem] * 7,
        out_shape=[like(*state.shape) for state in states] + [like(8, 128)],
        cost_estimate=cost(1),
        name="norm_moments",
    )(packed, *states)


def apply_body(squares_ref, *refs):
    masters, updates, outs = refs[:6], refs[6:12], refs[12:]
    squares = squares_ref[...]
    ratio = jnp.sqrt(squares[0:1, :] / (squares[1:2, :] + 1e-06)) * RATE
    lanes = lax.broadcasted_iota(jnp.int32, ratio.shape, 1)

    def scale(lane):
        return jnp.sum(jnp.where(lanes == lane, ratio, 0.0), axis=1, keepdims=True)

    lane = 0
    for master_ref, update_ref, out_ref in zip(masters, updates, outs):
        if out_ref.ndim == 3:
            for part in range(out_ref.shape[0]):
                out_ref[part] = master_ref[part] - scale(lane) * update_ref[part]
            lane += 1
        elif lane < 4:
            out_ref[...] = master_ref[...] - scale(lane) * update_ref[...]
            lane += 1
        else:
            rows = out_ref.shape[0]
            factors = jnp.concatenate([scale(lane + row) for row in range(rows)], axis=0)
            out_ref[...] = master_ref[...] - factors * update_ref[...]
            lane += rows


def apply_updates(squares, masters, updates):
    in_vmem = pl.BlockSpec(memory_space=pltpu.VMEM)
    return pl.pallas_call(
        apply_body,
        in_specs=[in_vmem] * 13,
        out_specs=[in_vmem] * 6,
        out_shape=[like(*master.shape) for master in masters],
        compiler_params=params(40),
        cost_estimate=cost(3),
        name="apply_updates",
    )(squares, *masters, *updates)


def shards(
    paths,
    tokens,
    cotangent,
    seq_lengths,
    attn_in,
    attn_out,
    ffn_up,
    ffn_down,
    first_attn_in,
    second_attn_in,
    first_attn_out,
    second_attn_out,
    first_ffn_up,
    second_ffn_up,
    first_ffn_down,
    second_ffn_down,
    width_norm_params,
    first_width_norms,
    second_width_norms,
    hidden_norm_params,
    first_hidden_norms,
    second_hidden_norms,
):
    core = lax.axis_index("tensor")
    index = lax.axis_index("dp")
    mine = index ^ (core * (paths.count // 2))
    place = jnp.stack([core, index, mine]).astype(jnp.int32)
    tok_rows, half = tokens.shape
    units = ffn_up.shape[1]
    layout = Layout(paths, ffn_up.shape[0])

    shard_in = jnp.transpose(attn_in, (1, 0, 2)).reshape(attn_in.shape[1], -1).astype(LOW)
    shard_mid = jnp.concatenate([ffn_up, attn_out.T], axis=1).astype(LOW)
    shard_down = ffn_down.T.astype(LOW)
    cut_in, cut_mid, cut_down = 512, 1024, units // 2
    get_in, get_mid, get_down = [Gather(paths, cut, mine) for cut in (cut_in, cut_mid, cut_down)]
    scatter = Scatter(paths)

    arrived_in = get_in.send_shared(shard_in, 0)
    tok_other = swap(tokens)
    cot_other = swap(cotangent)
    norms = jnp.concatenate([width_norm_params, swap(width_norm_params)], axis=1)
    gains = jnp.concatenate([hidden_norm_params, swap(hidden_norm_params)], axis=1)
    ends = jnp.cumsum(seq_lengths[0])
    shard_in, arrived_in, shard_mid, shard_down = tie(shard_in, arrived_in, shard_mid, shard_down)
    pair_in = get_in.join_shared(shard_in, arrived_in, 0)
    arrived_in = get_in.send_shared(pair_in, 1)
    pair_in, arrived_in, shard_mid, shard_down, tok_other, cot_other, norms, gains, ends = tie(
        pair_in, arrived_in, shard_mid, shard_down, tok_other, cot_other, norms, gains, ends
    )
    line_in = get_in.join_shared(pair_in, arrived_in, 1).reshape(1, -1, *shard_in.shape)
    held_in = get_in.send_one(line_in)
    arrived_mid = get_mid.send_shared(shard_mid, 0)
    held_in, shard_down = tie(held_in, shard_down)
    pieces_in = get_in.send_two(get_in.join_one(held_in))
    pair_mid = get_mid.join_shared(shard_mid, arrived_mid, 0)
    arrived_mid = get_mid.send_shared(pair_mid, 1)
    if get_down.even():
        early_down = get_down.send_one(shard_down[None])
        stack_down = jnp.concatenate(get_down.join_one(early_down), axis=2)
    else:
        stack_down = shard_down
    pieces_in, stack_down = tie(pieces_in, stack_down)
    line_mid = get_mid.join_shared(pair_mid, arrived_mid, 1).reshape(1, -1, *shard_mid.shape)
    held_mid = get_mid.send_one(line_mid)
    arrived_down = get_down.send_shared(stack_down, 0)
    weights_in = layout.prepare(pieces_in, mine)
    mixed, feat_one = qkv_forward(layout, place, tokens, tok_other, norms, weights_in)
    mixed, feat_one, held_mid, stack_down, arrived_down = tie(
        mixed, feat_one, held_mid, stack_down, arrived_down
    )
    stack_down = get_down.join_shared(stack_down, arrived_down, 0)
    arrived_down = get_down.send_shared(stack_down, 1)
    stacks_mid = get_mid.join_one(held_mid)
    pieces_mid = get_mid.send_two(stacks_mid)
    early_mid = [swap(pieces_mid[0]), swap(pieces_mid[2])]
    att_own, att_send, logs = attn_forward(place, ends, mixed)
    att_own, att_send, pieces_mid, early_mid, stack_down, arrived_down = tie(
        att_own, att_send, pieces_mid, early_mid, stack_down, arrived_down
    )
    att_other = swap(att_send)
    late_mid = [swap(pieces_mid[1]), swap(pieces_mid[3])]
    line_down = get_down.join_shared(stack_down, arrived_down, 1)
    if get_down.even():
        line_down = line_down.reshape(-1, *line_down.shape[2:])
        stacks_down = [line_down[..., :cut_down], line_down[..., cut_down:]]
    else:
        line_down = line_down.reshape(1, -1, *shard_down.shape)
        stacks_down = get_down.join_one(get_down.send_one(line_down))
    pieces_down = get_down.send_two(stacks_down)
    att_other, late_mid = tie(att_other, late_mid)
    weights_mid = layout.prepare(pieces_mid, mine) + layout.prepare(
        [early_mid[0], late_mid[0], early_mid[1], late_mid[1]], mine, True
    )
    early_down = [swap(pieces_down[0]), swap(pieces_down[2])]
    (
        inner_own,
        inner_send,
        residual,
        feat_two,
        hidden_own,
        hidden_send,
        hidden_normed,
        slope,
        hidden_inv,
    ) = up_forward(
        layout, place, att_own, att_other, tokens, tok_other, norms, gains, weights_mid
    )
    pieces_down, early_down, hidden_send, feat_two, inner_send = tie(
        pieces_down, early_down, hidden_send, feat_two, inner_send
    )
    hidden_there = swap(hidden_send)
    late_down = [swap(pieces_down[1]), swap(pieces_down[3])]
    hidden_there, late_down, hidden_own = tie(hidden_there, late_down, hidden_own)
    weights_down = layout.prepare(pieces_down, mine) + layout.prepare(
        [early_down[0], late_down[0], early_down[1], late_down[1]], mine, True
    )
    grad_down = weight_grad(
        layout,
        layout.outer,
        down_grad_body,
        "down_grad",
        place,
        cut_down,
        units,
        tok_rows,
        (cotangent, cot_other, hidden_own, hidden_there),
        4,
    )
    grad_down, hidden_own, feat_two, inner_send = tie(grad_down, hidden_own, feat_two, inner_send)
    feat_two_there, inner_there = swap(feat_two), swap(inner_send)
    held_down = scatter.send_one(grad_down)
    (
        raised_own,
        raised_send,
        residual_grad,
        residual_low,
        att_grad_own,
        att_grad_send,
        width_sum,
        hidden_sum,
    ) = down_backward(
        layout,
        place,
        (
            hidden_normed,
            slope,
            hidden_inv,
            residual,
            cotangent,
            cot_other,
            att_own,
            att_other,
        ),
        norms,
        gains,
        weights_mid + weights_down,
    )
    held_down, raised_send, residual_low, att_grad_send, feat_two_there, inner_there = tie(
        held_down, raised_send, residual_low, att_grad_send, feat_two_there, inner_there
    )
    raised_there, residual_there = swap(raised_send), swap(residual_low)
    att_grad_other = swap(att_grad_send)
    held_down = scatter.send_two(held_down)
    raised_there, residual_there, att_grad_other = tie(raised_there, residual_there, att_grad_other)
    grad_mid = weight_grad(
        layout,
        layout.outer,
        mid_grad_body,
        "mid_grad",
        place,
        cut_mid,
        units + half,
        tok_rows,
        (
            feat_two,
            feat_two_there,
            raised_own,
            raised_there,
            residual_low,
            residual_there,
            inner_own,
            inner_there,
        ),
        6,
    )
    grad_mid, held_down, att_grad_other = tie(grad_mid, held_down, att_grad_other)
    held_mid = scatter.send_one(grad_mid)
    keep_down, arrived_down = scatter.send_shared_at_once(held_down)
    grad_mixed = attn_backward(place, ends, mixed, att_grad_own, att_grad_other, logs)
    grad_mixed, held_mid, keep_down, arrived_down = tie(grad_mixed, held_mid, keep_down, arrived_down)
    settled_mid = [scatter.settle(pair) for pair in held_mid]
    grad_mixed, settled_mid = tie(grad_mixed, settled_mid)
    held_mid = scatter.send_settled(settled_mid)
    grad_in = weight_grad(
        layout, layout.outer, in_grad_body, "in_grad", place, cut_in, 3 * half, tok_rows, (feat_one, grad_mixed), 5
    )
    grad_in, grad_mixed, held_mid = tie(grad_in, grad_mixed, held_mid)
    held_in = scatter.send_one(grad_in)
    held_mid = scatter.send_shared(scatter.join(held_mid))
    first_own, first_send, first_sum, output_own, output_send = first_backward(
        layout,
        place,
        grad_mixed,
        tokens,
        tok_other,
        hidden_own,
        hidden_send,
        residual,
        weights_in + weights_down,
    )
    held_in, first_own, first_send, first_sum, output_send, arrived_down, held_mid = tie(
        held_in, first_own, first_send, first_sum, output_send, arrived_down, held_mid
    )
    held_in = scatter.send_two(held_in)
    keep_mid, arrived_mid = scatter.send_last(held_mid)
    first_there = swap(first_send)
    down_state = moments(
        (3,),
        ((0, units),),
        [keep_down],
        arrived_down,
        (ffn_down.T, first_ffn_down.T, second_ffn_down.T),
        "down_moments",
    )
    held_in, arrived_mid, first_there, output_send, down_state = tie(
        held_in, arrived_mid, first_there, output_send, down_state
    )
    held_in = scatter.send_shared(scatter.join(held_in))
    output_there = swap(output_send)
    width_sum = width_sum + first_sum
    packed = jnp.concatenate([hidden_sum[:, :units], width_sum[:, :half]], axis=1) + swap(
        jnp.concatenate([hidden_sum[:, units:], width_sum[:, half:]], axis=1)
    )
    held_in, packed, first_there = tie(held_in, packed, first_there)
    keep_in, arrived_in = scatter.send_last(held_in)
    token_own, token_send = token_backward(
        place, first_own, first_there, tokens, tok_other, norms, residual_grad
    )
    packed = paths.sum_send(packed, 0)
    token_there = swap(token_send)
    arrived_in, arrived_mid, down_state, packed, token_own, token_there, output_own, output_there = tie(
        arrived_in, arrived_mid, down_state, packed, token_own, token_there, output_own, output_there
    )
    packed = paths.sum_send(sum(packed), 1)
    in_state = moments(
        (0,),
        ((0, 3 * half),),
        [keep_in],
        [arrived_in],
        (attn_in, first_attn_in, second_attn_in),
        "in_moments",
    )
    mid_state = moments(
        (2, 1),
        ((0, units), (units, units + half)),
        [keep_mid],
        [arrived_mid],
        (ffn_up, first_ffn_up, second_ffn_up, attn_out.T, first_attn_out.T, second_attn_out.T),
        "mid_moments",
    )
    squares = in_state[3] + (mid_state[6] + down_state[3])
    packed = sum(packed)
    squares, packed = tie(squares, packed)
    squares = paths.sum_send(squares, 0)
    packed = paths.sum_send(packed, 2)
    block_output = fill_there(place, output_own, output_there)
    squares, packed, block_output = tie(squares, packed, block_output)
    squares = paths.sum_send(sum(squares), 1)
    for step in range(3, paths.steps()):
        packed = paths.sum_send(sum(packed), step)
    grad_tokens = fill_there(place, token_own, token_there)
    squares, packed, grad_tokens = tie(squares, packed, grad_tokens)
    squares = paths.sum_send(sum(squares), 2)
    packed = sum(packed)
    norm_state = norm_moments(
        packed,
        (
            width_norm_params,
            first_width_norms,
            second_width_norms,
            hidden_norm_params,
            first_hidden_norms,
            second_hidden_norms,
        ),
    )
    squares, norm_state = tie(squares, norm_state)
    for step in range(3, paths.steps()):
        squares = paths.sum_send(sum(squares), step)
    squares = sum(squares) + norm_state[6]
    squares = squares + swap(squares)
    new_in, new_out, new_up, new_down, new_width, new_hidden = apply_updates(
        squares,
        (attn_in, attn_out.T, ffn_up, ffn_down.T, width_norm_params, hidden_norm_params),
        (in_state[2], mid_state[5], mid_state[2], down_state[2], norm_state[2], norm_state[5]),
    )
    return (
        block_output,
        grad_tokens,
        new_in,
        new_out.T,
        new_up,
        new_down.T,
        in_state[0],
        mid_state[3].T,
        mid_state[0],
        down_state[0].T,
        in_state[1],
        mid_state[4].T,
        mid_state[1],
        down_state[1].T,
        new_width,
        norm_state[0],
        norm_state[1],
        new_hidden,
        norm_state[3],
        norm_state[4],
    )


def solution(mesh):
    rows = P("dp", "tensor")
    stacked_rows = P(None, "dp", "tensor")
    upright_rows = P("tensor", "dp")
    narrow = P(None, "tensor")
    in_specs = (
        (rows, rows, P("dp", None), stacked_rows, upright_rows, rows, upright_rows)
        + (stacked_rows, stacked_rows, upright_rows, upright_rows)
        + (rows, rows, upright_rows, upright_rows)
        + (narrow,) * 6
    )
    out_specs = (rows, rows) + (stacked_rows, upright_rows, rows, upright_rows) * 3 + (narrow,) * 6
    paths = Paths(mesh.shape["dp"])

    def body(*arrays):
        return shards(paths, *arrays)

    return jax.shard_map(
        body, mesh=mesh, in_specs=in_specs, out_specs=out_specs, check_vma=False
    )
```

```python
import functools

import jax
import jax.numpy as jnp
import numpy as np
from jax import lax
from jax.experimental import pallas as pl
from jax.experimental.pallas import tpu as pltpu
from jax.sharding import PartitionSpec as P

HD = 64
STEP = 10
EPS_NORM = 1e-05
BETA_ONE = 0.9
BETA_TWO = 0.999
EPS_ADAM = 1e-06
DECAY = 0.01
RATE = 0.25
MASKED = -1e30
ROOT_HALF = 0.7071067811865476
ROOT_TURN = 0.3989422804014327
LOW = jnp.bfloat16
F32 = jnp.float32
MIB = 2**20
RATE_FLOPS = 1_000_000
PACKED_ROWS = 16

NN = ((1,), (0,))
NT = ((1,), (1,))
TN = ((0,), (0,))


def dot(left, right, dims):
    return lax.dot_general(left, right, (dims, ((), ())), preferred_element_type=F32)


def tie(*values):
    return lax.optimization_barrier(values)


class Paths:
    def __init__(self, count):
        self.count = count
        if count == 16:
            self.shared, self.one, self.two = (8, 4), (1,), (2,)
        elif count == 128:
            self.shared, self.one, self.two = (64, 32), (4, 2, 1), (16, 8)
        else:
            raise ValueError("dp size")
        self.left = self.shared + self.one + self.two
        self.right = self.shared + self.two + self.one
        self.inner_left = self.one + self.shared + self.two
        self.inner_right = self.two + self.shared + self.one

    def send(self, source, mask):
        pairs = [(device, device ^ mask) for device in range(self.count)]
        return lax.ppermute(source, "dp", pairs)

    def owners(self, masks):
        found = [0]
        for mask in masks:
            found = found + [owner ^ mask for owner in found]
        return np.array(found, np.int32)

    def steps(self):
        return len(self.left)

    def sum_send(self, source, step):
        return source, self.send(source, self.left[-1 - step])

    def all_sum(self, source):
        for step in range(self.steps()):
            source = sum(self.sum_send(source, step))
        return source


class Gather:
    def __init__(self, paths, cut, mine):
        self.paths, self.cut, self.mine = paths, cut, mine

    def send_shared(self, source, step):
        return self.paths.send(source, self.paths.shared[step])

    def join_shared(self, source, arrived, step):
        low = (self.mine & self.paths.shared[step]) == 0
        pair = [jnp.where(low, source, arrived), jnp.where(low, arrived, source)]
        return jnp.stack(pair, axis=step)

    def grow(self, stack, masks):
        for mask in masks:
            stack = jnp.concatenate([stack, self.paths.send(stack, mask)])
        return stack

    def send_one(self, line):
        found = []
        for part, masks in (
            (line[..., : self.cut], self.paths.one),
            (line[..., self.cut :], self.paths.two),
        ):
            part = self.grow(part, masks[:-1])
            found.append((part, self.paths.send(part, masks[-1])))
        return found

    def join_one(self, pairs):
        return [jnp.concatenate(pair) for pair in pairs]

    def send_two(self, stacks):
        found = []
        for stack, masks in zip(stacks, (self.paths.two, self.paths.one)):
            stack = self.grow(stack, masks[:-1])
            found += [stack, self.paths.send(stack, masks[-1])]
        return found

    def even(self):
        return len(self.paths.one) == len(self.paths.two)


class Scatter:
    def __init__(self, paths):
        self.paths = paths

    def settle(self, pair):
        keep, arrived = pair
        size = keep.shape[0] // 2
        kept = keep[:size].astype(F32) + arrived[:size].astype(F32)
        sent = (keep[size:].astype(F32) + arrived[size:].astype(F32)).astype(LOW)
        return kept, sent

    def exchange(self, pair, masks):
        for mask in reversed(masks[1:]):
            pair = self.settle((pair[0], self.paths.send(pair[1], mask)))
        return pair[0], self.paths.send(pair[1], masks[0])

    def send_one(self, blocks):
        return self.exchange(blocks[:2], self.paths.two), self.exchange(blocks[2:], self.paths.one)

    def send_two(self, held):
        return self.send_settled([self.settle(pair) for pair in held])

    def send_settled(self, settled):
        left, right = settled
        return self.exchange(left, self.paths.one), self.exchange(right, self.paths.two)

    def join(self, held):
        left, right = [self.settle(pair) for pair in held]
        return [jnp.concatenate(pair, axis=2) for pair in zip(left, right)]

    def send_shared(self, pair):
        return self.exchange(pair, self.paths.shared[1:])

    def send_shared_at_once(self, held):
        top, low = self.paths.shared
        parts = [
            keep.astype(F32) + arrived.astype(F32) for keep, arrived in held
        ]
        total = jnp.concatenate(parts, axis=2)
        sends = total[1:].astype(LOW)
        return total[0], [
            self.paths.send(sends[number], mask) for number, mask in enumerate((top, low, top ^ low))
        ]

    def send_inner(self, held):
        return self.exchange(self.join(held), self.paths.shared[1:])

    def send_inner_last(self, held):
        return self.exchange(self.settle(held), self.paths.shared[:1])

    def send_ends(self, held, cut):
        keep, send = self.settle(held)
        left = self.exchange((keep[..., :cut], send[..., :cut]), self.paths.one)
        right = self.exchange((keep[..., cut:], send[..., cut:]), self.paths.two)
        return [part[0][0] for part in (left, right)], [part[1][0] for part in (left, right)]

    def send_last(self, held):
        keep, send = self.settle(held)
        return keep[0], self.paths.send(send, self.paths.shared[0])[0]


def swap(source):
    return lax.ppermute(source, "tensor", [(0, 1), (1, 0)])


def own_first(place_ref):
    return place_ref[2]


class Layout:
    def __init__(self, paths, rows):
        self.paths, self.rows = paths, rows
        self.direct = rows % PACKED_ROWS == 0
        self.outer = paths.owners(paths.left), paths.owners(paths.right)
        self.inner = paths.owners(paths.inner_left), paths.owners(paths.inner_right)
        self.wide = 2 ** len(paths.shared)
        self.left_lines = paths.owners(paths.one + paths.two)
        self.right_lines = paths.owners(paths.two + paths.one)

    def prepare(self, pieces, mine, there=False):
        if self.direct:
            return list(pieces)
        whole = []
        lines = self.paths.count // self.wide
        for part, owners in ((pieces[:2], self.left_lines), (pieces[2:], self.right_lines)):
            stack = jnp.concatenate(part)
            inverse = np.argsort(owners).astype(np.int32)
            order = jnp.take(jnp.asarray(inverse), jnp.arange(lines) ^ (mine % lines))
            stack = jnp.swapaxes(jnp.take(stack, order, axis=0), 0, 1)
            if there:
                stack = jnp.roll(stack, self.wide // 2, axis=0)
            whole.append(stack.reshape(-1, stack.shape[3]))
        return whole

    def count(self):
        return 4 if self.direct else 2

    def columns(self, refs):
        return refs[0].shape[-1], refs[-1].shape[-1]

    def scratch(self, columns):
        rows = self.rows * self.paths.count
        if not self.direct:
            return pltpu.VMEM((rows, columns), LOW)
        return pltpu.VMEM((self.wide, self.paths.count // self.wide, self.rows, columns), LOW)

    def read(self, ref, start=0, stop=None):
        value = ref[..., start : ref.shape[-1] if stop is None else stop]
        return value.reshape(-1, value.shape[-1])

    def copies(self, refs, place_ref, spans, there=False, shared_first=False):
        found = []
        cut = refs[0].shape[-1]
        lines = self.paths.count // self.wide
        groups = (
            (0, refs[: len(refs) // 2], self.left_lines),
            (cut, refs[len(refs) // 2 :], self.right_lines),
        )
        for base, part, owners in groups:
            width = part[0].shape[-1]
            for start, stop, target, column in spans:
                low, high = max(start, base), min(stop, base + width)
                if low >= high:
                    continue
                source = pl.ds(low - base, high - low)
                to = pl.ds(column + low - start, high - low)
                if not self.direct:
                    found.append((part[0].at[:, source], target.at[:, to]))
                    continue
                number = 0
                for ref in part:
                    for line in range(ref.shape[1 if shared_first else 0]):
                        owner = (own_first(place_ref) % lines) ^ int(owners[number])
                        size = self.wide // 2 if there else self.wide
                        for at in range(0, self.wide, size):
                            past = self.wide - size - at if there else at
                            block = (pl.ds(at, size), line) if shared_first else (line, pl.ds(at, size))
                            found.append(
                                (ref.at[(*block, slice(None), source)], target.at[pl.ds(past, size), owner, :, to])
                            )
                        number += 1
        return found

    def order_rows(self, source_ref, target_ref, place_ref, owners):
        if not self.direct:
            target_ref[...] = source_ref[...]
            return
        for number, owner in enumerate(owners):
            row = pl.multiple_of((own_first(place_ref) ^ int(owner)) * self.rows, PACKED_ROWS)
            target_ref[number * self.rows : (number + 1) * self.rows, :] = source_ref[
                pl.ds(row, self.rows), :
            ]

    def right_rows(self, order):
        if not self.direct:
            size = self.rows * self.paths.count // 2
            return [(0, 0, size), (size, size, size)]
        left, right = order
        place = {int(owner): number for number, owner in enumerate(right)}
        return [
            (number * self.rows, place[int(owner)] * self.rows, self.rows)
            for number, owner in enumerate(left)
        ]

    def finish(self, blocks, mine, order):
        if self.direct:
            return [block.reshape(-1, self.rows, block.shape[1]) for block in blocks]
        found = []
        for part, owners in zip((blocks[:2], blocks[2:]), order):
            whole = jnp.concatenate(part).reshape(-1, self.rows, part[0].shape[1])
            whole = jnp.take(whole, jnp.asarray(owners) ^ mine, axis=0)
            found += [whole[: self.paths.count // 2], whole[self.paths.count // 2 :]]
        return found


def start_all(copies, sems):
    started = [
        pltpu.make_async_copy(source, target, sems.at[number])
        for number, (source, target) in enumerate(copies)
    ]
    for copy in started:
        copy.start()
    return started


def wait_all(copies):
    for copy in copies:
        copy.wait()


def norm_of(source):
    width = source.shape[1]
    centred = source - jnp.sum(source, axis=1, keepdims=True) * (1.0 / width)
    variance = jnp.sum(centred * centred, axis=1, keepdims=True) * (1.0 / width)
    inv_std = lax.rsqrt(variance + EPS_NORM)
    return centred * inv_std, inv_std


def norm_back(grad_out, normed, inv_std, gain_row):
    width = normed.shape[1]
    scaled = grad_out * gain_row
    mean_plain = jnp.sum(scaled, axis=1, keepdims=True) * (1.0 / width)
    mean_cross = jnp.sum(scaled * normed, axis=1, keepdims=True) * (1.0 / width)
    return inv_std * (scaled - mean_plain - normed * mean_cross)


def add_rows(ref, row, first, at, value):
    columns = value.shape[1]
    held = jnp.where(first, 0.0, ref[row : row + 1, at : at + columns])
    ref[row : row + 1, at : at + columns] = held + jnp.sum(value, axis=0, keepdims=True)


def joined(mine_ref, other_ref):
    return jnp.concatenate([mine_ref[...], other_ref[...]], axis=1)


def whole_block(array):
    zeros = (0,) * array.ndim
    return pl.BlockSpec(array.shape, lambda *_: zeros, pipeline_mode=pl.Buffered(1))


ANYWHERE = pl.BlockSpec(memory_space=pl.ANY)


def like(*shape, dtype=F32):
    return jax.ShapeDtypeStruct(shape, dtype)


def rows_of(block, columns, shift=None):
    if shift is None:
        return pl.BlockSpec((block, columns), lambda i, place: (i, 0))
    return pl.BlockSpec((block, columns), lambda i, place: (i + place[0] * shift, 0))


def cost(micros):
    return pl.CostEstimate(flops=micros * RATE_FLOPS, bytes_accessed=0, transcendentals=0)


def params(mib):
    return pltpu.CompilerParams(vmem_limit_bytes=mib * MIB)


def qkv_body(layout, place, mine_ref, other_ref, norms_ref, *refs):
    weights, (mixed_ref, feat_ref, scratch, sems) = refs[:-4], refs[-4:]
    first = pl.program_id(0) == 0
    copies = layout.copies(weights, place, [(0, scratch.shape[-1], scratch, 0)])

    @pl.when(first)
    def _():
        start_all(copies, sems)

    normed, _ = norm_of(joined(mine_ref, other_ref).astype(F32))
    feat = (normed * norms_ref[0:1, :] + norms_ref[1:2, :]).astype(LOW)
    feat_ref[...] = feat

    @pl.when(first)
    def _():
        wait_all([pltpu.make_async_copy(*copy, sems.at[n]) for n, copy in enumerate(copies)])

    result = dot(feat, layout.read(scratch), NN).astype(LOW)
    width = mixed_ref.shape[2]
    for part in range(3):
        mixed_ref[part] = result[:, part * width : (part + 1) * width]


def qkv_forward(layout, place, mine, other, norms, weights):
    rows, width = mine.shape
    block = min(256, rows)
    return pl.pallas_call(
        functools.partial(qkv_body, layout),
        grid_spec=pltpu.PrefetchScalarGridSpec(
            num_scalar_prefetch=1,
            grid=(rows // block,),
            in_specs=[rows_of(block, width), rows_of(block, width), whole_block(norms)]
            + [ANYWHERE] * len(weights),
            out_specs=[
                pl.BlockSpec((3, block, width), lambda i, place: (0, i, 0)),
                rows_of(block, 2 * width),
            ],
            scratch_shapes=[
                layout.scratch(3 * width),
                pltpu.SemaphoreType.DMA((64,)),
            ],
        ),
        out_shape=[like(3, rows, width, dtype=LOW), like(rows, 2 * width, dtype=LOW)],
        compiler_params=params(24),
        cost_estimate=cost(5),
        name="qkv_forward",
    )(place, mine, other, norms, *weights)


def write_bias(ends_ref, bias_ref, block):
    for at in range(0, bias_ref.shape[1], block):
        keys = at + block
        place = at + lax.broadcasted_iota(jnp.int32, (1, block), 1)
        start = jnp.zeros_like(place)
        for slot in range(ends_ref.shape[0]):
            end = ends_ref[slot]
            start = jnp.maximum(start, jnp.where(end <= place, end, 0))
        key_place = lax.broadcasted_iota(jnp.int32, (keys, block), 0)
        visible = (key_place >= start) & (key_place <= place)
        bias_ref[0:keys, at : at + block] = jnp.where(visible, 0.0, MASKED)


def per_head(source):
    lane = lax.broadcasted_iota(jnp.int32, source.shape, 1)
    zero = jnp.zeros_like(source)
    return jnp.where(lane < HD, source, zero), jnp.where(lane < HD, zero, source)


def attn_forward_body(block, place, ends_ref, mixed_ref, own_ref, send_ref, log_ref, bias_ref):
    rows = mixed_ref.shape[1]

    @pl.when(pl.program_id(0) == 0)
    def _():
        write_bias(ends_ref, bias_ref, block)

    for at in range(0, rows, block):
        keys = at + block
        query = mixed_ref[0, at : at + block, :] * jnp.asarray(HD**-0.5, LOW)
        key = mixed_ref[1, 0:keys, :]
        value = mixed_ref[2, 0:keys, :]
        bias = bias_ref[0:keys, at : at + block]
        total, logs = None, []
        for query_head, value_head in zip(per_head(query), per_head(value)):
            scores = dot(key, query_head, NT) + bias
            top = jnp.max(scores, axis=0, keepdims=True)
            weight = jnp.exp(scores - top)
            norm = jnp.sum(weight, axis=0, keepdims=True)
            logs.append(top + jnp.log(norm))
            part = dot((weight * (1.0 / norm)).astype(LOW), value_head, TN)
            total = part if total is None else total + part
        log_ref[0, :, at : at + block] = jnp.concatenate(logs, axis=0)
        side = (2 * at) // rows
        inner = at - side * (rows // 2)

        @pl.when(place[0] == side)
        def _():
            own_ref[inner : inner + block, :] = total

        @pl.when(place[0] != side)
        def _():
            send_ref[inner : inner + block, :] = total


def attn_forward(place, ends, mixed):
    _, rows, width = mixed.shape
    block = 256
    pairs = width // 128
    return pl.pallas_call(
        functools.partial(attn_forward_body, block),
        grid_spec=pltpu.PrefetchScalarGridSpec(
            num_scalar_prefetch=2,
            grid=(pairs,),
            in_specs=[pl.BlockSpec((3, rows, 128), lambda i, *_: (0, 0, i))],
            out_specs=[
                pl.BlockSpec((rows // 2, 128), lambda i, *_: (0, i)),
                pl.BlockSpec((rows // 2, 128), lambda i, *_: (0, i)),
                pl.BlockSpec((1, 2, rows), lambda i, *_: (i, 0, 0)),
            ],
            scratch_shapes=[pltpu.VMEM((rows, rows), F32)],
        ),
        out_shape=[like(rows // 2, width), like(rows // 2, width), like(pairs, 2, rows)],
        compiler_params=params(40),
        cost_estimate=cost(12),
        name="attn_forward",
    )(place, ends, mixed)


def attn_backward_body(
    block, place, ends_ref, mixed_ref, own_ref, other_ref, log_ref, out_ref, bias_ref, key_sum, value_sum
):
    rows = mixed_ref.shape[1]

    @pl.when(pl.program_id(0) == 0)
    def _():
        write_bias(ends_ref, bias_ref, block)

    scale = jnp.asarray(HD**-0.5, LOW)
    for at in reversed(range(0, rows, block)):
        keys = at + block
        side = (2 * at) // rows
        inner = at - side * (rows // 2)
        query = mixed_ref[0, at : at + block, :] * scale
        grad = jnp.where(
            place[0] == side, own_ref[inner : inner + block, :], other_ref[inner : inner + block, :]
        )
        key = mixed_ref[1, 0:keys, :]
        value = mixed_ref[2, 0:keys, :]
        bias = bias_ref[0:keys, at : at + block]
        sums = None
        heads = zip(per_head(query), per_head(grad), per_head(key))
        for head, (query_head, grad_head, key_head) in enumerate(heads):
            log_total = log_ref[0, head : head + 1, at : at + block]
            probs = jnp.exp(dot(key, query_head, NT) + bias - log_total)
            grad_p = dot(value, grad_head, NT)
            row_sum = jnp.sum(probs * grad_p, axis=0, keepdims=True)
            grad_scores = (probs * (grad_p - row_sum)).astype(LOW)
            parts = (
                dot(grad_scores, key_head, TN),
                dot(grad_scores, query_head, NN),
                dot(probs.astype(LOW), grad_head, NN),
            )
            sums = parts if sums is None else [one + two for one, two in zip(sums, parts)]
        out_ref[0, at : at + block, :] = (sums[0] * HD**-0.5).astype(LOW)
        if keys == rows:
            key_sum[...] = sums[1]
            value_sum[...] = sums[2]
        else:
            key_sum[0:keys, :] += sums[1]
            value_sum[0:keys, :] += sums[2]
    out_ref[1] = key_sum[...].astype(LOW)
    out_ref[2] = value_sum[...].astype(LOW)


def attn_backward(place, ends, mixed, own, other, logs):
    _, rows, width = mixed.shape
    block = 256
    return pl.pallas_call(
        functools.partial(attn_backward_body, block),
        grid_spec=pltpu.PrefetchScalarGridSpec(
            num_scalar_prefetch=2,
            grid=(width // 128,),
            in_specs=[
                pl.BlockSpec((3, rows, 128), lambda i, *_: (0, 0, i)),
                pl.BlockSpec((rows // 2, 128), lambda i, *_: (0, i)),
                pl.BlockSpec((rows // 2, 128), lambda i, *_: (0, i)),
                pl.BlockSpec((1, 2, rows), lambda i, *_: (i, 0, 0)),
            ],
            out_specs=pl.BlockSpec((3, rows, 128), lambda i, *_: (0, 0, i)),
            scratch_shapes=[
                pltpu.VMEM((rows, rows), F32),
                pltpu.VMEM((rows, 128), F32),
                pltpu.VMEM((rows, 128), F32),
            ],
        ),
        out_shape=like(3, rows, width, dtype=LOW),
        compiler_params=params(40),
        cost_estimate=cost(16),
        name="attn_backward",
    )(place, ends, mixed, own, other, logs)


def turned(source):
    half = source.shape[1] // 2
    return jnp.concatenate([source[:, half:], source[:, :half]], axis=1)


def mid_spans(up_scratch, out_scratch, side):
    units, half = up_scratch.shape[-1] // 2, out_scratch.shape[-1] // 2
    return [
        (0, units, up_scratch, side * units),
        (units, units + half, out_scratch, side * half),
    ]


def part_copies(layout, place, groups, shared_first=False):
    found = []
    for side, (refs, spans) in enumerate(groups):
        found += layout.copies(refs, place, spans, side == 1, shared_first)
    return found


def up_body(layout, place, *refs):
    (
        att_own_ref,
        att_other_ref,
        tok_own_ref,
        tok_other_ref,
        norms_ref,
        gains_ref,
    ) = refs[:6]
    count = layout.count()
    own_weights, other_weights = refs[6 : 6 + count], refs[6 + count : 6 + 2 * count]
    (
        inner_own_ref,
        inner_send_ref,
        residual_ref,
        feat_ref,
        hidden_own_ref,
        hidden_send_ref,
        normed_ref,
        slope_ref,
        inv_ref,
        active_ref,
        up_ref,
        out_ref,
        sems,
    ) = refs[6 + 2 * count :]
    half = att_own_ref.shape[1]
    units = hidden_own_ref.shape[1]
    step = 512
    first = pl.program_id(0) == 0
    spans = [mid_spans(up_ref, out_ref, side) for side in range(2)]
    out_copies = part_copies(
        layout, place, [(own_weights, spans[0][1:]), (other_weights, spans[1][1:])]
    )
    up_copies = part_copies(
        layout, place, [(own_weights, spans[0][:1]), (other_weights, spans[1][:1])]
    )
    copies = [
        pltpu.make_async_copy(*copy, sems.at[n]) for n, copy in enumerate(out_copies + up_copies)
    ]

    @pl.when(first)
    def _():
        for copy in copies:
            copy.start()

    normed, _ = norm_of(joined(att_own_ref, att_other_ref))
    inner = (normed * norms_ref[2:3, :] + norms_ref[3:4, :]).astype(LOW)
    inner_own_ref[...] = inner[:, :half]
    inner_send_ref[...] = inner[:, half:]

    @pl.when(first)
    def _():
        wait_all(copies[: len(out_copies)])

    residual = joined(tok_own_ref, tok_other_ref).astype(F32) + dot(inner, layout.read(out_ref), NT)
    residual_ref[...] = residual
    normed, _ = norm_of(residual)
    feat = (normed * norms_ref[4:5, :] + norms_ref[5:6, :]).astype(LOW)
    feat_ref[...] = feat

    @pl.when(first)
    def _():
        wait_all(copies[len(out_copies) :])

    total = None
    for at in range(0, 2 * units, step):
        raised = dot(feat, layout.read(up_ref, at, at + step), NN)
        lower = 0.5 + 0.5 * lax.erf(raised * ROOT_HALF)
        active = raised * lower
        slope = lower + raised * (jnp.exp(raised * raised * -0.5) * ROOT_TURN)
        slope_ref[:, at : at + step] = slope.astype(LOW)
        active_ref[:, at : at + step] = active
        part = jnp.sum(active, axis=1, keepdims=True)
        total = part if total is None else total + part
    mean = total * (1.0 / (2 * units))
    total = None
    for at in range(0, 2 * units, step):
        centred = active_ref[:, at : at + step] - mean
        part = jnp.sum(centred * centred, axis=1, keepdims=True)
        total = part if total is None else total + part
    inv_std = lax.rsqrt(total * (1.0 / (2 * units)) + EPS_NORM)
    inv_ref[...] = jnp.broadcast_to(inv_std, inv_ref.shape)
    for at in range(0, 2 * units, step):
        normed = (active_ref[:, at : at + step] - mean) * inv_std
        normed_ref[:, at : at + step] = normed.astype(LOW)
        hidden = (normed * gains_ref[0:1, at : at + step] + gains_ref[1:2, at : at + step]).astype(LOW)
        if at < units:
            hidden_own_ref[:, at : at + step] = hidden
        else:
            hidden_send_ref[:, at - units : at - units + step] = hidden


def up_forward(layout, place, att_own, att_other, tok_mine, tok_other, norms, gains, weights):
    rows, half = att_own.shape
    units = gains.shape[1] // 2
    block = min(256, rows)
    shift = rows // block
    return pl.pallas_call(
        functools.partial(up_body, layout),
        grid_spec=pltpu.PrefetchScalarGridSpec(
            num_scalar_prefetch=1,
            grid=(rows // block,),
            in_specs=[
                rows_of(block, half),
                rows_of(block, half),
                rows_of(block, half, shift),
                rows_of(block, half, shift),
                whole_block(norms),
                whole_block(gains),
            ]
            + [ANYWHERE] * len(weights),
            out_specs=[
                rows_of(block, half),
                rows_of(block, half),
                rows_of(block, 2 * half),
                rows_of(block, 2 * half),
                rows_of(block, units),
                rows_of(block, units),
                rows_of(block, 2 * units),
                rows_of(block, 2 * units),
                rows_of(block, 128),
            ],
            scratch_shapes=[
                pltpu.VMEM((block, 2 * units), F32),
                layout.scratch(2 * units),
                layout.scratch(2 * half),
                pltpu.SemaphoreType.DMA((128,)),
            ],
        ),
        out_shape=[
            like(rows, half, dtype=LOW),
            like(rows, half, dtype=LOW),
            like(rows, 2 * half),
            like(rows, 2 * half, dtype=LOW),
            like(rows, units, dtype=LOW),
            like(rows, units, dtype=LOW),
            like(rows, 2 * units, dtype=LOW),
            like(rows, 2 * units, dtype=LOW),
            like(rows, 128),
        ],
        compiler_params=params(48),
        cost_estimate=cost(15),
        name="up_forward",
    )(place, att_own, att_other, tok_mine, tok_other, norms, gains, *weights)


def down_body(layout, place, *refs):
    (
        normed_ref,
        slope_ref,
        inv_ref,
        residual_ref,
        cot_mine_ref,
        cot_other_ref,
        att_own_ref,
        att_other_ref,
        norms_ref,
        gains_ref,
    ) = refs[:10]
    count = layout.count()
    weights = [refs[10 + number * count : 10 + (number + 1) * count] for number in range(4)]
    (
        raised_own_ref,
        raised_send_ref,
        residual_grad_ref,
        residual_low_ref,
        att_grad_own_ref,
        att_grad_send_ref,
        width_sum_ref,
        hidden_sum_ref,
        scaled_ref,
        up_ref,
        out_ref,
        down_ref,
        sems,
    ) = refs[10 + 4 * count :]
    first = pl.program_id(0) == 0
    half = att_own_ref.shape[1]
    units = normed_ref.shape[1] // 2
    spans = [mid_spans(up_ref, out_ref, side) for side in range(2)]
    down_copies = part_copies(
        layout,
        place,
        [(weights[2 + side], [(0, units, down_ref, side * units)]) for side in range(2)],
        shared_first=True,
    )
    up_copies = part_copies(layout, place, [(weights[side], spans[side][:1]) for side in range(2)])
    out_copies = part_copies(layout, place, [(weights[side], spans[side][1:]) for side in range(2)])
    copies = [
        pltpu.make_async_copy(*copy, sems.at[n])
        for n, copy in enumerate(down_copies + up_copies + out_copies)
    ]
    marks = (0, len(down_copies), len(down_copies) + len(up_copies), len(copies))

    @pl.when(first)
    def _():
        for copy in copies:
            copy.start()
        width_sum_ref[...] = jnp.zeros_like(width_sum_ref)
        hidden_sum_ref[...] = jnp.zeros_like(hidden_sum_ref)
        wait_all(copies[marks[0] : marks[1]])

    cot = joined(cot_mine_ref, cot_other_ref)
    residual = residual_ref[...]
    inv_std = inv_ref[:, 0:1]
    sum_plain, sum_cross = None, None
    step = 512
    for at in range(0, 2 * units, step):
        grad = dot(cot, layout.read(down_ref, at, at + step), NN)
        cross = grad * normed_ref[:, at : at + step].astype(F32)
        add_rows(hidden_sum_ref, 0, first, at, cross)
        add_rows(hidden_sum_ref, 1, first, at, grad)
        gain = gains_ref[0:1, at : at + step]
        scaled = grad * gain
        scaled_ref[:, at : at + step] = scaled
        plain = jnp.sum(scaled, axis=1, keepdims=True)
        crossed = jnp.sum(cross * gain, axis=1, keepdims=True)
        sum_plain = plain if sum_plain is None else sum_plain + plain
        sum_cross = crossed if sum_cross is None else sum_cross + crossed
    mean_plain = sum_plain * (1.0 / (2 * units))
    mean_cross = sum_cross * (1.0 / (2 * units))

    @pl.when(first)
    def _():
        wait_all(copies[marks[1] : marks[2]])

    middle = None
    for at in range(0, 2 * units, step):
        active = inv_std * (
            scaled_ref[:, at : at + step]
            - mean_plain
            - normed_ref[:, at : at + step].astype(F32) * mean_cross
        )
        raised = (active * slope_ref[:, at : at + step].astype(F32)).astype(LOW)
        if at < units:
            raised_own_ref[:, at : at + step] = raised
        else:
            raised_send_ref[:, at - units : at - units + step] = raised
        part = dot(raised, layout.read(up_ref, at, at + step), NT)
        middle = part if middle is None else middle + part
    normed, inv_std = norm_of(residual)
    add_rows(width_sum_ref, 4, first, 0, middle * normed)
    add_rows(width_sum_ref, 5, first, 0, middle)
    residual_grad = cot.astype(F32) + norm_back(middle, normed, inv_std, norms_ref[4:5, :])
    residual_grad_ref[...] = residual_grad
    low = residual_grad.astype(LOW)
    residual_low_ref[...] = low

    @pl.when(first)
    def _():
        wait_all(copies[marks[2] : marks[3]])

    inner = dot(low, layout.read(out_ref), NN)
    normed, inv_std = norm_of(joined(att_own_ref, att_other_ref))
    add_rows(width_sum_ref, 2, first, 0, inner * normed)
    add_rows(width_sum_ref, 3, first, 0, inner)
    att_grad = norm_back(inner, normed, inv_std, norms_ref[2:3, :]).astype(LOW)
    att_grad_own_ref[...] = att_grad[:, :half]
    att_grad_send_ref[...] = att_grad[:, half:]


def down_backward(layout, place, rowwise, norms, gains, weights):
    hidden_normed, att_own = rowwise[0], rowwise[6]
    rows, half = att_own.shape
    units = hidden_normed.shape[1] // 2
    block = min(256, rows)
    shift = rows // block
    return pl.pallas_call(
        functools.partial(down_body, layout),
        grid_spec=pltpu.PrefetchScalarGridSpec(
            num_scalar_prefetch=1,
            grid=(rows // block,),
            in_specs=[
                rows_of(block, 2 * units),
                rows_of(block, 2 * units),
                rows_of(block, 128),
                rows_of(block, 2 * half),
                rows_of(block, half, shift),
                rows_of(block, half, shift),
                rows_of(block, half),
                rows_of(block, half),
                whole_block(norms),
                whole_block(gains),
            ]
            + [ANYWHERE] * len(weights),
            out_specs=[
                rows_of(block, units),
                rows_of(block, units),
                rows_of(block, 2 * half),
                rows_of(block, 2 * half),
                rows_of(block, half),
                rows_of(block, half),
                pl.BlockSpec((8, 2 * half), lambda i, place: (0, 0)),
                pl.BlockSpec((8, 2 * units), lambda i, place: (0, 0)),
            ],
            scratch_shapes=[
                pltpu.VMEM((block, 2 * units), F32),
                layout.scratch(2 * units),
                layout.scratch(2 * half),
                layout.scratch(2 * units),
                pltpu.SemaphoreType.DMA((192,)),
            ],
        ),
        out_shape=[
            like(rows, units, dtype=LOW),
            like(rows, units, dtype=LOW),
            like(rows, 2 * half),
            like(rows, 2 * half, dtype=LOW),
            like(rows, half, dtype=LOW),
            like(rows, half, dtype=LOW),
            like(8, 2 * half),
            like(8, 2 * units),
        ],
        compiler_params=params(56),
        cost_estimate=cost(23),
        name="down_backward",
    )(place, *rowwise, norms, gains, *weights)


def emit(layout, order, ordered_ref, columns, cut, blocks):
    keep_left, send_left, keep_right, send_right = blocks
    middle = keep_left.shape[0]
    rows = ordered_ref[...]
    for value, start in columns:
        result = dot(rows, value, NN).astype(LOW)
        width = value.shape[1]
        if start < cut:
            to = slice(start, start + width)
            keep_left[:, to] = result[:middle]
            send_left[:, to] = result[middle:]
            continue
        to = slice(start - cut, start - cut + width)
        for at, where, size in layout.right_rows(order):
            target, where = (keep_right, where) if where < middle else (send_right, where - middle)
            target[where : where + size, to] = result[at : at + size]


def column_cuts(width, base, cut, step):
    found, at = [], 0
    while at < width:
        stop = min(at + step, width)
        if base + at < cut < base + stop:
            stop = cut - base
        found.append((at, stop))
        at = stop
    return found


def stacked(own_ref, there_ref, base, cut):
    return [
        (jnp.concatenate([own_ref[:, at:stop], there_ref[:, at:stop]], axis=0), base + at)
        for at, stop in column_cuts(own_ref.shape[1], base, cut, 512)
    ]


def down_grad_body(layout, order, cut, place, mine_ref, other_ref, own_ref, there_ref, *refs):
    blocks, (columns_ref, ordered_ref) = refs[:4], refs[4:]
    half, tokens = mine_ref.shape[1], own_ref.shape[0]
    for side in range(2):
        row = pl.multiple_of(jnp.bitwise_xor(place[0], side) * tokens, PACKED_ROWS)
        to = slice(side * tokens, (side + 1) * tokens)
        columns_ref[:half, to] = mine_ref[pl.ds(row, tokens), :].T
        columns_ref[half:, to] = other_ref[pl.ds(row, tokens), :].T
    layout.order_rows(columns_ref, ordered_ref, place, order[0])
    emit(layout, order, ordered_ref, stacked(own_ref, there_ref, 0, cut), cut, blocks)


def mid_grad_body(layout, order, cut, place, *refs):
    pairs, blocks, (columns_ref, ordered_ref) = refs[:8], refs[8:12], refs[12:]
    base = 0
    for number in range(2):
        feat_ref, feat_there_ref, own_ref, there_ref = pairs[4 * number : 4 * number + 4]
        tokens, half = feat_ref.shape[0], feat_ref.shape[1] // 2
        columns_ref[:, :tokens] = feat_ref[...].T
        columns_ref[:half, tokens:] = feat_there_ref[:, half:].T
        columns_ref[half:, tokens:] = feat_there_ref[:, :half].T
        layout.order_rows(columns_ref, ordered_ref, place, order[0])
        emit(layout, order, ordered_ref, stacked(own_ref, there_ref, base, cut), cut, blocks)
        base += own_ref.shape[1]


def in_grad_body(layout, order, cut, place, feat_ref, mixed_ref, *refs):
    blocks, (columns_ref, ordered_ref) = refs[:4], refs[4:]
    columns_ref[...] = feat_ref[...].T
    layout.order_rows(columns_ref, ordered_ref, place, order[0])
    width = mixed_ref.shape[2]
    columns = [
        (mixed_ref[part, :, at:stop], part * width + at)
        for part in range(3)
        for at, stop in column_cuts(width, part * width, cut, width)
    ]
    emit(layout, order, ordered_ref, columns, cut, blocks)


def weight_grad(layout, order, body, name, place, cut, width, tokens, arrays, micros):
    rows = layout.rows * layout.paths.count
    columns = (cut, cut, width - cut, width - cut)
    found = pl.pallas_call(
        functools.partial(body, layout, order, cut),
        grid_spec=pltpu.PrefetchScalarGridSpec(
            num_scalar_prefetch=1,
            grid=(1,),
            in_specs=[whole_block(array) for array in arrays],
            out_specs=[pl.BlockSpec((rows // 2, size), lambda i, place: (0, 0)) for size in columns],
            scratch_shapes=[pltpu.VMEM((rows, tokens), LOW), pltpu.VMEM((rows, tokens), LOW)],
        ),
        out_shape=[like(rows // 2, size, dtype=LOW) for size in columns],
        compiler_params=params(40),
        cost_estimate=cost(micros),
        name=name,
    )(place, *arrays)
    return layout.finish(found, place[2], order)


def first_body(layout, place, mixed_ref, mine_ref, other_ref, hidden_own_ref, hidden_send_ref, residual_ref, *refs):
    count = layout.count()
    in_refs, down_own_refs, down_other_refs = refs[:count], refs[count : 2 * count], refs[2 * count : 3 * count]
    own_ref, send_ref, sum_ref, output_own_ref, output_send_ref, in_ref, down_ref, sems = refs[3 * count :]
    first = pl.program_id(0) == 0
    own_blocks = pl.num_programs(0) // 2
    half, units = output_send_ref.shape[1], hidden_own_ref.shape[1]
    in_copies = layout.copies(in_refs, place, [(0, in_ref.shape[-1], in_ref, 0)])
    down_copies = part_copies(
        layout,
        place,
        [
            (down_own_refs, [(0, units, down_ref, 0)]),
            (down_other_refs, [(0, units, down_ref, units)]),
        ],
        shared_first=True,
    )
    copies = [
        pltpu.make_async_copy(*copy, sems.at[n]) for n, copy in enumerate(in_copies + down_copies)
    ]

    @pl.when(first)
    def _():
        for copy in copies:
            copy.start()
        sum_ref[...] = jnp.zeros_like(sum_ref)

    normed, _ = norm_of(joined(mine_ref, other_ref).astype(F32))
    grad_mixed = jnp.concatenate([mixed_ref[part] for part in range(3)], axis=1)

    @pl.when(first)
    def _():
        wait_all(copies[: len(in_copies)])

    grad = dot(grad_mixed, layout.read(in_ref), NT)
    add_rows(sum_ref, 0, first, 0, grad * normed)
    add_rows(sum_ref, 1, first, 0, grad)

    @pl.when(first)
    def _():
        wait_all(copies[len(in_copies) :])

    @pl.when(pl.program_id(0) < own_blocks)
    def _():
        own_ref[...] = grad
        output = (
            residual_ref[...]
            + dot(hidden_own_ref[...], layout.read(down_ref, 0, units), NT)
            + dot(hidden_send_ref[...], layout.read(down_ref, units), NT)
        )
        output_own_ref[...] = output[:, :half]
        output_send_ref[...] = output[:, half:]

    @pl.when(pl.program_id(0) >= own_blocks)
    def _():
        send_ref[...] = grad


def first_backward(layout, place, grad_mixed, mine, other, hidden_own, hidden_send, residual, weights):
    rows, half = mine.shape
    units = hidden_own.shape[1]
    block = min(256, rows // 2)
    count = rows // block
    owned = count // 2

    def own_rows_first(i, place):
        return (i + place[0] * owned) % count

    def own_rows(columns):
        return pl.BlockSpec((block, columns), lambda i, place: (jnp.minimum(i, owned - 1), 0))

    return pl.pallas_call(
        functools.partial(first_body, layout),
        grid_spec=pltpu.PrefetchScalarGridSpec(
            num_scalar_prefetch=1,
            grid=(count,),
            in_specs=[
                pl.BlockSpec((3, block, half), lambda i, place: (0, own_rows_first(i, place), 0)),
                pl.BlockSpec((block, half), lambda i, place: (own_rows_first(i, place), 0)),
                pl.BlockSpec((block, half), lambda i, place: (own_rows_first(i, place), 0)),
                own_rows(units),
                own_rows(units),
                own_rows(2 * half),
            ]
            + [ANYWHERE] * len(weights),
            out_specs=[
                own_rows(2 * half),
                pl.BlockSpec((block, 2 * half), lambda i, place: (jnp.maximum(i - owned, 0), 0)),
                pl.BlockSpec((8, 2 * half), lambda i, place: (0, 0)),
                pl.BlockSpec(
                    (block, half),
                    lambda i, place: (jnp.minimum(i, owned - 1) + place[0] * owned, 0),
                ),
                own_rows(half),
            ],
            scratch_shapes=[
                layout.scratch(3 * half),
                layout.scratch(2 * units),
                pltpu.SemaphoreType.DMA((96,)),
            ],
        ),
        out_shape=[
            like(rows // 2, 2 * half),
            like(rows // 2, 2 * half),
            like(8, 2 * half),
            like(rows, half),
            like(rows // 2, half),
        ],
        compiler_params=params(40),
        cost_estimate=cost(11),
        name="first_backward",
    )(place, grad_mixed, mine, other, hidden_own, hidden_send, residual, *weights)


def token_body(place, own_ref, there_ref, mine_ref, other_ref, norms_ref, residual_ref, keep_ref, send_ref):
    half = mine_ref.shape[1]
    normed, inv_std = norm_of(joined(mine_ref, other_ref).astype(F32))
    grad = own_ref[...] + turned(there_ref[...])
    result = residual_ref[...] + norm_back(grad, normed, inv_std, norms_ref[0:1, :])
    keep_ref[...] = result[:, :half]
    send_ref[...] = result[:, half:]


def token_backward(place, own, there, mine, other, norms, residual):
    rows, half = own.shape[0], mine.shape[1]
    block = min(256, rows)
    shift = rows // block
    return pl.pallas_call(
        token_body,
        grid_spec=pltpu.PrefetchScalarGridSpec(
            num_scalar_prefetch=1,
            grid=(rows // block,),
            in_specs=[
                rows_of(block, 2 * half),
                rows_of(block, 2 * half),
                rows_of(block, half, shift),
                rows_of(block, half, shift),
                whole_block(norms),
                rows_of(block, 2 * half),
            ],
            out_specs=[rows_of(block, half, shift), rows_of(block, half)],
        ),
        out_shape=[like(2 * rows, half), like(rows, half)],
        compiler_params=params(24),
        cost_estimate=cost(3),
        name="token_backward",
    )(place, own, there, mine, other, norms, residual)


def fill_body(place, there_ref, whole_ref, out_ref):
    out_ref[...] = there_ref[...]


def fill_there(place, whole, there):
    rows, columns = there.shape
    return pl.pallas_call(
        fill_body,
        grid_spec=pltpu.PrefetchScalarGridSpec(
            num_scalar_prefetch=1,
            grid=(1,),
            in_specs=[pl.BlockSpec((rows, columns), lambda i, place: (0, 0)), ANYWHERE],
            out_specs=pl.BlockSpec((rows, columns), lambda i, place: (1 - place[0], 0)),
        ),
        out_shape=like(2 * rows, columns),
        input_output_aliases={2: 0},
        cost_estimate=cost(2),
        name="fill_there",
    )(place, there, whole)


def adam_moments(grad, first, second):
    new_first = BETA_ONE * first + (1.0 - BETA_ONE) * grad
    new_second = BETA_TWO * second + (1.0 - BETA_TWO) * grad * grad
    step_dir = (
        new_first
        / (1.0 - BETA_ONE**STEP)
        / (jnp.sqrt(new_second / (1.0 - BETA_TWO**STEP)) + EPS_ADAM)
    )
    return (new_first, new_second, step_dir)


def at_lane(row, lane, value):
    rows = lax.broadcasted_iota(jnp.int32, (8, 128), 0)
    lanes = lax.broadcasted_iota(jnp.int32, (8, 128), 1)
    return jnp.where((rows == row) & (lanes == lane), value, 0.0)


def sum_of(source):
    return jnp.sum(jnp.sum(source * source, axis=1, keepdims=True), axis=0, keepdims=True)


def moments_body(numbers, cuts, counts, *refs):
    kept, arrived, refs = refs[: counts[0]], refs[counts[0] : sum(counts)], refs[sum(counts) :]
    count = len(numbers)
    states, outs, squares_ref = refs[: 3 * count], refs[3 * count : 6 * count], refs[6 * count]
    whole = []
    for at, keep_ref in enumerate(kept):
        total = keep_ref[...]
        for ref in arrived[at :: len(kept)]:
            total = total + ref[...].astype(F32)
        whole.append(total)
    whole = jnp.concatenate(whole, axis=1) if len(whole) > 1 else whole[0]
    squares = jnp.zeros((8, 128), F32)
    for number in range(count):
        master_ref, first_ref, second_ref = states[3 * number : 3 * number + 3]
        new_first_ref, new_second_ref, update_ref = outs[3 * number : 3 * number + 3]
        start, stop = cuts[number]
        parts = master_ref.shape[0] if master_ref.ndim == 3 else 1
        width = (stop - start) // parts
        for part in range(parts):
            pick = (lambda ref: ref.at[part]) if master_ref.ndim == 3 else (lambda ref: ref)
            master = pick(master_ref)[...]
            new_first, new_second, step_dir = adam_moments(
                whole[:, start + part * width : start + (part + 1) * width],
                pick(first_ref)[...],
                pick(second_ref)[...],
            )
            update = step_dir + DECAY * master
            pick(new_first_ref)[...] = new_first
            pick(new_second_ref)[...] = new_second
            pick(update_ref)[...] = update
            squares = squares + at_lane(0, numbers[number], sum_of(master))
            squares = squares + at_lane(1, numbers[number], sum_of(update))
    squares_ref[...] = squares


def moments(numbers, cuts, kept, arrived, states, name):
    in_vmem = pl.BlockSpec(memory_space=pltpu.VMEM)
    outs = [like(*state.shape) for state in states]
    counts = (len(kept), len(arrived))
    return pl.pallas_call(
        functools.partial(moments_body, numbers, cuts, counts),
        in_specs=[in_vmem] * (sum(counts) + len(states)),
        out_specs=[in_vmem] * (len(states) + 1),
        out_shape=outs + [like(8, 128)],
        compiler_params=params(40),
        cost_estimate=cost(3),
        name=name,
    )(*kept, *arrived, *states)


def norm_moments_body(packed_ref, *refs):
    states, outs, squares_ref = refs[:6], refs[6:12], refs[12]
    units = states[3].shape[1]
    squares = jnp.zeros((8, 128), F32)
    lane = 4
    for number, (rows, start) in enumerate(((6, units), (2, 0))):
        master_ref, first_ref, second_ref = states[3 * number : 3 * number + 3]
        grad = packed_ref[0:rows, start : start + master_ref.shape[1]]
        master = master_ref[...]
        results = adam_moments(grad, first_ref[...], second_ref[...])
        for ref, result in zip(outs[3 * number : 3 * number + 3], results):
            ref[...] = result
        for row in range(rows):
            squares = squares + at_lane(0, lane, sum_of(master[row : row + 1]))
            squares = squares + at_lane(1, lane, sum_of(results[2][row : row + 1]))
            lane += 1
    squares_ref[...] = squares


def norm_moments(packed, states):
    in_vmem = pl.BlockSpec(memory_space=pltpu.VMEM)
    return pl.pallas_call(
        norm_moments_body,
        in_specs=[in_vmem] * 7,
        out_specs=[in_vmem] * 7,
        out_shape=[like(*state.shape) for state in states] + [like(8, 128)],
        cost_estimate=cost(1),
        name="norm_moments",
    )(packed, *states)


def apply_body(squares_ref, *refs):
    masters, updates, outs = refs[:6], refs[6:12], refs[12:]
    squares = squares_ref[...]
    ratio = jnp.sqrt(squares[0:1, :] / (squares[1:2, :] + 1e-06)) * RATE
    lanes = lax.broadcasted_iota(jnp.int32, ratio.shape, 1)

    def scale(lane):
        return jnp.sum(jnp.where(lanes == lane, ratio, 0.0), axis=1, keepdims=True)

    lane = 0
    for master_ref, update_ref, out_ref in zip(masters, updates, outs):
        if out_ref.ndim == 3:
            for part in range(out_ref.shape[0]):
                out_ref[part] = master_ref[part] - scale(lane) * update_ref[part]
            lane += 1
        elif lane < 4:
            out_ref[...] = master_ref[...] - scale(lane) * update_ref[...]
            lane += 1
        else:
            rows = out_ref.shape[0]
            factors = jnp.concatenate([scale(lane + row) for row in range(rows)], axis=0)
            out_ref[...] = master_ref[...] - factors * update_ref[...]
            lane += rows


def apply_updates(squares, masters, updates):
    in_vmem = pl.BlockSpec(memory_space=pltpu.VMEM)
    return pl.pallas_call(
        apply_body,
        in_specs=[in_vmem] * 13,
        out_specs=[in_vmem] * 6,
        out_shape=[like(*master.shape) for master in masters],
        compiler_params=params(40),
        cost_estimate=cost(3),
        name="apply_updates",
    )(squares, *masters, *updates)


def shards(
    paths,
    tokens,
    cotangent,
    seq_lengths,
    attn_in,
    attn_out,
    ffn_up,
    ffn_down,
    first_attn_in,
    second_attn_in,
    first_attn_out,
    second_attn_out,
    first_ffn_up,
    second_ffn_up,
    first_ffn_down,
    second_ffn_down,
    width_norm_params,
    first_width_norms,
    second_width_norms,
    hidden_norm_params,
    first_hidden_norms,
    second_hidden_norms,
):
    core = lax.axis_index("tensor")
    index = lax.axis_index("dp")
    mine = index ^ (core * (paths.count // 2))
    place = jnp.stack([core, index, mine]).astype(jnp.int32)
    tok_rows, half = tokens.shape
    units = ffn_up.shape[1]
    layout = Layout(paths, ffn_up.shape[0])

    shard_in = jnp.transpose(attn_in, (1, 0, 2)).reshape(attn_in.shape[1], -1).astype(LOW)
    shard_mid = jnp.concatenate([ffn_up, attn_out.T], axis=1).astype(LOW)
    shard_down = ffn_down.T.astype(LOW)
    cut_in, cut_mid, cut_down = 512, 1024, units // 2
    get_in, get_mid, get_down = [Gather(paths, cut, mine) for cut in (cut_in, cut_mid, cut_down)]
    scatter = Scatter(paths)

    arrived_in = get_in.send_shared(shard_in, 0)
    tok_other = swap(tokens)
    cot_other = swap(cotangent)
    norms = jnp.concatenate([width_norm_params, swap(width_norm_params)], axis=1)
    gains = jnp.concatenate([hidden_norm_params, swap(hidden_norm_params)], axis=1)
    ends = jnp.cumsum(seq_lengths[0])
    shard_in, arrived_in, shard_mid, shard_down = tie(shard_in, arrived_in, shard_mid, shard_down)
    pair_in = get_in.join_shared(shard_in, arrived_in, 0)
    arrived_in = get_in.send_shared(pair_in, 1)
    pair_in, arrived_in, shard_mid, shard_down, tok_other, cot_other, norms, gains, ends = tie(
        pair_in, arrived_in, shard_mid, shard_down, tok_other, cot_other, norms, gains, ends
    )
    line_in = get_in.join_shared(pair_in, arrived_in, 1).reshape(1, -1, *shard_in.shape)
    held_in = get_in.send_one(line_in)
    arrived_mid = get_mid.send_shared(shard_mid, 0)
    held_in, shard_down = tie(held_in, shard_down)
    pieces_in = get_in.send_two(get_in.join_one(held_in))
    pair_mid = get_mid.join_shared(shard_mid, arrived_mid, 0)
    arrived_mid = get_mid.send_shared(pair_mid, 1)
    if get_down.even():
        early_down = get_down.send_one(shard_down[None])
        stack_down = jnp.concatenate(get_down.join_one(early_down), axis=2)
    else:
        stack_down = shard_down
    pieces_in, stack_down = tie(pieces_in, stack_down)
    line_mid = get_mid.join_shared(pair_mid, arrived_mid, 1).reshape(1, -1, *shard_mid.shape)
    held_mid = get_mid.send_one(line_mid)
    arrived_down = get_down.send_shared(stack_down, 0)
    weights_in = layout.prepare(pieces_in, mine)
    mixed, feat_one = qkv_forward(layout, place, tokens, tok_other, norms, weights_in)
    mixed, feat_one, held_mid, stack_down, arrived_down = tie(
        mixed, feat_one, held_mid, stack_down, arrived_down
    )
    stack_down = get_down.join_shared(stack_down, arrived_down, 0)
    arrived_down = get_down.send_shared(stack_down, 1)
    stacks_mid = get_mid.join_one(held_mid)
    pieces_mid = get_mid.send_two(stacks_mid)
    early_mid = [swap(pieces_mid[0]), swap(pieces_mid[2])]
    att_own, att_send, logs = attn_forward(place, ends, mixed)
    att_own, att_send, pieces_mid, early_mid, stack_down, arrived_down = tie(
        att_own, att_send, pieces_mid, early_mid, stack_down, arrived_down
    )
    att_other = swap(att_send)
    late_mid = [swap(pieces_mid[1]), swap(pieces_mid[3])]
    line_down = get_down.join_shared(stack_down, arrived_down, 1)
    if get_down.even():
        line_down = line_down.reshape(-1, *line_down.shape[2:])
        stacks_down = [line_down[..., :cut_down], line_down[..., cut_down:]]
    else:
        line_down = line_down.reshape(1, -1, *shard_down.shape)
        stacks_down = get_down.join_one(get_down.send_one(line_down))
    pieces_down = get_down.send_two(stacks_down)
    att_other, late_mid = tie(att_other, late_mid)
    weights_mid = layout.prepare(pieces_mid, mine) + layout.prepare(
        [early_mid[0], late_mid[0], early_mid[1], late_mid[1]], mine, True
    )
    early_down = [swap(pieces_down[0]), swap(pieces_down[2])]
    (
        inner_own,
        inner_send,
        residual,
        feat_two,
        hidden_own,
        hidden_send,
        hidden_normed,
        slope,
        hidden_inv,
    ) = up_forward(
        layout, place, att_own, att_other, tokens, tok_other, norms, gains, weights_mid
    )
    pieces_down, early_down, hidden_send, feat_two, inner_send = tie(
        pieces_down, early_down, hidden_send, feat_two, inner_send
    )
    hidden_there = swap(hidden_send)
    late_down = [swap(pieces_down[1]), swap(pieces_down[3])]
    hidden_there, hidden_own = tie(hidden_there, hidden_own)
    grad_down = weight_grad(
        layout,
        layout.outer,
        down_grad_body,
        "down_grad",
        place,
        cut_down,
        units,
        tok_rows,
        (cotangent, cot_other, hidden_own, hidden_there),
        4,
    )
    grad_down, hidden_own, feat_two, inner_send, late_down = tie(
        grad_down, hidden_own, feat_two, inner_send, late_down
    )
    weights_down = layout.prepare(pieces_down, mine) + layout.prepare(
        [early_down[0], late_down[0], early_down[1], late_down[1]], mine, True
    )
    feat_two_there, inner_there = swap(feat_two), swap(inner_send)
    held_down = scatter.send_one(grad_down)
    (
        raised_own,
        raised_send,
        residual_grad,
        residual_low,
        att_grad_own,
        att_grad_send,
        width_sum,
        hidden_sum,
    ) = down_backward(
        layout,
        place,
        (
            hidden_normed,
            slope,
            hidden_inv,
            residual,
            cotangent,
            cot_other,
            att_own,
            att_other,
        ),
        norms,
        gains,
        weights_mid + weights_down,
    )
    held_down, raised_send, residual_low, att_grad_send, feat_two_there, inner_there = tie(
        held_down, raised_send, residual_low, att_grad_send, feat_two_there, inner_there
    )
    raised_there, residual_there = swap(raised_send), swap(residual_low)
    att_grad_other = swap(att_grad_send)
    held_down = scatter.send_two(held_down)
    raised_there, residual_there = tie(raised_there, residual_there)
    grad_mid = weight_grad(
        layout,
        layout.outer,
        mid_grad_body,
        "mid_grad",
        place,
        cut_mid,
        units + half,
        tok_rows,
        (
            feat_two,
            feat_two_there,
            raised_own,
            raised_there,
            residual_low,
            residual_there,
            inner_own,
            inner_there,
        ),
        6,
    )
    grad_mid, held_down, att_grad_other = tie(grad_mid, held_down, att_grad_other)
    held_mid = scatter.send_one(grad_mid)
    held_down = scatter.send_shared(scatter.join(held_down))
    grad_mixed = attn_backward(place, ends, mixed, att_grad_own, att_grad_other, logs)
    grad_mixed, held_mid, held_down = tie(grad_mixed, held_mid, held_down)
    keep_down, arrived_down = scatter.send_last(held_down)
    settled_mid = [scatter.settle(pair) for pair in held_mid]
    grad_mixed, settled_mid = tie(grad_mixed, settled_mid)
    held_mid = scatter.send_settled(settled_mid)
    grad_in = weight_grad(
        layout, layout.outer, in_grad_body, "in_grad", place, cut_in, 3 * half, tok_rows, (feat_one, grad_mixed), 5
    )
    grad_in, grad_mixed, held_mid = tie(grad_in, grad_mixed, held_mid)
    held_in = scatter.send_one(grad_in)
    held_mid = scatter.send_shared(scatter.join(held_mid))
    first_own, first_send, first_sum, output_own, output_send = first_backward(
        layout,
        place,
        grad_mixed,
        tokens,
        tok_other,
        hidden_own,
        hidden_send,
        residual,
        weights_in + weights_down,
    )
    held_in, first_own, first_send, first_sum, output_send, arrived_down, held_mid = tie(
        held_in, first_own, first_send, first_sum, output_send, arrived_down, held_mid
    )
    held_in = scatter.send_two(held_in)
    keep_mid, arrived_mid = scatter.send_last(held_mid)
    first_there = swap(first_send)
    down_state = moments(
        (3,),
        ((0, units),),
        [keep_down],
        [arrived_down],
        (ffn_down.T, first_ffn_down.T, second_ffn_down.T),
        "down_moments",
    )
    width_sum = width_sum + first_sum
    packed = jnp.concatenate([hidden_sum[:, :units], width_sum[:, :half]], axis=1) + swap(
        jnp.concatenate([hidden_sum[:, units:], width_sum[:, half:]], axis=1)
    )
    held_in, arrived_mid, first_there, output_send, down_state, packed = tie(
        held_in, arrived_mid, first_there, output_send, down_state, packed
    )
    held_in = scatter.send_shared(scatter.join(held_in))
    packed = paths.sum_send(packed, 0)
    output_there = swap(output_send)
    held_in, packed, first_there, output_there = tie(held_in, packed, first_there, output_there)
    keep_in, arrived_in = scatter.send_last(held_in)
    token_own, token_send = token_backward(
        place, first_own, first_there, tokens, tok_other, norms, residual_grad
    )
    arrived_in, token_send, packed = tie(arrived_in, token_send, packed)
    packed = paths.sum_send(sum(packed), 1)
    token_there = swap(token_send)
    in_state = moments(
        (0,),
        ((0, 3 * half),),
        [keep_in],
        [arrived_in],
        (attn_in, first_attn_in, second_attn_in),
        "in_moments",
    )
    mid_state = moments(
        (2, 1),
        ((0, units), (units, units + half)),
        [keep_mid],
        [arrived_mid],
        (ffn_up, first_ffn_up, second_ffn_up, attn_out.T, first_attn_out.T, second_attn_out.T),
        "mid_moments",
    )
    squares = in_state[3] + (mid_state[6] + down_state[3])
    packed = sum(packed)
    squares, packed, token_there = tie(squares, packed, token_there)
    squares = paths.sum_send(squares, 0)
    packed = paths.sum_send(packed, 2)
    block_output = fill_there(place, output_own, output_there)
    squares, packed, block_output = tie(squares, packed, block_output)
    squares = paths.sum_send(sum(squares), 1)
    for step in range(3, paths.steps()):
        packed = paths.sum_send(sum(packed), step)
    squares, packed = tie(squares, packed)
    squares = paths.sum_send(sum(squares), 2)
    packed = sum(packed)
    norm_state = norm_moments(
        packed,
        (
            width_norm_params,
            first_width_norms,
            second_width_norms,
            hidden_norm_params,
            first_hidden_norms,
            second_hidden_norms,
        ),
    )
    squares, norm_state = tie(squares, norm_state)
    squares = paths.sum_send(sum(squares), 3)
    grad_tokens = fill_there(place, token_own, token_there)
    squares, grad_tokens = tie(squares, grad_tokens)
    for step in range(4, paths.steps()):
        squares = paths.sum_send(sum(squares), step)
    squares = sum(squares) + norm_state[6]
    squares = squares + swap(squares)
    new_in, new_out, new_up, new_down, new_width, new_hidden = apply_updates(
        squares,
        (attn_in, attn_out.T, ffn_up, ffn_down.T, width_norm_params, hidden_norm_params),
        (in_state[2], mid_state[5], mid_state[2], down_state[2], norm_state[2], norm_state[5]),
    )
    return (
        block_output,
        grad_tokens,
        new_in,
        new_out.T,
        new_up,
        new_down.T,
        in_state[0],
        mid_state[3].T,
        mid_state[0],
        down_state[0].T,
        in_state[1],
        mid_state[4].T,
        mid_state[1],
        down_state[1].T,
        new_width,
        norm_state[0],
        norm_state[1],
        new_hidden,
        norm_state[3],
        norm_state[4],
    )


def solution(mesh):
    rows = P("dp", "tensor")
    stacked_rows = P(None, "dp", "tensor")
    upright_rows = P("tensor", "dp")
    narrow = P(None, "tensor")
    in_specs = (
        (rows, rows, P("dp", None), stacked_rows, upright_rows, rows, upright_rows)
        + (stacked_rows, stacked_rows, upright_rows, upright_rows)
        + (rows, rows, upright_rows, upright_rows)
        + (narrow,) * 6
    )
    out_specs = (rows, rows) + (stacked_rows, upright_rows, rows, upright_rows) * 3 + (narrow,) * 6
    paths = Paths(mesh.shape["dp"])

    def body(*arrays):
        return shards(paths, *arrays)

    return jax.shard_map(
        body, mesh=mesh, in_specs=in_specs, out_specs=out_specs, check_vma=False
    )
```

```python
import functools

import jax
import jax.numpy as jnp
import numpy as np
from jax import lax
from jax.experimental import pallas as pl
from jax.experimental.pallas import tpu as pltpu
from jax.sharding import PartitionSpec as P

HD = 64
STEP = 10
EPS_NORM = 1e-05
BETA_ONE = 0.9
BETA_TWO = 0.999
EPS_ADAM = 1e-06
DECAY = 0.01
RATE = 0.25
MASKED = -1e30
ROOT_HALF = 0.7071067811865476
ROOT_TURN = 0.3989422804014327
LOW = jnp.bfloat16
F32 = jnp.float32
MIB = 2**20
RATE_FLOPS = 1_000_000
PACKED_ROWS = 16

NN = ((1,), (0,))
NT = ((1,), (1,))
TN = ((0,), (0,))


def dot(left, right, dims):
    return lax.dot_general(left, right, (dims, ((), ())), preferred_element_type=F32)


def tie(*values):
    return lax.optimization_barrier(values)


class Paths:
    def __init__(self, count):
        self.count = count
        if count == 16:
            self.shared, self.one, self.two = (8, 4), (1,), (2,)
        elif count == 128:
            self.shared, self.one, self.two = (64, 32), (4, 2, 1), (16, 8)
        else:
            raise ValueError("dp size")
        self.left = self.shared + self.one + self.two
        self.right = self.shared + self.two + self.one
        self.inner_left = self.one + self.shared + self.two
        self.inner_right = self.two + self.shared + self.one

    def send(self, source, mask):
        pairs = [(device, device ^ mask) for device in range(self.count)]
        return lax.ppermute(source, "dp", pairs)

    def owners(self, masks):
        found = [0]
        for mask in masks:
            found = found + [owner ^ mask for owner in found]
        return np.array(found, np.int32)

    def steps(self):
        return len(self.left)

    def sum_send(self, source, step):
        return source, self.send(source, self.left[-1 - step])

    def all_sum(self, source):
        for step in range(self.steps()):
            source = sum(self.sum_send(source, step))
        return source


class Gather:
    def __init__(self, paths, cut, mine):
        self.paths, self.cut, self.mine = paths, cut, mine

    def send_shared(self, source, step):
        return self.paths.send(source, self.paths.shared[step])

    def join_shared(self, source, arrived, step):
        low = (self.mine & self.paths.shared[step]) == 0
        pair = [jnp.where(low, source, arrived), jnp.where(low, arrived, source)]
        return jnp.stack(pair, axis=step)

    def grow(self, stack, masks):
        for mask in masks:
            stack = jnp.concatenate([stack, self.paths.send(stack, mask)])
        return stack

    def send_one(self, line):
        found = []
        for part, masks in (
            (line[..., : self.cut], self.paths.one),
            (line[..., self.cut :], self.paths.two),
        ):
            part = self.grow(part, masks[:-1])
            found.append((part, self.paths.send(part, masks[-1])))
        return found

    def join_one(self, pairs):
        return [jnp.concatenate(pair) for pair in pairs]

    def send_two(self, stacks):
        found = []
        for stack, masks in zip(stacks, (self.paths.two, self.paths.one)):
            stack = self.grow(stack, masks[:-1])
            found += [stack, self.paths.send(stack, masks[-1])]
        return found

    def even(self):
        return len(self.paths.one) == len(self.paths.two)


class Scatter:
    def __init__(self, paths):
        self.paths = paths

    def settle(self, pair):
        keep, arrived = pair
        size = keep.shape[0] // 2
        kept = keep[:size].astype(F32) + arrived[:size].astype(F32)
        sent = (keep[size:].astype(F32) + arrived[size:].astype(F32)).astype(LOW)
        return kept, sent

    def exchange(self, pair, masks):
        for mask in reversed(masks[1:]):
            pair = self.settle((pair[0], self.paths.send(pair[1], mask)))
        return pair[0], self.paths.send(pair[1], masks[0])

    def send_one(self, blocks):
        return self.exchange(blocks[:2], self.paths.two), self.exchange(blocks[2:], self.paths.one)

    def send_two(self, held):
        return self.send_settled([self.settle(pair) for pair in held])

    def send_settled(self, settled):
        left, right = settled
        return self.exchange(left, self.paths.one), self.exchange(right, self.paths.two)

    def join(self, held):
        left, right = [self.settle(pair) for pair in held]
        return [jnp.concatenate(pair, axis=2) for pair in zip(left, right)]

    def send_shared(self, pair):
        return self.exchange(pair, self.paths.shared[1:])

    def send_shared_at_once(self, held):
        top, low = self.paths.shared
        parts = [
            keep.astype(F32) + arrived.astype(F32) for keep, arrived in held
        ]
        total = jnp.concatenate(parts, axis=2)
        sends = total[1:].astype(LOW)
        return total[0], [
            self.paths.send(sends[number], mask) for number, mask in enumerate((top, low, top ^ low))
        ]

    def send_inner(self, held):
        return self.exchange(self.join(held), self.paths.shared[1:])

    def send_inner_last(self, held):
        return self.exchange(self.settle(held), self.paths.shared[:1])

    def send_ends(self, held, cut):
        keep, send = self.settle(held)
        left = self.exchange((keep[..., :cut], send[..., :cut]), self.paths.one)
        right = self.exchange((keep[..., cut:], send[..., cut:]), self.paths.two)
        return [part[0][0] for part in (left, right)], [part[1][0] for part in (left, right)]

    def send_last(self, held):
        keep, send = self.settle(held)
        return keep[0], self.paths.send(send, self.paths.shared[0])[0]


def swap(source):
    return lax.ppermute(source, "tensor", [(0, 1), (1, 0)])


def own_first(place_ref):
    return place_ref[2]


class Layout:
    def __init__(self, paths, rows):
        self.paths, self.rows = paths, rows
        self.direct = rows % PACKED_ROWS == 0
        self.outer = paths.owners(paths.left), paths.owners(paths.right)
        self.inner = paths.owners(paths.inner_left), paths.owners(paths.inner_right)
        self.wide = 2 ** len(paths.shared)
        self.left_lines = paths.owners(paths.one + paths.two)
        self.right_lines = paths.owners(paths.two + paths.one)

    def prepare(self, pieces, mine, there=False):
        if self.direct:
            return list(pieces)
        whole = []
        lines = self.paths.count // self.wide
        for part, owners in ((pieces[:2], self.left_lines), (pieces[2:], self.right_lines)):
            stack = jnp.concatenate(part)
            inverse = np.argsort(owners).astype(np.int32)
            order = jnp.take(jnp.asarray(inverse), jnp.arange(lines) ^ (mine % lines))
            stack = jnp.swapaxes(jnp.take(stack, order, axis=0), 0, 1)
            if there:
                stack = jnp.roll(stack, self.wide // 2, axis=0)
            whole.append(stack.reshape(-1, stack.shape[3]))
        return whole

    def count(self):
        return 4 if self.direct else 2

    def columns(self, refs):
        return refs[0].shape[-1], refs[-1].shape[-1]

    def scratch(self, columns):
        rows = self.rows * self.paths.count
        if not self.direct:
            return pltpu.VMEM((rows, columns), LOW)
        return pltpu.VMEM((self.wide, self.paths.count // self.wide, self.rows, columns), LOW)

    def read(self, ref, start=0, stop=None):
        value = ref[..., start : ref.shape[-1] if stop is None else stop]
        return value.reshape(-1, value.shape[-1])

    def copies(self, refs, place_ref, spans, there=False, shared_first=False):
        found = []
        cut = refs[0].shape[-1]
        lines = self.paths.count // self.wide
        groups = (
            (0, refs[: len(refs) // 2], self.left_lines),
            (cut, refs[len(refs) // 2 :], self.right_lines),
        )
        for base, part, owners in groups:
            width = part[0].shape[-1]
            for start, stop, target, column in spans:
                low, high = max(start, base), min(stop, base + width)
                if low >= high:
                    continue
                source = pl.ds(low - base, high - low)
                to = pl.ds(column + low - start, high - low)
                if not self.direct:
                    found.append((part[0].at[:, source], target.at[:, to]))
                    continue
                number = 0
                for ref in part:
                    for line in range(ref.shape[1 if shared_first else 0]):
                        owner = (own_first(place_ref) % lines) ^ int(owners[number])
                        size = self.wide // 2 if there else self.wide
                        for at in range(0, self.wide, size):
                            past = self.wide - size - at if there else at
                            block = (pl.ds(at, size), line) if shared_first else (line, pl.ds(at, size))
                            found.append(
                                (ref.at[(*block, slice(None), source)], target.at[pl.ds(past, size), owner, :, to])
                            )
                        number += 1
        return found

    def order_rows(self, source_ref, target_ref, place_ref, owners):
        if not self.direct:
            target_ref[...] = source_ref[...]
            return
        for number, owner in enumerate(owners):
            row = pl.multiple_of((own_first(place_ref) ^ int(owner)) * self.rows, PACKED_ROWS)
            target_ref[number * self.rows : (number + 1) * self.rows, :] = source_ref[
                pl.ds(row, self.rows), :
            ]

    def right_rows(self, order):
        if not self.direct:
            size = self.rows * self.paths.count // 2
            return [(0, 0, size), (size, size, size)]
        left, right = order
        place = {int(owner): number for number, owner in enumerate(right)}
        return [
            (number * self.rows, place[int(owner)] * self.rows, self.rows)
            for number, owner in enumerate(left)
        ]

    def finish(self, blocks, mine, order):
        if self.direct:
            return [block.reshape(-1, self.rows, block.shape[1]) for block in blocks]
        found = []
        for part, owners in zip((blocks[:2], blocks[2:]), order):
            whole = jnp.concatenate(part).reshape(-1, self.rows, part[0].shape[1])
            whole = jnp.take(whole, jnp.asarray(owners) ^ mine, axis=0)
            found += [whole[: self.paths.count // 2], whole[self.paths.count // 2 :]]
        return found


def start_all(copies, sems):
    started = [
        pltpu.make_async_copy(source, target, sems.at[number])
        for number, (source, target) in enumerate(copies)
    ]
    for copy in started:
        copy.start()
    return started


def wait_all(copies):
    for copy in copies:
        copy.wait()


def norm_of(source):
    width = source.shape[1]
    centred = source - jnp.sum(source, axis=1, keepdims=True) * (1.0 / width)
    variance = jnp.sum(centred * centred, axis=1, keepdims=True) * (1.0 / width)
    inv_std = lax.rsqrt(variance + EPS_NORM)
    return centred * inv_std, inv_std


def norm_back(grad_out, normed, inv_std, gain_row):
    width = normed.shape[1]
    scaled = grad_out * gain_row
    mean_plain = jnp.sum(scaled, axis=1, keepdims=True) * (1.0 / width)
    mean_cross = jnp.sum(scaled * normed, axis=1, keepdims=True) * (1.0 / width)
    return inv_std * (scaled - mean_plain - normed * mean_cross)


def add_rows(ref, row, first, at, value):
    columns = value.shape[1]
    held = jnp.where(first, 0.0, ref[row : row + 1, at : at + columns])
    ref[row : row + 1, at : at + columns] = held + jnp.sum(value, axis=0, keepdims=True)


def joined(mine_ref, other_ref):
    return jnp.concatenate([mine_ref[...], other_ref[...]], axis=1)


def whole_block(array):
    zeros = (0,) * array.ndim
    return pl.BlockSpec(array.shape, lambda *_: zeros, pipeline_mode=pl.Buffered(1))


ANYWHERE = pl.BlockSpec(memory_space=pl.ANY)


def like(*shape, dtype=F32):
    return jax.ShapeDtypeStruct(shape, dtype)


def rows_of(block, columns, shift=None):
    if shift is None:
        return pl.BlockSpec((block, columns), lambda i, place: (i, 0))
    return pl.BlockSpec((block, columns), lambda i, place: (i + place[0] * shift, 0))


def cost(micros):
    return pl.CostEstimate(flops=micros * RATE_FLOPS, bytes_accessed=0, transcendentals=0)


def params(mib):
    return pltpu.CompilerParams(vmem_limit_bytes=mib * MIB)


def qkv_body(layout, place, mine_ref, other_ref, norms_ref, *refs):
    weights, (mixed_ref, feat_ref, scratch, sems) = refs[:-4], refs[-4:]
    first = pl.program_id(0) == 0
    copies = layout.copies(weights, place, [(0, scratch.shape[-1], scratch, 0)])

    @pl.when(first)
    def _():
        start_all(copies, sems)

    normed, _ = norm_of(joined(mine_ref, other_ref).astype(F32))
    feat = (normed * norms_ref[0:1, :] + norms_ref[1:2, :]).astype(LOW)
    feat_ref[...] = feat

    @pl.when(first)
    def _():
        wait_all([pltpu.make_async_copy(*copy, sems.at[n]) for n, copy in enumerate(copies)])

    result = dot(feat, layout.read(scratch), NN).astype(LOW)
    width = mixed_ref.shape[2]
    for part in range(3):
        mixed_ref[part] = result[:, part * width : (part + 1) * width]


def qkv_forward(layout, place, mine, other, norms, weights):
    rows, width = mine.shape
    block = min(256, rows)
    return pl.pallas_call(
        functools.partial(qkv_body, layout),
        grid_spec=pltpu.PrefetchScalarGridSpec(
            num_scalar_prefetch=1,
            grid=(rows // block,),
            in_specs=[rows_of(block, width), rows_of(block, width), whole_block(norms)]
            + [ANYWHERE] * len(weights),
            out_specs=[
                pl.BlockSpec((3, block, width), lambda i, place: (0, i, 0)),
                rows_of(block, 2 * width),
            ],
            scratch_shapes=[
                layout.scratch(3 * width),
                pltpu.SemaphoreType.DMA((64,)),
            ],
        ),
        out_shape=[like(3, rows, width, dtype=LOW), like(rows, 2 * width, dtype=LOW)],
        compiler_params=params(24),
        cost_estimate=cost(5),
        name="qkv_forward",
    )(place, mine, other, norms, *weights)


def write_bias(ends_ref, bias_ref, block):
    for at in range(0, bias_ref.shape[1], block):
        keys = at + block
        place = at + lax.broadcasted_iota(jnp.int32, (1, block), 1)
        start = jnp.zeros_like(place)
        for slot in range(ends_ref.shape[0]):
            end = ends_ref[slot]
            start = jnp.maximum(start, jnp.where(end <= place, end, 0))
        key_place = lax.broadcasted_iota(jnp.int32, (keys, block), 0)
        visible = (key_place >= start) & (key_place <= place)
        bias_ref[0:keys, at : at + block] = jnp.where(visible, 0.0, MASKED)


def per_head(source):
    lane = lax.broadcasted_iota(jnp.int32, source.shape, 1)
    zero = jnp.zeros_like(source)
    return jnp.where(lane < HD, source, zero), jnp.where(lane < HD, zero, source)


def attn_forward_body(block, place, ends_ref, mixed_ref, own_ref, send_ref, log_ref, bias_ref):
    rows = mixed_ref.shape[1]

    @pl.when(pl.program_id(0) == 0)
    def _():
        write_bias(ends_ref, bias_ref, block)

    for at in range(0, rows, block):
        keys = at + block
        query = mixed_ref[0, at : at + block, :] * jnp.asarray(HD**-0.5, LOW)
        key = mixed_ref[1, 0:keys, :]
        value = mixed_ref[2, 0:keys, :]
        bias = bias_ref[0:keys, at : at + block]
        total, logs = None, []
        for query_head, value_head in zip(per_head(query), per_head(value)):
            scores = dot(key, query_head, NT) + bias
            top = jnp.max(scores, axis=0, keepdims=True)
            weight = jnp.exp(scores - top)
            norm = jnp.sum(weight, axis=0, keepdims=True)
            logs.append(top + jnp.log(norm))
            part = dot((weight * (1.0 / norm)).astype(LOW), value_head, TN)
            total = part if total is None else total + part
        log_ref[0, :, at : at + block] = jnp.concatenate(logs, axis=0)
        side = (2 * at) // rows
        inner = at - side * (rows // 2)

        @pl.when(place[0] == side)
        def _():
            own_ref[inner : inner + block, :] = total

        @pl.when(place[0] != side)
        def _():
            send_ref[inner : inner + block, :] = total


def attn_forward(place, ends, mixed):
    _, rows, width = mixed.shape
    block = 256
    pairs = width // 128
    return pl.pallas_call(
        functools.partial(attn_forward_body, block),
        grid_spec=pltpu.PrefetchScalarGridSpec(
            num_scalar_prefetch=2,
            grid=(pairs,),
            in_specs=[pl.BlockSpec((3, rows, 128), lambda i, *_: (0, 0, i))],
            out_specs=[
                pl.BlockSpec((rows // 2, 128), lambda i, *_: (0, i)),
                pl.BlockSpec((rows // 2, 128), lambda i, *_: (0, i)),
                pl.BlockSpec((1, 2, rows), lambda i, *_: (i, 0, 0)),
            ],
            scratch_shapes=[pltpu.VMEM((rows, rows), F32)],
        ),
        out_shape=[like(rows // 2, width), like(rows // 2, width), like(pairs, 2, rows)],
        compiler_params=params(40),
        cost_estimate=cost(12),
        name="attn_forward",
    )(place, ends, mixed)


def attn_backward_body(
    block, place, ends_ref, mixed_ref, own_ref, other_ref, log_ref, out_ref, bias_ref, key_sum, value_sum
):
    rows = mixed_ref.shape[1]

    @pl.when(pl.program_id(0) == 0)
    def _():
        write_bias(ends_ref, bias_ref, block)

    scale = jnp.asarray(HD**-0.5, LOW)
    for at in reversed(range(0, rows, block)):
        keys = at + block
        side = (2 * at) // rows
        inner = at - side * (rows // 2)
        query = mixed_ref[0, at : at + block, :] * scale
        grad = jnp.where(
            place[0] == side, own_ref[inner : inner + block, :], other_ref[inner : inner + block, :]
        )
        key = mixed_ref[1, 0:keys, :]
        value = mixed_ref[2, 0:keys, :]
        bias = bias_ref[0:keys, at : at + block]
        sums = None
        heads = zip(per_head(query), per_head(grad), per_head(key))
        for head, (query_head, grad_head, key_head) in enumerate(heads):
            log_total = log_ref[0, head : head + 1, at : at + block]
            probs = jnp.exp(dot(key, query_head, NT) + bias - log_total)
            grad_p = dot(value, grad_head, NT)
            row_sum = jnp.sum(probs * grad_p, axis=0, keepdims=True)
            grad_scores = (probs * (grad_p - row_sum)).astype(LOW)
            parts = (
                dot(grad_scores, key_head, TN),
                dot(grad_scores, query_head, NN),
                dot(probs.astype(LOW), grad_head, NN),
            )
            sums = parts if sums is None else [one + two for one, two in zip(sums, parts)]
        out_ref[0, at : at + block, :] = (sums[0] * HD**-0.5).astype(LOW)
        if keys == rows:
            key_sum[...] = sums[1]
            value_sum[...] = sums[2]
        else:
            key_sum[0:keys, :] += sums[1]
            value_sum[0:keys, :] += sums[2]
    out_ref[1] = key_sum[...].astype(LOW)
    out_ref[2] = value_sum[...].astype(LOW)


def attn_backward(place, ends, mixed, own, other, logs):
    _, rows, width = mixed.shape
    block = 256
    return pl.pallas_call(
        functools.partial(attn_backward_body, block),
        grid_spec=pltpu.PrefetchScalarGridSpec(
            num_scalar_prefetch=2,
            grid=(width // 128,),
            in_specs=[
                pl.BlockSpec((3, rows, 128), lambda i, *_: (0, 0, i)),
                pl.BlockSpec((rows // 2, 128), lambda i, *_: (0, i)),
                pl.BlockSpec((rows // 2, 128), lambda i, *_: (0, i)),
                pl.BlockSpec((1, 2, rows), lambda i, *_: (i, 0, 0)),
            ],
            out_specs=pl.BlockSpec((3, rows, 128), lambda i, *_: (0, 0, i)),
            scratch_shapes=[
                pltpu.VMEM((rows, rows), F32),
                pltpu.VMEM((rows, 128), F32),
                pltpu.VMEM((rows, 128), F32),
            ],
        ),
        out_shape=like(3, rows, width, dtype=LOW),
        compiler_params=params(40),
        cost_estimate=cost(16),
        name="attn_backward",
    )(place, ends, mixed, own, other, logs)


def turned(source):
    half = source.shape[1] // 2
    return jnp.concatenate([source[:, half:], source[:, :half]], axis=1)


def mid_spans(up_scratch, out_scratch, side):
    units, half = up_scratch.shape[-1] // 2, out_scratch.shape[-1] // 2
    return [
        (0, units, up_scratch, side * units),
        (units, units + half, out_scratch, side * half),
    ]


def part_copies(layout, place, groups, shared_first=False):
    found = []
    for side, (refs, spans) in enumerate(groups):
        found += layout.copies(refs, place, spans, side == 1, shared_first)
    return found


def up_body(layout, place, *refs):
    (
        att_own_ref,
        att_other_ref,
        tok_own_ref,
        tok_other_ref,
        norms_ref,
        gains_ref,
    ) = refs[:6]
    count = layout.count()
    own_weights, other_weights = refs[6 : 6 + count], refs[6 + count : 6 + 2 * count]
    (
        inner_own_ref,
        inner_send_ref,
        residual_ref,
        feat_ref,
        hidden_own_ref,
        hidden_send_ref,
        normed_ref,
        slope_ref,
        inv_ref,
        active_ref,
        up_ref,
        out_ref,
        sems,
    ) = refs[6 + 2 * count :]
    half = att_own_ref.shape[1]
    units = hidden_own_ref.shape[1]
    step = 512
    first = pl.program_id(0) == 0
    spans = [mid_spans(up_ref, out_ref, side) for side in range(2)]
    out_copies = part_copies(
        layout, place, [(own_weights, spans[0][1:]), (other_weights, spans[1][1:])]
    )
    up_copies = part_copies(
        layout, place, [(own_weights, spans[0][:1]), (other_weights, spans[1][:1])]
    )
    copies = [
        pltpu.make_async_copy(*copy, sems.at[n]) for n, copy in enumerate(out_copies + up_copies)
    ]

    @pl.when(first)
    def _():
        for copy in copies:
            copy.start()

    normed, _ = norm_of(joined(att_own_ref, att_other_ref))
    inner = (normed * norms_ref[2:3, :] + norms_ref[3:4, :]).astype(LOW)
    inner_own_ref[...] = inner[:, :half]
    inner_send_ref[...] = inner[:, half:]

    @pl.when(first)
    def _():
        wait_all(copies[: len(out_copies)])

    residual = joined(tok_own_ref, tok_other_ref).astype(F32) + dot(inner, layout.read(out_ref), NT)
    residual_ref[...] = residual
    normed, _ = norm_of(residual)
    feat = (normed * norms_ref[4:5, :] + norms_ref[5:6, :]).astype(LOW)
    feat_ref[...] = feat

    @pl.when(first)
    def _():
        wait_all(copies[len(out_copies) :])

    total = None
    for at in range(0, 2 * units, step):
        raised = dot(feat, layout.read(up_ref, at, at + step), NN)
        lower = 0.5 + 0.5 * lax.erf(raised * ROOT_HALF)
        active = raised * lower
        slope = lower + raised * (jnp.exp(raised * raised * -0.5) * ROOT_TURN)
        slope_ref[:, at : at + step] = slope.astype(LOW)
        active_ref[:, at : at + step] = active
        part = jnp.sum(active, axis=1, keepdims=True)
        total = part if total is None else total + part
    mean = total * (1.0 / (2 * units))
    total = None
    for at in range(0, 2 * units, step):
        centred = active_ref[:, at : at + step] - mean
        part = jnp.sum(centred * centred, axis=1, keepdims=True)
        total = part if total is None else total + part
    inv_std = lax.rsqrt(total * (1.0 / (2 * units)) + EPS_NORM)
    inv_ref[...] = jnp.broadcast_to(inv_std, inv_ref.shape)
    for at in range(0, 2 * units, step):
        normed = (active_ref[:, at : at + step] - mean) * inv_std
        normed_ref[:, at : at + step] = normed.astype(LOW)
        hidden = (normed * gains_ref[0:1, at : at + step] + gains_ref[1:2, at : at + step]).astype(LOW)
        if at < units:
            hidden_own_ref[:, at : at + step] = hidden
        else:
            hidden_send_ref[:, at - units : at - units + step] = hidden


def up_forward(layout, place, att_own, att_other, tok_mine, tok_other, norms, gains, weights):
    rows, half = att_own.shape
    units = gains.shape[1] // 2
    block = min(256, rows)
    shift = rows // block
    return pl.pallas_call(
        functools.partial(up_body, layout),
        grid_spec=pltpu.PrefetchScalarGridSpec(
            num_scalar_prefetch=1,
            grid=(rows // block,),
            in_specs=[
                rows_of(block, half),
                rows_of(block, half),
                rows_of(block, half, shift),
                rows_of(block, half, shift),
                whole_block(norms),
                whole_block(gains),
            ]
            + [ANYWHERE] * len(weights),
            out_specs=[
                rows_of(block, half),
                rows_of(block, half),
                rows_of(block, 2 * half),
                rows_of(block, 2 * half),
                rows_of(block, units),
                rows_of(block, units),
                rows_of(block, 2 * units),
                rows_of(block, 2 * units),
                rows_of(block, 128),
            ],
            scratch_shapes=[
                pltpu.VMEM((block, 2 * units), F32),
                layout.scratch(2 * units),
                layout.scratch(2 * half),
                pltpu.SemaphoreType.DMA((128,)),
            ],
        ),
        out_shape=[
            like(rows, half, dtype=LOW),
            like(rows, half, dtype=LOW),
            like(rows, 2 * half),
            like(rows, 2 * half, dtype=LOW),
            like(rows, units, dtype=LOW),
            like(rows, units, dtype=LOW),
            like(rows, 2 * units, dtype=LOW),
            like(rows, 2 * units, dtype=LOW),
            like(rows, 128),
        ],
        compiler_params=params(48),
        cost_estimate=cost(15),
        name="up_forward",
    )(place, att_own, att_other, tok_mine, tok_other, norms, gains, *weights)


def down_body(layout, place, *refs):
    (
        normed_ref,
        slope_ref,
        inv_ref,
        residual_ref,
        cot_mine_ref,
        cot_other_ref,
        att_own_ref,
        att_other_ref,
        norms_ref,
        gains_ref,
    ) = refs[:10]
    count = layout.count()
    weights = [refs[10 + number * count : 10 + (number + 1) * count] for number in range(4)]
    (
        raised_own_ref,
        raised_send_ref,
        residual_grad_ref,
        residual_low_ref,
        att_grad_own_ref,
        att_grad_send_ref,
        width_sum_ref,
        hidden_sum_ref,
        scaled_ref,
        up_ref,
        out_ref,
        down_ref,
        sems,
    ) = refs[10 + 4 * count :]
    first = pl.program_id(0) == 0
    half = att_own_ref.shape[1]
    units = normed_ref.shape[1] // 2
    spans = [mid_spans(up_ref, out_ref, side) for side in range(2)]
    down_copies = part_copies(
        layout,
        place,
        [(weights[2 + side], [(0, units, down_ref, side * units)]) for side in range(2)],
        shared_first=True,
    )
    up_copies = part_copies(layout, place, [(weights[side], spans[side][:1]) for side in range(2)])
    out_copies = part_copies(layout, place, [(weights[side], spans[side][1:]) for side in range(2)])
    copies = [
        pltpu.make_async_copy(*copy, sems.at[n])
        for n, copy in enumerate(down_copies + up_copies + out_copies)
    ]
    marks = (0, len(down_copies), len(down_copies) + len(up_copies), len(copies))

    @pl.when(first)
    def _():
        for copy in copies:
            copy.start()
        width_sum_ref[...] = jnp.zeros_like(width_sum_ref)
        hidden_sum_ref[...] = jnp.zeros_like(hidden_sum_ref)
        wait_all(copies[marks[0] : marks[1]])

    cot = joined(cot_mine_ref, cot_other_ref)
    residual = residual_ref[...]
    inv_std = inv_ref[:, 0:1]
    sum_plain, sum_cross = None, None
    step = 512
    for at in range(0, 2 * units, step):
        grad = dot(cot, layout.read(down_ref, at, at + step), NN)
        cross = grad * normed_ref[:, at : at + step].astype(F32)
        add_rows(hidden_sum_ref, 0, first, at, cross)
        add_rows(hidden_sum_ref, 1, first, at, grad)
        gain = gains_ref[0:1, at : at + step]
        scaled = grad * gain
        scaled_ref[:, at : at + step] = scaled
        plain = jnp.sum(scaled, axis=1, keepdims=True)
        crossed = jnp.sum(cross * gain, axis=1, keepdims=True)
        sum_plain = plain if sum_plain is None else sum_plain + plain
        sum_cross = crossed if sum_cross is None else sum_cross + crossed
    mean_plain = sum_plain * (1.0 / (2 * units))
    mean_cross = sum_cross * (1.0 / (2 * units))

    @pl.when(first)
    def _():
        wait_all(copies[marks[1] : marks[2]])

    middle = None
    for at in range(0, 2 * units, step):
        active = inv_std * (
            scaled_ref[:, at : at + step]
            - mean_plain
            - normed_ref[:, at : at + step].astype(F32) * mean_cross
        )
        raised = (active * slope_ref[:, at : at + step].astype(F32)).astype(LOW)
        if at < units:
            raised_own_ref[:, at : at + step] = raised
        else:
            raised_send_ref[:, at - units : at - units + step] = raised
        part = dot(raised, layout.read(up_ref, at, at + step), NT)
        middle = part if middle is None else middle + part
    normed, inv_std = norm_of(residual)
    add_rows(width_sum_ref, 4, first, 0, middle * normed)
    add_rows(width_sum_ref, 5, first, 0, middle)
    residual_grad = cot.astype(F32) + norm_back(middle, normed, inv_std, norms_ref[4:5, :])
    residual_grad_ref[...] = residual_grad
    low = residual_grad.astype(LOW)
    residual_low_ref[...] = low

    @pl.when(first)
    def _():
        wait_all(copies[marks[2] : marks[3]])

    inner = dot(low, layout.read(out_ref), NN)
    normed, inv_std = norm_of(joined(att_own_ref, att_other_ref))
    add_rows(width_sum_ref, 2, first, 0, inner * normed)
    add_rows(width_sum_ref, 3, first, 0, inner)
    att_grad = norm_back(inner, normed, inv_std, norms_ref[2:3, :]).astype(LOW)
    att_grad_own_ref[...] = att_grad[:, :half]
    att_grad_send_ref[...] = att_grad[:, half:]


def down_backward(layout, place, rowwise, norms, gains, weights):
    hidden_normed, att_own = rowwise[0], rowwise[6]
    rows, half = att_own.shape
    units = hidden_normed.shape[1] // 2
    block = min(256, rows)
    shift = rows // block
    return pl.pallas_call(
        functools.partial(down_body, layout),
        grid_spec=pltpu.PrefetchScalarGridSpec(
            num_scalar_prefetch=1,
            grid=(rows // block,),
            in_specs=[
                rows_of(block, 2 * units),
                rows_of(block, 2 * units),
                rows_of(block, 128),
                rows_of(block, 2 * half),
                rows_of(block, half, shift),
                rows_of(block, half, shift),
                rows_of(block, half),
                rows_of(block, half),
                whole_block(norms),
                whole_block(gains),
            ]
            + [ANYWHERE] * len(weights),
            out_specs=[
                rows_of(block, units),
                rows_of(block, units),
                rows_of(block, 2 * half),
                rows_of(block, 2 * half),
                rows_of(block, half),
                rows_of(block, half),
                pl.BlockSpec((8, 2 * half), lambda i, place: (0, 0)),
                pl.BlockSpec((8, 2 * units), lambda i, place: (0, 0)),
            ],
            scratch_shapes=[
                pltpu.VMEM((block, 2 * units), F32),
                layout.scratch(2 * units),
                layout.scratch(2 * half),
                layout.scratch(2 * units),
                pltpu.SemaphoreType.DMA((192,)),
            ],
        ),
        out_shape=[
            like(rows, units, dtype=LOW),
            like(rows, units, dtype=LOW),
            like(rows, 2 * half),
            like(rows, 2 * half, dtype=LOW),
            like(rows, half, dtype=LOW),
            like(rows, half, dtype=LOW),
            like(8, 2 * half),
            like(8, 2 * units),
        ],
        compiler_params=params(56),
        cost_estimate=cost(23),
        name="down_backward",
    )(place, *rowwise, norms, gains, *weights)


def emit(layout, order, ordered_ref, columns, cut, blocks):
    keep_left, send_left, keep_right, send_right = blocks
    middle = keep_left.shape[0]
    rows = ordered_ref[...]
    for value, start in columns:
        result = dot(rows, value, NN).astype(LOW)
        width = value.shape[1]
        if start < cut:
            to = slice(start, start + width)
            keep_left[:, to] = result[:middle]
            send_left[:, to] = result[middle:]
            continue
        to = slice(start - cut, start - cut + width)
        for at, where, size in layout.right_rows(order):
            target, where = (keep_right, where) if where < middle else (send_right, where - middle)
            target[where : where + size, to] = result[at : at + size]


def column_cuts(width, base, cut, step):
    found, at = [], 0
    while at < width:
        stop = min(at + step, width)
        if base + at < cut < base + stop:
            stop = cut - base
        found.append((at, stop))
        at = stop
    return found


def stacked(own_ref, there_ref, base, cut):
    return [
        (jnp.concatenate([own_ref[:, at:stop], there_ref[:, at:stop]], axis=0), base + at)
        for at, stop in column_cuts(own_ref.shape[1], base, cut, 512)
    ]


def down_grad_body(layout, order, cut, place, mine_ref, other_ref, own_ref, there_ref, *refs):
    blocks, (columns_ref, ordered_ref) = refs[:4], refs[4:]
    half, tokens = mine_ref.shape[1], own_ref.shape[0]
    for side in range(2):
        row = pl.multiple_of(jnp.bitwise_xor(place[0], side) * tokens, PACKED_ROWS)
        to = slice(side * tokens, (side + 1) * tokens)
        columns_ref[:half, to] = mine_ref[pl.ds(row, tokens), :].T
        columns_ref[half:, to] = other_ref[pl.ds(row, tokens), :].T
    layout.order_rows(columns_ref, ordered_ref, place, order[0])
    emit(layout, order, ordered_ref, stacked(own_ref, there_ref, 0, cut), cut, blocks)


def mid_grad_body(layout, order, cut, place, *refs):
    pairs, blocks, (columns_ref, ordered_ref) = refs[:8], refs[8:12], refs[12:]
    base = 0
    for number in range(2):
        feat_ref, feat_there_ref, own_ref, there_ref = pairs[4 * number : 4 * number + 4]
        tokens, half = feat_ref.shape[0], feat_ref.shape[1] // 2
        columns_ref[:, :tokens] = feat_ref[...].T
        columns_ref[:half, tokens:] = feat_there_ref[:, half:].T
        columns_ref[half:, tokens:] = feat_there_ref[:, :half].T
        layout.order_rows(columns_ref, ordered_ref, place, order[0])
        emit(layout, order, ordered_ref, stacked(own_ref, there_ref, base, cut), cut, blocks)
        base += own_ref.shape[1]


def in_grad_body(layout, order, cut, place, feat_ref, mixed_ref, *refs):
    blocks, (columns_ref, ordered_ref) = refs[:4], refs[4:]
    columns_ref[...] = feat_ref[...].T
    layout.order_rows(columns_ref, ordered_ref, place, order[0])
    width = mixed_ref.shape[2]
    columns = [
        (mixed_ref[part, :, at:stop], part * width + at)
        for part in range(3)
        for at, stop in column_cuts(width, part * width, cut, width)
    ]
    emit(layout, order, ordered_ref, columns, cut, blocks)


def weight_grad(layout, order, body, name, place, cut, width, tokens, arrays, micros):
    rows = layout.rows * layout.paths.count
    columns = (cut, cut, width - cut, width - cut)
    found = pl.pallas_call(
        functools.partial(body, layout, order, cut),
        grid_spec=pltpu.PrefetchScalarGridSpec(
            num_scalar_prefetch=1,
            grid=(1,),
            in_specs=[whole_block(array) for array in arrays],
            out_specs=[pl.BlockSpec((rows // 2, size), lambda i, place: (0, 0)) for size in columns],
            scratch_shapes=[pltpu.VMEM((rows, tokens), LOW), pltpu.VMEM((rows, tokens), LOW)],
        ),
        out_shape=[like(rows // 2, size, dtype=LOW) for size in columns],
        compiler_params=params(40),
        cost_estimate=cost(micros),
        name=name,
    )(place, *arrays)
    return layout.finish(found, place[2], order)


def first_body(layout, place, mixed_ref, mine_ref, other_ref, hidden_own_ref, hidden_send_ref, residual_ref, *refs):
    count = layout.count()
    in_refs, down_own_refs, down_other_refs = refs[:count], refs[count : 2 * count], refs[2 * count : 3 * count]
    own_ref, send_ref, sum_ref, output_own_ref, output_send_ref, in_ref, down_ref, sems = refs[3 * count :]
    first = pl.program_id(0) == 0
    own_blocks = pl.num_programs(0) // 2
    half, units = output_send_ref.shape[1], hidden_own_ref.shape[1]
    in_copies = layout.copies(in_refs, place, [(0, in_ref.shape[-1], in_ref, 0)])
    down_copies = part_copies(
        layout,
        place,
        [
            (down_own_refs, [(0, units, down_ref, 0)]),
            (down_other_refs, [(0, units, down_ref, units)]),
        ],
        shared_first=True,
    )
    copies = [
        pltpu.make_async_copy(*copy, sems.at[n]) for n, copy in enumerate(in_copies + down_copies)
    ]

    @pl.when(first)
    def _():
        for copy in copies:
            copy.start()
        sum_ref[...] = jnp.zeros_like(sum_ref)

    normed, _ = norm_of(joined(mine_ref, other_ref).astype(F32))
    grad_mixed = jnp.concatenate([mixed_ref[part] for part in range(3)], axis=1)

    @pl.when(first)
    def _():
        wait_all(copies[: len(in_copies)])

    grad = dot(grad_mixed, layout.read(in_ref), NT)
    add_rows(sum_ref, 0, first, 0, grad * normed)
    add_rows(sum_ref, 1, first, 0, grad)

    @pl.when(first)
    def _():
        wait_all(copies[len(in_copies) :])

    @pl.when(pl.program_id(0) < own_blocks)
    def _():
        own_ref[...] = grad
        output = (
            residual_ref[...]
            + dot(hidden_own_ref[...], layout.read(down_ref, 0, units), NT)
            + dot(hidden_send_ref[...], layout.read(down_ref, units), NT)
        )
        output_own_ref[...] = output[:, :half]
        output_send_ref[...] = output[:, half:]

    @pl.when(pl.program_id(0) >= own_blocks)
    def _():
        send_ref[...] = grad


def first_backward(layout, place, grad_mixed, mine, other, hidden_own, hidden_send, residual, weights):
    rows, half = mine.shape
    units = hidden_own.shape[1]
    block = min(256, rows // 2)
    count = rows // block
    owned = count // 2

    def own_rows_first(i, place):
        return (i + place[0] * owned) % count

    def own_rows(columns):
        return pl.BlockSpec((block, columns), lambda i, place: (jnp.minimum(i, owned - 1), 0))

    return pl.pallas_call(
        functools.partial(first_body, layout),
        grid_spec=pltpu.PrefetchScalarGridSpec(
            num_scalar_prefetch=1,
            grid=(count,),
            in_specs=[
                pl.BlockSpec((3, block, half), lambda i, place: (0, own_rows_first(i, place), 0)),
                pl.BlockSpec((block, half), lambda i, place: (own_rows_first(i, place), 0)),
                pl.BlockSpec((block, half), lambda i, place: (own_rows_first(i, place), 0)),
                own_rows(units),
                own_rows(units),
                own_rows(2 * half),
            ]
            + [ANYWHERE] * len(weights),
            out_specs=[
                own_rows(2 * half),
                pl.BlockSpec((block, 2 * half), lambda i, place: (jnp.maximum(i - owned, 0), 0)),
                pl.BlockSpec((8, 2 * half), lambda i, place: (0, 0)),
                pl.BlockSpec(
                    (block, half),
                    lambda i, place: (jnp.minimum(i, owned - 1) + place[0] * owned, 0),
                ),
                own_rows(half),
            ],
            scratch_shapes=[
                layout.scratch(3 * half),
                layout.scratch(2 * units),
                pltpu.SemaphoreType.DMA((96,)),
            ],
        ),
        out_shape=[
            like(rows // 2, 2 * half),
            like(rows // 2, 2 * half),
            like(8, 2 * half),
            like(rows, half),
            like(rows // 2, half),
        ],
        compiler_params=params(40),
        cost_estimate=cost(11),
        name="first_backward",
    )(place, grad_mixed, mine, other, hidden_own, hidden_send, residual, *weights)


def token_body(place, own_ref, there_ref, mine_ref, other_ref, norms_ref, residual_ref, keep_ref, send_ref):
    half = mine_ref.shape[1]
    normed, inv_std = norm_of(joined(mine_ref, other_ref).astype(F32))
    grad = own_ref[...] + turned(there_ref[...])
    result = residual_ref[...] + norm_back(grad, normed, inv_std, norms_ref[0:1, :])
    keep_ref[...] = result[:, :half]
    send_ref[...] = result[:, half:]


def token_backward(place, own, there, mine, other, norms, residual):
    rows, half = own.shape[0], mine.shape[1]
    block = min(256, rows)
    shift = rows // block
    return pl.pallas_call(
        token_body,
        grid_spec=pltpu.PrefetchScalarGridSpec(
            num_scalar_prefetch=1,
            grid=(rows // block,),
            in_specs=[
                rows_of(block, 2 * half),
                rows_of(block, 2 * half),
                rows_of(block, half, shift),
                rows_of(block, half, shift),
                whole_block(norms),
                rows_of(block, 2 * half),
            ],
            out_specs=[rows_of(block, half, shift), rows_of(block, half)],
        ),
        out_shape=[like(2 * rows, half), like(rows, half)],
        compiler_params=params(24),
        cost_estimate=cost(3),
        name="token_backward",
    )(place, own, there, mine, other, norms, residual)


def fill_body(place, there_ref, whole_ref, out_ref):
    out_ref[...] = there_ref[...]


def fill_there(place, whole, there):
    rows, columns = there.shape
    return pl.pallas_call(
        fill_body,
        grid_spec=pltpu.PrefetchScalarGridSpec(
            num_scalar_prefetch=1,
            grid=(1,),
            in_specs=[pl.BlockSpec((rows, columns), lambda i, place: (0, 0)), ANYWHERE],
            out_specs=pl.BlockSpec((rows, columns), lambda i, place: (1 - place[0], 0)),
        ),
        out_shape=like(2 * rows, columns),
        input_output_aliases={2: 0},
        cost_estimate=cost(2),
        name="fill_there",
    )(place, there, whole)


def adam_moments(grad, first, second):
    new_first = BETA_ONE * first + (1.0 - BETA_ONE) * grad
    new_second = BETA_TWO * second + (1.0 - BETA_TWO) * grad * grad
    step_dir = (
        new_first
        / (1.0 - BETA_ONE**STEP)
        / (jnp.sqrt(new_second / (1.0 - BETA_TWO**STEP)) + EPS_ADAM)
    )
    return (new_first, new_second, step_dir)


def at_lane(row, lane, value):
    rows = lax.broadcasted_iota(jnp.int32, (8, 128), 0)
    lanes = lax.broadcasted_iota(jnp.int32, (8, 128), 1)
    return jnp.where((rows == row) & (lanes == lane), value, 0.0)


def sum_of(source):
    return jnp.sum(jnp.sum(source * source, axis=1, keepdims=True), axis=0, keepdims=True)


def moments_body(numbers, cuts, counts, *refs):
    kept, arrived, refs = refs[: counts[0]], refs[counts[0] : sum(counts)], refs[sum(counts) :]
    count = len(numbers)
    states, outs, squares_ref = refs[: 3 * count], refs[3 * count : 6 * count], refs[6 * count]
    whole = []
    for at, keep_ref in enumerate(kept):
        total = keep_ref[...]
        for ref in arrived[at :: len(kept)]:
            total = total + ref[...].astype(F32)
        whole.append(total)
    whole = jnp.concatenate(whole, axis=1) if len(whole) > 1 else whole[0]
    squares = jnp.zeros((8, 128), F32)
    for number in range(count):
        master_ref, first_ref, second_ref = states[3 * number : 3 * number + 3]
        new_first_ref, new_second_ref, update_ref = outs[3 * number : 3 * number + 3]
        start, stop = cuts[number]
        parts = master_ref.shape[0] if master_ref.ndim == 3 else 1
        width = (stop - start) // parts
        for part in range(parts):
            pick = (lambda ref: ref.at[part]) if master_ref.ndim == 3 else (lambda ref: ref)
            master = pick(master_ref)[...]
            new_first, new_second, step_dir = adam_moments(
                whole[:, start + part * width : start + (part + 1) * width],
                pick(first_ref)[...],
                pick(second_ref)[...],
            )
            update = step_dir + DECAY * master
            pick(new_first_ref)[...] = new_first
            pick(new_second_ref)[...] = new_second
            pick(update_ref)[...] = update
            squares = squares + at_lane(0, numbers[number], sum_of(master))
            squares = squares + at_lane(1, numbers[number], sum_of(update))
    squares_ref[...] = squares


def moments(numbers, cuts, kept, arrived, states, name):
    in_vmem = pl.BlockSpec(memory_space=pltpu.VMEM)
    outs = [like(*state.shape) for state in states]
    counts = (len(kept), len(arrived))
    return pl.pallas_call(
        functools.partial(moments_body, numbers, cuts, counts),
        in_specs=[in_vmem] * (sum(counts) + len(states)),
        out_specs=[in_vmem] * (len(states) + 1),
        out_shape=outs + [like(8, 128)],
        compiler_params=params(40),
        cost_estimate=cost(3),
        name=name,
    )(*kept, *arrived, *states)


def norm_moments_body(packed_ref, *refs):
    states, outs, squares_ref = refs[:6], refs[6:12], refs[12]
    units = states[3].shape[1]
    squares = jnp.zeros((8, 128), F32)
    lane = 4
    for number, (rows, start) in enumerate(((6, units), (2, 0))):
        master_ref, first_ref, second_ref = states[3 * number : 3 * number + 3]
        grad = packed_ref[0:rows, start : start + master_ref.shape[1]]
        master = master_ref[...]
        results = adam_moments(grad, first_ref[...], second_ref[...])
        for ref, result in zip(outs[3 * number : 3 * number + 3], results):
            ref[...] = result
        for row in range(rows):
            squares = squares + at_lane(0, lane, sum_of(master[row : row + 1]))
            squares = squares + at_lane(1, lane, sum_of(results[2][row : row + 1]))
            lane += 1
    squares_ref[...] = squares


def norm_moments(packed, states):
    in_vmem = pl.BlockSpec(memory_space=pltpu.VMEM)
    return pl.pallas_call(
        norm_moments_body,
        in_specs=[in_vmem] * 7,
        out_specs=[in_vmem] * 7,
        out_shape=[like(*state.shape) for state in states] + [like(8, 128)],
        cost_estimate=cost(1),
        name="norm_moments",
    )(packed, *states)


def apply_body(squares_ref, squares_there_ref, *refs):
    masters, updates, outs = refs[:6], refs[6:12], refs[12:]
    squares = squares_ref[...] + squares_there_ref[...]
    ratio = jnp.sqrt(squares[0:1, :] / (squares[1:2, :] + 1e-06)) * RATE
    lanes = lax.broadcasted_iota(jnp.int32, ratio.shape, 1)

    def scale(lane):
        return jnp.sum(jnp.where(lanes == lane, ratio, 0.0), axis=1, keepdims=True)

    lane = 0
    for master_ref, update_ref, out_ref in zip(masters, updates, outs):
        if out_ref.ndim == 3:
            for part in range(out_ref.shape[0]):
                out_ref[part] = master_ref[part] - scale(lane) * update_ref[part]
            lane += 1
        elif lane < 4:
            out_ref[...] = master_ref[...] - scale(lane) * update_ref[...]
            lane += 1
        else:
            rows = out_ref.shape[0]
            factors = jnp.concatenate([scale(lane + row) for row in range(rows)], axis=0)
            out_ref[...] = master_ref[...] - factors * update_ref[...]
            lane += rows


def apply_updates(squares, squares_there, masters, updates):
    in_vmem = pl.BlockSpec(memory_space=pltpu.VMEM)
    return pl.pallas_call(
        apply_body,
        in_specs=[in_vmem] * 14,
        out_specs=[in_vmem] * 6,
        out_shape=[like(*master.shape) for master in masters],
        compiler_params=params(40),
        cost_estimate=cost(3),
        name="apply_updates",
    )(squares, squares_there, *masters, *updates)


def shards(
    paths,
    tokens,
    cotangent,
    seq_lengths,
    attn_in,
    attn_out,
    ffn_up,
    ffn_down,
    first_attn_in,
    second_attn_in,
    first_attn_out,
    second_attn_out,
    first_ffn_up,
    second_ffn_up,
    first_ffn_down,
    second_ffn_down,
    width_norm_params,
    first_width_norms,
    second_width_norms,
    hidden_norm_params,
    first_hidden_norms,
    second_hidden_norms,
):
    core = lax.axis_index("tensor")
    index = lax.axis_index("dp")
    mine = index ^ (core * (paths.count // 2))
    place = jnp.stack([core, index, mine]).astype(jnp.int32)
    tok_rows, half = tokens.shape
    units = ffn_up.shape[1]
    layout = Layout(paths, ffn_up.shape[0])

    shard_in = jnp.transpose(attn_in, (1, 0, 2)).reshape(attn_in.shape[1], -1).astype(LOW)
    shard_mid = jnp.concatenate([ffn_up, attn_out.T], axis=1).astype(LOW)
    shard_down = ffn_down.T.astype(LOW)
    cut_in, cut_mid, cut_down = 512, 1024, units // 2
    get_in, get_mid, get_down = [Gather(paths, cut, mine) for cut in (cut_in, cut_mid, cut_down)]
    scatter = Scatter(paths)

    arrived_in = get_in.send_shared(shard_in, 0)
    tok_other = swap(tokens)
    cot_other = swap(cotangent)
    norms = jnp.concatenate([width_norm_params, swap(width_norm_params)], axis=1)
    gains = jnp.concatenate([hidden_norm_params, swap(hidden_norm_params)], axis=1)
    ends = jnp.cumsum(seq_lengths[0])
    shard_in, arrived_in, shard_mid, shard_down = tie(shard_in, arrived_in, shard_mid, shard_down)
    pair_in = get_in.join_shared(shard_in, arrived_in, 0)
    arrived_in = get_in.send_shared(pair_in, 1)
    pair_in, arrived_in, shard_mid, shard_down, tok_other, cot_other, norms, gains, ends = tie(
        pair_in, arrived_in, shard_mid, shard_down, tok_other, cot_other, norms, gains, ends
    )
    line_in = get_in.join_shared(pair_in, arrived_in, 1).reshape(1, -1, *shard_in.shape)
    held_in = get_in.send_one(line_in)
    arrived_mid = get_mid.send_shared(shard_mid, 0)
    held_in, shard_down = tie(held_in, shard_down)
    pieces_in = get_in.send_two(get_in.join_one(held_in))
    pair_mid = get_mid.join_shared(shard_mid, arrived_mid, 0)
    arrived_mid = get_mid.send_shared(pair_mid, 1)
    if get_down.even():
        early_down = get_down.send_one(shard_down[None])
        stack_down = jnp.concatenate(get_down.join_one(early_down), axis=2)
    else:
        stack_down = shard_down
    pieces_in, stack_down = tie(pieces_in, stack_down)
    line_mid = get_mid.join_shared(pair_mid, arrived_mid, 1).reshape(1, -1, *shard_mid.shape)
    held_mid = get_mid.send_one(line_mid)
    arrived_down = get_down.send_shared(stack_down, 0)
    weights_in = layout.prepare(pieces_in, mine)
    mixed, feat_one = qkv_forward(layout, place, tokens, tok_other, norms, weights_in)
    mixed, feat_one, held_mid, stack_down, arrived_down = tie(
        mixed, feat_one, held_mid, stack_down, arrived_down
    )
    stack_down = get_down.join_shared(stack_down, arrived_down, 0)
    arrived_down = get_down.send_shared(stack_down, 1)
    stacks_mid = get_mid.join_one(held_mid)
    pieces_mid = get_mid.send_two(stacks_mid)
    early_mid = [swap(pieces_mid[0]), swap(pieces_mid[2])]
    att_own, att_send, logs = attn_forward(place, ends, mixed)
    att_own, att_send, pieces_mid, early_mid, stack_down, arrived_down = tie(
        att_own, att_send, pieces_mid, early_mid, stack_down, arrived_down
    )
    att_other = swap(att_send)
    late_mid = [swap(pieces_mid[1]), swap(pieces_mid[3])]
    line_down = get_down.join_shared(stack_down, arrived_down, 1)
    if get_down.even():
        line_down = line_down.reshape(-1, *line_down.shape[2:])
        stacks_down = [line_down[..., :cut_down], line_down[..., cut_down:]]
    else:
        line_down = line_down.reshape(1, -1, *shard_down.shape)
        stacks_down = get_down.join_one(get_down.send_one(line_down))
    pieces_down = get_down.send_two(stacks_down)
    att_other, late_mid = tie(att_other, late_mid)
    weights_mid = layout.prepare(pieces_mid, mine) + layout.prepare(
        [early_mid[0], late_mid[0], early_mid[1], late_mid[1]], mine, True
    )
    early_down = [swap(pieces_down[0]), swap(pieces_down[2])]
    (
        inner_own,
        inner_send,
        residual,
        feat_two,
        hidden_own,
        hidden_send,
        hidden_normed,
        slope,
        hidden_inv,
    ) = up_forward(
        layout, place, att_own, att_other, tokens, tok_other, norms, gains, weights_mid
    )
    pieces_down, early_down, hidden_send, feat_two, inner_send = tie(
        pieces_down, early_down, hidden_send, feat_two, inner_send
    )
    hidden_there = swap(hidden_send)
    late_down = [swap(pieces_down[1]), swap(pieces_down[3])]
    hidden_there, hidden_own = tie(hidden_there, hidden_own)
    grad_down = weight_grad(
        layout,
        layout.outer,
        down_grad_body,
        "down_grad",
        place,
        cut_down,
        units,
        tok_rows,
        (cotangent, cot_other, hidden_own, hidden_there),
        4,
    )
    grad_down, hidden_own, feat_two, inner_send, late_down = tie(
        grad_down, hidden_own, feat_two, inner_send, late_down
    )
    weights_down = layout.prepare(pieces_down, mine) + layout.prepare(
        [early_down[0], late_down[0], early_down[1], late_down[1]], mine, True
    )
    feat_two_there, inner_there = swap(feat_two), swap(inner_send)
    held_down = scatter.send_one(grad_down)
    (
        raised_own,
        raised_send,
        residual_grad,
        residual_low,
        att_grad_own,
        att_grad_send,
        width_sum,
        hidden_sum,
    ) = down_backward(
        layout,
        place,
        (
            hidden_normed,
            slope,
            hidden_inv,
            residual,
            cotangent,
            cot_other,
            att_own,
            att_other,
        ),
        norms,
        gains,
        weights_mid + weights_down,
    )
    held_down, raised_send, residual_low, att_grad_send, feat_two_there, inner_there = tie(
        held_down, raised_send, residual_low, att_grad_send, feat_two_there, inner_there
    )
    raised_there, residual_there = swap(raised_send), swap(residual_low)
    att_grad_other = swap(att_grad_send)
    held_down = scatter.send_two(held_down)
    raised_there, residual_there = tie(raised_there, residual_there)
    grad_mid = weight_grad(
        layout,
        layout.outer,
        mid_grad_body,
        "mid_grad",
        place,
        cut_mid,
        units + half,
        tok_rows,
        (
            feat_two,
            feat_two_there,
            raised_own,
            raised_there,
            residual_low,
            residual_there,
            inner_own,
            inner_there,
        ),
        6,
    )
    grad_mid, held_down, att_grad_other = tie(grad_mid, held_down, att_grad_other)
    held_mid = scatter.send_one(grad_mid)
    held_down = scatter.send_shared(scatter.join(held_down))
    grad_mixed = attn_backward(place, ends, mixed, att_grad_own, att_grad_other, logs)
    grad_mixed, held_mid, held_down = tie(grad_mixed, held_mid, held_down)
    keep_down, arrived_down = scatter.send_last(held_down)
    settled_mid = [scatter.settle(pair) for pair in held_mid]
    grad_mixed, settled_mid = tie(grad_mixed, settled_mid)
    held_mid = scatter.send_settled(settled_mid)
    grad_in = weight_grad(
        layout, layout.outer, in_grad_body, "in_grad", place, cut_in, 3 * half, tok_rows, (feat_one, grad_mixed), 5
    )
    grad_in, grad_mixed, held_mid = tie(grad_in, grad_mixed, held_mid)
    held_in = scatter.send_one(grad_in)
    held_mid = scatter.send_shared(scatter.join(held_mid))
    first_own, first_send, first_sum, output_own, output_send = first_backward(
        layout,
        place,
        grad_mixed,
        tokens,
        tok_other,
        hidden_own,
        hidden_send,
        residual,
        weights_in + weights_down,
    )
    held_in, first_own, first_send, first_sum, output_send, arrived_down, held_mid = tie(
        held_in, first_own, first_send, first_sum, output_send, arrived_down, held_mid
    )
    held_in = scatter.send_two(held_in)
    keep_mid, arrived_mid = scatter.send_last(held_mid)
    first_there = swap(first_send)
    down_state = moments(
        (3,),
        ((0, units),),
        [keep_down],
        [arrived_down],
        (ffn_down.T, first_ffn_down.T, second_ffn_down.T),
        "down_moments",
    )
    width_sum = width_sum + first_sum
    packed = jnp.concatenate([hidden_sum[:, :units], width_sum[:, :half]], axis=1) + swap(
        jnp.concatenate([hidden_sum[:, units:], width_sum[:, half:]], axis=1)
    )
    held_in, arrived_mid, first_there, output_send, down_state, packed = tie(
        held_in, arrived_mid, first_there, output_send, down_state, packed
    )
    held_in = scatter.send_shared(scatter.join(held_in))
    packed = paths.sum_send(packed, 0)
    output_there = swap(output_send)
    mid_state = moments(
        (2, 1),
        ((0, units), (units, units + half)),
        [keep_mid],
        [arrived_mid],
        (ffn_up, first_ffn_up, second_ffn_up, attn_out.T, first_attn_out.T, second_attn_out.T),
        "mid_moments",
    )
    held_in, packed, first_there, output_there, mid_state = tie(
        held_in, packed, first_there, output_there, mid_state
    )
    keep_in, arrived_in = scatter.send_last(held_in)
    token_own, token_send = token_backward(
        place, first_own, first_there, tokens, tok_other, norms, residual_grad
    )
    packed = paths.sum_send(sum(packed), 1)
    arrived_in, token_send, packed = tie(arrived_in, token_send, packed)
    packed = sum(packed)
    token_there = swap(token_send)
    in_state = moments(
        (0,),
        ((0, 3 * half),),
        [keep_in],
        [arrived_in],
        (attn_in, first_attn_in, second_attn_in),
        "in_moments",
    )
    squares = in_state[3] + (mid_state[6] + down_state[3])
    squares, packed = tie(squares, packed)
    squares = paths.sum_send(squares, 0)
    packed = paths.sum_send(packed, 2)
    block_output = fill_there(place, output_own, output_there)
    squares, packed, block_output, token_there = tie(squares, packed, block_output, token_there)
    squares = paths.sum_send(sum(squares), 1)
    for step in range(3, paths.steps()):
        packed = paths.sum_send(sum(packed), step)
    squares, packed = tie(squares, packed)
    squares = paths.sum_send(sum(squares), 2)
    norm_state = norm_moments(
        sum(packed),
        (
            width_norm_params,
            first_width_norms,
            second_width_norms,
            hidden_norm_params,
            first_hidden_norms,
            second_hidden_norms,
        ),
    )
    squares, norm_state = tie(squares, norm_state)
    squares = paths.sum_send(sum(squares), 3)
    grad_tokens = fill_there(place, token_own, token_there)
    squares, grad_tokens = tie(squares, grad_tokens)
    for step in range(4, paths.steps()):
        squares = paths.sum_send(sum(squares), step)
    squares = sum(squares) + norm_state[6]
    squares_there = swap(squares)
    new_in, new_out, new_up, new_down, new_width, new_hidden = apply_updates(
        squares,
        squares_there,
        (attn_in, attn_out.T, ffn_up, ffn_down.T, width_norm_params, hidden_norm_params),
        (in_state[2], mid_state[5], mid_state[2], down_state[2], norm_state[2], norm_state[5]),
    )
    return (
        block_output,
        grad_tokens,
        new_in,
        new_out.T,
        new_up,
        new_down.T,
        in_state[0],
        mid_state[3].T,
        mid_state[0],
        down_state[0].T,
        in_state[1],
        mid_state[4].T,
        mid_state[1],
        down_state[1].T,
        new_width,
        norm_state[0],
        norm_state[1],
        new_hidden,
        norm_state[3],
        norm_state[4],
    )


def solution(mesh):
    rows = P("dp", "tensor")
    stacked_rows = P(None, "dp", "tensor")
    upright_rows = P("tensor", "dp")
    narrow = P(None, "tensor")
    in_specs = (
        (rows, rows, P("dp", None), stacked_rows, upright_rows, rows, upright_rows)
        + (stacked_rows, stacked_rows, upright_rows, upright_rows)
        + (rows, rows, upright_rows, upright_rows)
        + (narrow,) * 6
    )
    out_specs = (rows, rows) + (stacked_rows, upright_rows, rows, upright_rows) * 3 + (narrow,) * 6
    paths = Paths(mesh.shape["dp"])

    def body(*arrays):
        return shards(paths, *arrays)

    return jax.shard_map(
        body, mesh=mesh, in_specs=in_specs, out_specs=out_specs, check_vma=False
    )
```

```python
import functools

import jax
import jax.numpy as jnp
import numpy as np
from jax import lax
from jax.experimental import pallas as pl
from jax.experimental.pallas import tpu as pltpu
from jax.sharding import PartitionSpec as P

HD = 64
STEP = 10
EPS_NORM = 1e-05
BETA_ONE = 0.9
BETA_TWO = 0.999
EPS_ADAM = 1e-06
DECAY = 0.01
RATE = 0.25
MASKED = -1e30
ROOT_HALF = 0.7071067811865476
ROOT_TURN = 0.3989422804014327
LOW = jnp.bfloat16
F32 = jnp.float32
MIB = 2**20
RATE_FLOPS = 1_000_000
PACKED_ROWS = 16

NN = ((1,), (0,))
NT = ((1,), (1,))
TN = ((0,), (0,))


def dot(left, right, dims):
    return lax.dot_general(left, right, (dims, ((), ())), preferred_element_type=F32)


def tie(*values):
    return lax.optimization_barrier(values)


class Paths:
    def __init__(self, count):
        self.count = count
        if count == 16:
            self.shared, self.one, self.two = (8, 4), (1,), (2,)
        elif count == 128:
            self.shared, self.one, self.two = (64, 32), (4, 2, 1), (16, 8)
        else:
            raise ValueError("dp size")
        self.left = self.shared + self.one + self.two
        self.right = self.shared + self.two + self.one
        self.inner_left = self.one + self.shared + self.two
        self.inner_right = self.two + self.shared + self.one

    def send(self, source, mask):
        pairs = [(device, device ^ mask) for device in range(self.count)]
        return lax.ppermute(source, "dp", pairs)

    def owners(self, masks):
        found = [0]
        for mask in masks:
            found = found + [owner ^ mask for owner in found]
        return np.array(found, np.int32)

    def steps(self):
        return len(self.left)

    def sum_send(self, source, step):
        return source, self.send(source, self.left[-1 - step])

    def all_sum(self, source):
        for step in range(self.steps()):
            source = sum(self.sum_send(source, step))
        return source


class Gather:
    def __init__(self, paths, cut, mine):
        self.paths, self.cut, self.mine = paths, cut, mine

    def send_shared(self, source, step):
        return self.paths.send(source, self.paths.shared[step])

    def join_shared(self, source, arrived, step):
        low = (self.mine & self.paths.shared[step]) == 0
        pair = [jnp.where(low, source, arrived), jnp.where(low, arrived, source)]
        return jnp.stack(pair, axis=step)

    def grow(self, stack, masks):
        for mask in masks:
            stack = jnp.concatenate([stack, self.paths.send(stack, mask)])
        return stack

    def send_one(self, line):
        found = []
        for part, masks in (
            (line[..., : self.cut], self.paths.one),
            (line[..., self.cut :], self.paths.two),
        ):
            part = self.grow(part, masks[:-1])
            found.append((part, self.paths.send(part, masks[-1])))
        return found

    def join_one(self, pairs):
        return [jnp.concatenate(pair) for pair in pairs]

    def send_two(self, stacks):
        found = []
        for stack, masks in zip(stacks, (self.paths.two, self.paths.one)):
            stack = self.grow(stack, masks[:-1])
            found += [stack, self.paths.send(stack, masks[-1])]
        return found

    def even(self):
        return len(self.paths.one) == len(self.paths.two)


class Scatter:
    def __init__(self, paths):
        self.paths = paths

    def settle(self, pair):
        keep, arrived = pair
        size = keep.shape[0] // 2
        kept = keep[:size].astype(F32) + arrived[:size].astype(F32)
        sent = (keep[size:].astype(F32) + arrived[size:].astype(F32)).astype(LOW)
        return kept, sent

    def exchange(self, pair, masks):
        for mask in reversed(masks[1:]):
            pair = self.settle((pair[0], self.paths.send(pair[1], mask)))
        return pair[0], self.paths.send(pair[1], masks[0])

    def send_one(self, blocks):
        return self.exchange(blocks[:2], self.paths.two), self.exchange(blocks[2:], self.paths.one)

    def send_two(self, held):
        return self.send_settled([self.settle(pair) for pair in held])

    def send_settled(self, settled):
        left, right = settled
        return self.exchange(left, self.paths.one), self.exchange(right, self.paths.two)

    def join(self, held):
        left, right = [self.settle(pair) for pair in held]
        return [jnp.concatenate(pair, axis=2) for pair in zip(left, right)]

    def send_shared(self, pair):
        return self.exchange(pair, self.paths.shared[1:])

    def send_shared_at_once(self, held):
        top, low = self.paths.shared
        parts = [
            keep.astype(F32) + arrived.astype(F32) for keep, arrived in held
        ]
        total = jnp.concatenate(parts, axis=2)
        sends = total[1:].astype(LOW)
        return total[0], [
            self.paths.send(sends[number], mask) for number, mask in enumerate((top, low, top ^ low))
        ]

    def send_inner(self, held):
        return self.exchange(self.join(held), self.paths.shared[1:])

    def send_inner_last(self, held):
        return self.exchange(self.settle(held), self.paths.shared[:1])

    def send_ends(self, held, cut):
        keep, send = self.settle(held)
        left = self.exchange((keep[..., :cut], send[..., :cut]), self.paths.one)
        right = self.exchange((keep[..., cut:], send[..., cut:]), self.paths.two)
        return [part[0][0] for part in (left, right)], [part[1][0] for part in (left, right)]

    def send_last(self, held):
        keep, send = self.settle(held)
        return keep[0], self.paths.send(send, self.paths.shared[0])[0]


def swap(source):
    return lax.ppermute(source, "tensor", [(0, 1), (1, 0)])


def own_first(place_ref):
    return place_ref[2]


class Layout:
    def __init__(self, paths, rows):
        self.paths, self.rows = paths, rows
        self.direct = rows % PACKED_ROWS == 0
        self.outer = paths.owners(paths.left), paths.owners(paths.right)
        self.inner = paths.owners(paths.inner_left), paths.owners(paths.inner_right)
        self.wide = 2 ** len(paths.shared)
        self.left_lines = paths.owners(paths.one + paths.two)
        self.right_lines = paths.owners(paths.two + paths.one)

    def prepare(self, pieces, mine, there=False):
        if self.direct:
            return list(pieces)
        whole = []
        lines = self.paths.count // self.wide
        for part, owners in ((pieces[:2], self.left_lines), (pieces[2:], self.right_lines)):
            stack = jnp.concatenate(part)
            inverse = np.argsort(owners).astype(np.int32)
            order = jnp.take(jnp.asarray(inverse), jnp.arange(lines) ^ (mine % lines))
            stack = jnp.swapaxes(jnp.take(stack, order, axis=0), 0, 1)
            if there:
                stack = jnp.roll(stack, self.wide // 2, axis=0)
            whole.append(stack.reshape(-1, stack.shape[3]))
        return whole

    def count(self):
        return 4 if self.direct else 2

    def columns(self, refs):
        return refs[0].shape[-1], refs[-1].shape[-1]

    def scratch(self, columns):
        rows = self.rows * self.paths.count
        if not self.direct:
            return pltpu.VMEM((rows, columns), LOW)
        return pltpu.VMEM((self.wide, self.paths.count // self.wide, self.rows, columns), LOW)

    def read(self, ref, start=0, stop=None):
        value = ref[..., start : ref.shape[-1] if stop is None else stop]
        return value.reshape(-1, value.shape[-1])

    def copies(self, refs, place_ref, spans, there=False, shared_first=False):
        found = []
        cut = refs[0].shape[-1]
        lines = self.paths.count // self.wide
        groups = (
            (0, refs[: len(refs) // 2], self.left_lines),
            (cut, refs[len(refs) // 2 :], self.right_lines),
        )
        for base, part, owners in groups:
            width = part[0].shape[-1]
            for start, stop, target, column in spans:
                low, high = max(start, base), min(stop, base + width)
                if low >= high:
                    continue
                source = pl.ds(low - base, high - low)
                to = pl.ds(column + low - start, high - low)
                if not self.direct:
                    found.append((part[0].at[:, source], target.at[:, to]))
                    continue
                number = 0
                for ref in part:
                    for line in range(ref.shape[1 if shared_first else 0]):
                        owner = (own_first(place_ref) % lines) ^ int(owners[number])
                        size = self.wide // 2 if there else self.wide
                        for at in range(0, self.wide, size):
                            past = self.wide - size - at if there else at
                            block = (pl.ds(at, size), line) if shared_first else (line, pl.ds(at, size))
                            found.append(
                                (ref.at[(*block, slice(None), source)], target.at[pl.ds(past, size), owner, :, to])
                            )
                        number += 1
        return found

    def order_rows(self, source_ref, target_ref, place_ref, owners):
        if not self.direct:
            target_ref[...] = source_ref[...]
            return
        for number, owner in enumerate(owners):
            row = pl.multiple_of((own_first(place_ref) ^ int(owner)) * self.rows, PACKED_ROWS)
            target_ref[number * self.rows : (number + 1) * self.rows, :] = source_ref[
                pl.ds(row, self.rows), :
            ]

    def right_rows(self, order):
        if not self.direct:
            size = self.rows * self.paths.count // 2
            return [(0, 0, size), (size, size, size)]
        left, right = order
        place = {int(owner): number for number, owner in enumerate(right)}
        return [
            (number * self.rows, place[int(owner)] * self.rows, self.rows)
            for number, owner in enumerate(left)
        ]

    def finish(self, blocks, mine, order):
        if self.direct:
            return [block.reshape(-1, self.rows, block.shape[1]) for block in blocks]
        found = []
        for part, owners in zip((blocks[:2], blocks[2:]), order):
            whole = jnp.concatenate(part).reshape(-1, self.rows, part[0].shape[1])
            whole = jnp.take(whole, jnp.asarray(owners) ^ mine, axis=0)
            found += [whole[: self.paths.count // 2], whole[self.paths.count // 2 :]]
        return found


def start_all(copies, sems):
    started = [
        pltpu.make_async_copy(source, target, sems.at[number])
        for number, (source, target) in enumerate(copies)
    ]
    for copy in started:
        copy.start()
    return started


def wait_all(copies):
    for copy in copies:
        copy.wait()


def norm_of(source):
    width = source.shape[1]
    centred = source - jnp.sum(source, axis=1, keepdims=True) * (1.0 / width)
    variance = jnp.sum(centred * centred, axis=1, keepdims=True) * (1.0 / width)
    inv_std = lax.rsqrt(variance + EPS_NORM)
    return centred * inv_std, inv_std


def norm_back(grad_out, normed, inv_std, gain_row):
    width = normed.shape[1]
    scaled = grad_out * gain_row
    mean_plain = jnp.sum(scaled, axis=1, keepdims=True) * (1.0 / width)
    mean_cross = jnp.sum(scaled * normed, axis=1, keepdims=True) * (1.0 / width)
    return inv_std * (scaled - mean_plain - normed * mean_cross)


def add_rows(ref, row, first, at, value):
    columns = value.shape[1]
    held = jnp.where(first, 0.0, ref[row : row + 1, at : at + columns])
    ref[row : row + 1, at : at + columns] = held + jnp.sum(value, axis=0, keepdims=True)


def joined(mine_ref, other_ref):
    return jnp.concatenate([mine_ref[...], other_ref[...]], axis=1)


def whole_block(array):
    zeros = (0,) * array.ndim
    return pl.BlockSpec(array.shape, lambda *_: zeros, pipeline_mode=pl.Buffered(1))


ANYWHERE = pl.BlockSpec(memory_space=pl.ANY)


def like(*shape, dtype=F32):
    return jax.ShapeDtypeStruct(shape, dtype)


def rows_of(block, columns, shift=None):
    if shift is None:
        return pl.BlockSpec((block, columns), lambda i, place: (i, 0))
    return pl.BlockSpec((block, columns), lambda i, place: (i + place[0] * shift, 0))


def cost(micros):
    return pl.CostEstimate(flops=micros * RATE_FLOPS, bytes_accessed=0, transcendentals=0)


def params(mib):
    return pltpu.CompilerParams(vmem_limit_bytes=mib * MIB)


def qkv_body(layout, place, mine_ref, other_ref, norms_ref, *refs):
    weights, (mixed_ref, feat_ref, scratch, sems) = refs[:-4], refs[-4:]
    first = pl.program_id(0) == 0
    copies = layout.copies(weights, place, [(0, scratch.shape[-1], scratch, 0)])

    @pl.when(first)
    def _():
        start_all(copies, sems)

    normed, _ = norm_of(joined(mine_ref, other_ref).astype(F32))
    feat = (normed * norms_ref[0:1, :] + norms_ref[1:2, :]).astype(LOW)
    feat_ref[...] = feat

    @pl.when(first)
    def _():
        wait_all([pltpu.make_async_copy(*copy, sems.at[n]) for n, copy in enumerate(copies)])

    result = dot(feat, layout.read(scratch), NN).astype(LOW)
    width = mixed_ref.shape[2]
    for part in range(3):
        mixed_ref[part] = result[:, part * width : (part + 1) * width]


def qkv_forward(layout, place, mine, other, norms, weights):
    rows, width = mine.shape
    block = min(256, rows)
    return pl.pallas_call(
        functools.partial(qkv_body, layout),
        grid_spec=pltpu.PrefetchScalarGridSpec(
            num_scalar_prefetch=1,
            grid=(rows // block,),
            in_specs=[rows_of(block, width), rows_of(block, width), whole_block(norms)]
            + [ANYWHERE] * len(weights),
            out_specs=[
                pl.BlockSpec((3, block, width), lambda i, place: (0, i, 0)),
                rows_of(block, 2 * width),
            ],
            scratch_shapes=[
                layout.scratch(3 * width),
                pltpu.SemaphoreType.DMA((64,)),
            ],
        ),
        out_shape=[like(3, rows, width, dtype=LOW), like(rows, 2 * width, dtype=LOW)],
        compiler_params=params(24),
        cost_estimate=cost(5),
        name="qkv_forward",
    )(place, mine, other, norms, *weights)


def write_bias(ends_ref, bias_ref, block):
    for at in range(0, bias_ref.shape[1], block):
        keys = at + block
        place = at + lax.broadcasted_iota(jnp.int32, (1, block), 1)
        start = jnp.zeros_like(place)
        for slot in range(ends_ref.shape[0]):
            end = ends_ref[slot]
            start = jnp.maximum(start, jnp.where(end <= place, end, 0))
        key_place = lax.broadcasted_iota(jnp.int32, (keys, block), 0)
        visible = (key_place >= start) & (key_place <= place)
        bias_ref[0:keys, at : at + block] = jnp.where(visible, 0.0, MASKED)


def per_head(source):
    lane = lax.broadcasted_iota(jnp.int32, source.shape, 1)
    zero = jnp.zeros_like(source)
    return jnp.where(lane < HD, source, zero), jnp.where(lane < HD, zero, source)


def attn_forward_body(block, place, ends_ref, mixed_ref, own_ref, send_ref, log_ref, bias_ref):
    rows = mixed_ref.shape[1]

    @pl.when(pl.program_id(0) == 0)
    def _():
        write_bias(ends_ref, bias_ref, block)

    for at in range(0, rows, block):
        keys = at + block
        query = mixed_ref[0, at : at + block, :] * jnp.asarray(HD**-0.5, LOW)
        key = mixed_ref[1, 0:keys, :]
        value = mixed_ref[2, 0:keys, :]
        bias = bias_ref[0:keys, at : at + block]
        total, logs = None, []
        for query_head, value_head in zip(per_head(query), per_head(value)):
            scores = dot(key, query_head, NT) + bias
            top = jnp.max(scores, axis=0, keepdims=True)
            weight = jnp.exp(scores - top)
            norm = jnp.sum(weight, axis=0, keepdims=True)
            logs.append(top + jnp.log(norm))
            part = dot((weight * (1.0 / norm)).astype(LOW), value_head, TN)
            total = part if total is None else total + part
        log_ref[0, :, at : at + block] = jnp.concatenate(logs, axis=0)
        side = (2 * at) // rows
        inner = at - side * (rows // 2)

        @pl.when(place[0] == side)
        def _():
            own_ref[inner : inner + block, :] = total

        @pl.when(place[0] != side)
        def _():
            send_ref[inner : inner + block, :] = total


def attn_forward(place, ends, mixed):
    _, rows, width = mixed.shape
    block = 256
    pairs = width // 128
    return pl.pallas_call(
        functools.partial(attn_forward_body, block),
        grid_spec=pltpu.PrefetchScalarGridSpec(
            num_scalar_prefetch=2,
            grid=(pairs,),
            in_specs=[pl.BlockSpec((3, rows, 128), lambda i, *_: (0, 0, i))],
            out_specs=[
                pl.BlockSpec((rows // 2, 128), lambda i, *_: (0, i)),
                pl.BlockSpec((rows // 2, 128), lambda i, *_: (0, i)),
                pl.BlockSpec((1, 2, rows), lambda i, *_: (i, 0, 0)),
            ],
            scratch_shapes=[pltpu.VMEM((rows, rows), F32)],
        ),
        out_shape=[like(rows // 2, width), like(rows // 2, width), like(pairs, 2, rows)],
        compiler_params=params(40),
        cost_estimate=cost(12),
        name="attn_forward",
    )(place, ends, mixed)


def attn_backward_body(
    block, place, ends_ref, mixed_ref, own_ref, other_ref, log_ref, out_ref, bias_ref, key_sum, value_sum
):
    rows = mixed_ref.shape[1]

    @pl.when(pl.program_id(0) == 0)
    def _():
        write_bias(ends_ref, bias_ref, block)

    scale = jnp.asarray(HD**-0.5, LOW)
    for at in reversed(range(0, rows, block)):
        keys = at + block
        side = (2 * at) // rows
        inner = at - side * (rows // 2)
        query = mixed_ref[0, at : at + block, :] * scale
        grad = jnp.where(
            place[0] == side, own_ref[inner : inner + block, :], other_ref[inner : inner + block, :]
        )
        key = mixed_ref[1, 0:keys, :]
        value = mixed_ref[2, 0:keys, :]
        bias = bias_ref[0:keys, at : at + block]
        sums = None
        heads = zip(per_head(query), per_head(grad), per_head(key))
        for head, (query_head, grad_head, key_head) in enumerate(heads):
            log_total = log_ref[0, head : head + 1, at : at + block]
            probs = jnp.exp(dot(key, query_head, NT) + bias - log_total)
            grad_p = dot(value, grad_head, NT)
            row_sum = jnp.sum(probs * grad_p, axis=0, keepdims=True)
            grad_scores = (probs * (grad_p - row_sum)).astype(LOW)
            parts = (
                dot(grad_scores, key_head, TN),
                dot(grad_scores, query_head, NN),
                dot(probs.astype(LOW), grad_head, NN),
            )
            sums = parts if sums is None else [one + two for one, two in zip(sums, parts)]
        out_ref[0, at : at + block, :] = (sums[0] * HD**-0.5).astype(LOW)
        if keys == rows:
            key_sum[...] = sums[1]
            value_sum[...] = sums[2]
        else:
            key_sum[0:keys, :] += sums[1]
            value_sum[0:keys, :] += sums[2]
    out_ref[1] = key_sum[...].astype(LOW)
    out_ref[2] = value_sum[...].astype(LOW)


def attn_backward(place, ends, mixed, own, other, logs):
    _, rows, width = mixed.shape
    block = 256
    return pl.pallas_call(
        functools.partial(attn_backward_body, block),
        grid_spec=pltpu.PrefetchScalarGridSpec(
            num_scalar_prefetch=2,
            grid=(width // 128,),
            in_specs=[
                pl.BlockSpec((3, rows, 128), lambda i, *_: (0, 0, i)),
                pl.BlockSpec((rows // 2, 128), lambda i, *_: (0, i)),
                pl.BlockSpec((rows // 2, 128), lambda i, *_: (0, i)),
                pl.BlockSpec((1, 2, rows), lambda i, *_: (i, 0, 0)),
            ],
            out_specs=pl.BlockSpec((3, rows, 128), lambda i, *_: (0, 0, i)),
            scratch_shapes=[
                pltpu.VMEM((rows, rows), F32),
                pltpu.VMEM((rows, 128), F32),
                pltpu.VMEM((rows, 128), F32),
            ],
        ),
        out_shape=like(3, rows, width, dtype=LOW),
        compiler_params=params(40),
        cost_estimate=cost(16),
        name="attn_backward",
    )(place, ends, mixed, own, other, logs)


def turned(source):
    half = source.shape[1] // 2
    return jnp.concatenate([source[:, half:], source[:, :half]], axis=1)


def mid_spans(up_scratch, out_scratch, side):
    units, half = up_scratch.shape[-1] // 2, out_scratch.shape[-1] // 2
    return [
        (0, units, up_scratch, side * units),
        (units, units + half, out_scratch, side * half),
    ]


def part_copies(layout, place, groups, shared_first=False):
    found = []
    for side, (refs, spans) in enumerate(groups):
        found += layout.copies(refs, place, spans, side == 1, shared_first)
    return found


def up_body(layout, place, *refs):
    (
        att_own_ref,
        att_other_ref,
        tok_own_ref,
        tok_other_ref,
        norms_ref,
        gains_ref,
    ) = refs[:6]
    count = layout.count()
    own_weights, other_weights = refs[6 : 6 + count], refs[6 + count : 6 + 2 * count]
    (
        inner_own_ref,
        inner_send_ref,
        residual_ref,
        feat_ref,
        hidden_own_ref,
        hidden_send_ref,
        normed_ref,
        slope_ref,
        inv_ref,
        active_ref,
        up_ref,
        out_ref,
        sems,
    ) = refs[6 + 2 * count :]
    half = att_own_ref.shape[1]
    units = hidden_own_ref.shape[1]
    step = 512
    first = pl.program_id(0) == 0
    spans = [mid_spans(up_ref, out_ref, side) for side in range(2)]
    out_copies = part_copies(
        layout, place, [(own_weights, spans[0][1:]), (other_weights, spans[1][1:])]
    )
    up_copies = part_copies(
        layout, place, [(own_weights, spans[0][:1]), (other_weights, spans[1][:1])]
    )
    copies = [
        pltpu.make_async_copy(*copy, sems.at[n]) for n, copy in enumerate(out_copies + up_copies)
    ]

    @pl.when(first)
    def _():
        for copy in copies:
            copy.start()

    normed, _ = norm_of(joined(att_own_ref, att_other_ref))
    inner = (normed * norms_ref[2:3, :] + norms_ref[3:4, :]).astype(LOW)
    inner_own_ref[...] = inner[:, :half]
    inner_send_ref[...] = inner[:, half:]

    @pl.when(first)
    def _():
        wait_all(copies[: len(out_copies)])

    residual = joined(tok_own_ref, tok_other_ref).astype(F32) + dot(inner, layout.read(out_ref), NT)
    residual_ref[...] = residual
    normed, _ = norm_of(residual)
    feat = (normed * norms_ref[4:5, :] + norms_ref[5:6, :]).astype(LOW)
    feat_ref[...] = feat

    own_copies = len(up_copies) // 3 if layout.direct else len(up_copies) // 2
    own_stop = len(out_copies) + own_copies

    @pl.when(first)
    def _():
        wait_all(copies[len(out_copies) : own_stop])

    total = None
    for at in range(0, 2 * units, step):
        if at == units:

            @pl.when(first)
            def _():
                wait_all(copies[own_stop:])

        raised = dot(feat, layout.read(up_ref, at, at + step), NN)
        lower = 0.5 + 0.5 * lax.erf(raised * ROOT_HALF)
        active = raised * lower
        slope = lower + raised * (jnp.exp(raised * raised * -0.5) * ROOT_TURN)
        slope_ref[:, at : at + step] = slope.astype(LOW)
        active_ref[:, at : at + step] = active
        part = jnp.sum(active, axis=1, keepdims=True)
        total = part if total is None else total + part
    mean = total * (1.0 / (2 * units))
    total = None
    for at in range(0, 2 * units, step):
        centred = active_ref[:, at : at + step] - mean
        part = jnp.sum(centred * centred, axis=1, keepdims=True)
        total = part if total is None else total + part
    inv_std = lax.rsqrt(total * (1.0 / (2 * units)) + EPS_NORM)
    inv_ref[...] = jnp.broadcast_to(inv_std, inv_ref.shape)
    for at in range(0, 2 * units, step):
        normed = (active_ref[:, at : at + step] - mean) * inv_std
        normed_ref[:, at : at + step] = normed.astype(LOW)
        hidden = (normed * gains_ref[0:1, at : at + step] + gains_ref[1:2, at : at + step]).astype(LOW)
        if at < units:
            hidden_own_ref[:, at : at + step] = hidden
        else:
            hidden_send_ref[:, at - units : at - units + step] = hidden


def up_forward(layout, place, att_own, att_other, tok_mine, tok_other, norms, gains, weights):
    rows, half = att_own.shape
    units = gains.shape[1] // 2
    block = min(256, rows)
    shift = rows // block
    return pl.pallas_call(
        functools.partial(up_body, layout),
        grid_spec=pltpu.PrefetchScalarGridSpec(
            num_scalar_prefetch=1,
            grid=(rows // block,),
            in_specs=[
                rows_of(block, half),
                rows_of(block, half),
                rows_of(block, half, shift),
                rows_of(block, half, shift),
                whole_block(norms),
                whole_block(gains),
            ]
            + [ANYWHERE] * len(weights),
            out_specs=[
                rows_of(block, half),
                rows_of(block, half),
                rows_of(block, 2 * half),
                rows_of(block, 2 * half),
                rows_of(block, units),
                rows_of(block, units),
                rows_of(block, 2 * units),
                rows_of(block, 2 * units),
                rows_of(block, 128),
            ],
            scratch_shapes=[
                pltpu.VMEM((block, 2 * units), F32),
                layout.scratch(2 * units),
                layout.scratch(2 * half),
                pltpu.SemaphoreType.DMA((128,)),
            ],
        ),
        out_shape=[
            like(rows, half, dtype=LOW),
            like(rows, half, dtype=LOW),
            like(rows, 2 * half),
            like(rows, 2 * half, dtype=LOW),
            like(rows, units, dtype=LOW),
            like(rows, units, dtype=LOW),
            like(rows, 2 * units, dtype=LOW),
            like(rows, 2 * units, dtype=LOW),
            like(rows, 128),
        ],
        compiler_params=params(48),
        cost_estimate=cost(15),
        name="up_forward",
    )(place, att_own, att_other, tok_mine, tok_other, norms, gains, *weights)


def down_body(layout, place, *refs):
    (
        normed_ref,
        slope_ref,
        inv_ref,
        residual_ref,
        cot_mine_ref,
        cot_other_ref,
        att_own_ref,
        att_other_ref,
        norms_ref,
        gains_ref,
    ) = refs[:10]
    count = layout.count()
    weights = [refs[10 + number * count : 10 + (number + 1) * count] for number in range(4)]
    (
        raised_own_ref,
        raised_send_ref,
        residual_grad_ref,
        residual_low_ref,
        att_grad_own_ref,
        att_grad_send_ref,
        width_sum_ref,
        hidden_sum_ref,
        scaled_ref,
        up_ref,
        out_ref,
        down_ref,
        sems,
    ) = refs[10 + 4 * count :]
    first = pl.program_id(0) == 0
    half = att_own_ref.shape[1]
    units = normed_ref.shape[1] // 2
    spans = [mid_spans(up_ref, out_ref, side) for side in range(2)]
    down_copies = part_copies(
        layout,
        place,
        [(weights[2 + side], [(0, units, down_ref, side * units)]) for side in range(2)],
        shared_first=True,
    )
    up_copies = part_copies(layout, place, [(weights[side], spans[side][:1]) for side in range(2)])
    out_copies = part_copies(layout, place, [(weights[side], spans[side][1:]) for side in range(2)])
    copies = [
        pltpu.make_async_copy(*copy, sems.at[n])
        for n, copy in enumerate(down_copies + up_copies + out_copies)
    ]
    marks = (0, len(down_copies), len(down_copies) + len(up_copies), len(copies))
    own_copies = len(down_copies) // 3 if layout.direct else len(down_copies) // 2

    @pl.when(first)
    def _():
        for copy in copies[: marks[1]]:
            copy.start()
        width_sum_ref[...] = jnp.zeros_like(width_sum_ref)
        hidden_sum_ref[...] = jnp.zeros_like(hidden_sum_ref)
        wait_all(copies[:own_copies])
        for copy in copies[marks[1] :]:
            copy.start()

    cot = joined(cot_mine_ref, cot_other_ref)
    residual = residual_ref[...]
    inv_std = inv_ref[:, 0:1]
    sum_plain, sum_cross = None, None
    step = 512
    for at in range(0, 2 * units, step):
        if at == units:

            @pl.when(first)
            def _():
                wait_all(copies[own_copies : marks[1]])

        grad = dot(cot, layout.read(down_ref, at, at + step), NN)
        cross = grad * normed_ref[:, at : at + step].astype(F32)
        add_rows(hidden_sum_ref, 0, first, at, cross)
        add_rows(hidden_sum_ref, 1, first, at, grad)
        gain = gains_ref[0:1, at : at + step]
        scaled = grad * gain
        scaled_ref[:, at : at + step] = scaled
        plain = jnp.sum(scaled, axis=1, keepdims=True)
        crossed = jnp.sum(cross * gain, axis=1, keepdims=True)
        sum_plain = plain if sum_plain is None else sum_plain + plain
        sum_cross = crossed if sum_cross is None else sum_cross + crossed
    mean_plain = sum_plain * (1.0 / (2 * units))
    mean_cross = sum_cross * (1.0 / (2 * units))

    @pl.when(first)
    def _():
        wait_all(copies[marks[1] : marks[2]])

    middle = None
    for at in range(0, 2 * units, step):
        active = inv_std * (
            scaled_ref[:, at : at + step]
            - mean_plain
            - normed_ref[:, at : at + step].astype(F32) * mean_cross
        )
        raised = (active * slope_ref[:, at : at + step].astype(F32)).astype(LOW)
        if at < units:
            raised_own_ref[:, at : at + step] = raised
        else:
            raised_send_ref[:, at - units : at - units + step] = raised
        part = dot(raised, layout.read(up_ref, at, at + step), NT)
        middle = part if middle is None else middle + part
    normed, inv_std = norm_of(residual)
    add_rows(width_sum_ref, 4, first, 0, middle * normed)
    add_rows(width_sum_ref, 5, first, 0, middle)
    residual_grad = cot.astype(F32) + norm_back(middle, normed, inv_std, norms_ref[4:5, :])
    residual_grad_ref[...] = residual_grad
    low = residual_grad.astype(LOW)
    residual_low_ref[...] = low

    @pl.when(first)
    def _():
        wait_all(copies[marks[2] : marks[3]])

    inner = dot(low, layout.read(out_ref), NN)
    normed, inv_std = norm_of(joined(att_own_ref, att_other_ref))
    add_rows(width_sum_ref, 2, first, 0, inner * normed)
    add_rows(width_sum_ref, 3, first, 0, inner)
    att_grad = norm_back(inner, normed, inv_std, norms_ref[2:3, :]).astype(LOW)
    att_grad_own_ref[...] = att_grad[:, :half]
    att_grad_send_ref[...] = att_grad[:, half:]


def down_backward(layout, place, rowwise, norms, gains, weights):
    hidden_normed, att_own = rowwise[0], rowwise[6]
    rows, half = att_own.shape
    units = hidden_normed.shape[1] // 2
    block = min(256, rows)
    shift = rows // block
    return pl.pallas_call(
        functools.partial(down_body, layout),
        grid_spec=pltpu.PrefetchScalarGridSpec(
            num_scalar_prefetch=1,
            grid=(rows // block,),
            in_specs=[
                rows_of(block, 2 * units),
                rows_of(block, 2 * units),
                rows_of(block, 128),
                rows_of(block, 2 * half),
                rows_of(block, half, shift),
                rows_of(block, half, shift),
                rows_of(block, half),
                rows_of(block, half),
                whole_block(norms),
                whole_block(gains),
            ]
            + [ANYWHERE] * len(weights),
            out_specs=[
                rows_of(block, units),
                rows_of(block, units),
                rows_of(block, 2 * half),
                rows_of(block, 2 * half),
                rows_of(block, half),
                rows_of(block, half),
                pl.BlockSpec((8, 2 * half), lambda i, place: (0, 0)),
                pl.BlockSpec((8, 2 * units), lambda i, place: (0, 0)),
            ],
            scratch_shapes=[
                pltpu.VMEM((block, 2 * units), F32),
                layout.scratch(2 * units),
                layout.scratch(2 * half),
                layout.scratch(2 * units),
                pltpu.SemaphoreType.DMA((192,)),
            ],
        ),
        out_shape=[
            like(rows, units, dtype=LOW),
            like(rows, units, dtype=LOW),
            like(rows, 2 * half),
            like(rows, 2 * half, dtype=LOW),
            like(rows, half, dtype=LOW),
            like(rows, half, dtype=LOW),
            like(8, 2 * half),
            like(8, 2 * units),
        ],
        compiler_params=params(56),
        cost_estimate=cost(23),
        name="down_backward",
    )(place, *rowwise, norms, gains, *weights)


def emit(layout, order, ordered_ref, columns, cut, blocks):
    keep_left, send_left, keep_right, send_right = blocks
    middle = keep_left.shape[0]
    rows = ordered_ref[...]
    for value, start in columns:
        result = dot(rows, value, NN).astype(LOW)
        width = value.shape[1]
        if start < cut:
            to = slice(start, start + width)
            keep_left[:, to] = result[:middle]
            send_left[:, to] = result[middle:]
            continue
        to = slice(start - cut, start - cut + width)
        for at, where, size in layout.right_rows(order):
            target, where = (keep_right, where) if where < middle else (send_right, where - middle)
            target[where : where + size, to] = result[at : at + size]


def column_cuts(width, base, cut, step):
    found, at = [], 0
    while at < width:
        stop = min(at + step, width)
        if base + at < cut < base + stop:
            stop = cut - base
        found.append((at, stop))
        at = stop
    return found


def stacked(own_ref, there_ref, base, cut):
    return [
        (jnp.concatenate([own_ref[:, at:stop], there_ref[:, at:stop]], axis=0), base + at)
        for at, stop in column_cuts(own_ref.shape[1], base, cut, 512)
    ]


def down_grad_body(layout, order, cut, place, mine_ref, other_ref, own_ref, there_ref, *refs):
    blocks, (columns_ref, ordered_ref) = refs[:4], refs[4:]
    half, tokens = mine_ref.shape[1], own_ref.shape[0]
    for side in range(2):
        row = pl.multiple_of(jnp.bitwise_xor(place[0], side) * tokens, PACKED_ROWS)
        to = slice(side * tokens, (side + 1) * tokens)
        columns_ref[:half, to] = mine_ref[pl.ds(row, tokens), :].T
        columns_ref[half:, to] = other_ref[pl.ds(row, tokens), :].T
    layout.order_rows(columns_ref, ordered_ref, place, order[0])
    emit(layout, order, ordered_ref, stacked(own_ref, there_ref, 0, cut), cut, blocks)


def mid_grad_body(layout, order, cut, place, *refs):
    pairs, blocks, (columns_ref, ordered_ref) = refs[:8], refs[8:12], refs[12:]
    base = 0
    for number in range(2):
        feat_ref, feat_there_ref, own_ref, there_ref = pairs[4 * number : 4 * number + 4]
        tokens, half = feat_ref.shape[0], feat_ref.shape[1] // 2
        columns_ref[:, :tokens] = feat_ref[...].T
        columns_ref[:half, tokens:] = feat_there_ref[:, half:].T
        columns_ref[half:, tokens:] = feat_there_ref[:, :half].T
        layout.order_rows(columns_ref, ordered_ref, place, order[0])
        emit(layout, order, ordered_ref, stacked(own_ref, there_ref, base, cut), cut, blocks)
        base += own_ref.shape[1]


def in_grad_body(layout, order, cut, place, feat_ref, mixed_ref, *refs):
    blocks, (columns_ref, ordered_ref) = refs[:4], refs[4:]
    columns_ref[...] = feat_ref[...].T
    layout.order_rows(columns_ref, ordered_ref, place, order[0])
    width = mixed_ref.shape[2]
    columns = [
        (mixed_ref[part, :, at:stop], part * width + at)
        for part in range(3)
        for at, stop in column_cuts(width, part * width, cut, width)
    ]
    emit(layout, order, ordered_ref, columns, cut, blocks)


def weight_grad(layout, order, body, name, place, cut, width, tokens, arrays, micros):
    rows = layout.rows * layout.paths.count
    columns = (cut, cut, width - cut, width - cut)
    found = pl.pallas_call(
        functools.partial(body, layout, order, cut),
        grid_spec=pltpu.PrefetchScalarGridSpec(
            num_scalar_prefetch=1,
            grid=(1,),
            in_specs=[whole_block(array) for array in arrays],
            out_specs=[pl.BlockSpec((rows // 2, size), lambda i, place: (0, 0)) for size in columns],
            scratch_shapes=[pltpu.VMEM((rows, tokens), LOW), pltpu.VMEM((rows, tokens), LOW)],
        ),
        out_shape=[like(rows // 2, size, dtype=LOW) for size in columns],
        compiler_params=params(40),
        cost_estimate=cost(micros),
        name=name,
    )(place, *arrays)
    return layout.finish(found, place[2], order)


def first_body(layout, place, mixed_ref, mine_ref, other_ref, hidden_own_ref, hidden_send_ref, residual_ref, *refs):
    count = layout.count()
    in_refs, down_own_refs, down_other_refs = refs[:count], refs[count : 2 * count], refs[2 * count : 3 * count]
    own_ref, send_ref, sum_ref, output_own_ref, output_send_ref, in_ref, down_ref, sems = refs[3 * count :]
    first = pl.program_id(0) == 0
    own_blocks = pl.num_programs(0) // 2
    half, units = output_send_ref.shape[1], hidden_own_ref.shape[1]
    in_copies = layout.copies(in_refs, place, [(0, in_ref.shape[-1], in_ref, 0)])
    down_copies = part_copies(
        layout,
        place,
        [
            (down_own_refs, [(0, units, down_ref, 0)]),
            (down_other_refs, [(0, units, down_ref, units)]),
        ],
        shared_first=True,
    )
    copies = [
        pltpu.make_async_copy(*copy, sems.at[n]) for n, copy in enumerate(in_copies + down_copies)
    ]

    @pl.when(first)
    def _():
        for copy in copies:
            copy.start()
        sum_ref[...] = jnp.zeros_like(sum_ref)

    normed, _ = norm_of(joined(mine_ref, other_ref).astype(F32))
    grad_mixed = jnp.concatenate([mixed_ref[part] for part in range(3)], axis=1)

    @pl.when(first)
    def _():
        wait_all(copies[: len(in_copies)])

    grad = dot(grad_mixed, layout.read(in_ref), NT)
    add_rows(sum_ref, 0, first, 0, grad * normed)
    add_rows(sum_ref, 1, first, 0, grad)

    @pl.when(first)
    def _():
        wait_all(copies[len(in_copies) :])

    @pl.when(pl.program_id(0) < own_blocks)
    def _():
        own_ref[...] = grad
        output = (
            residual_ref[...]
            + dot(hidden_own_ref[...], layout.read(down_ref, 0, units), NT)
            + dot(hidden_send_ref[...], layout.read(down_ref, units), NT)
        )
        output_own_ref[...] = output[:, :half]
        output_send_ref[...] = output[:, half:]

    @pl.when(pl.program_id(0) >= own_blocks)
    def _():
        send_ref[...] = grad


def first_backward(layout, place, grad_mixed, mine, other, hidden_own, hidden_send, residual, weights):
    rows, half = mine.shape
    units = hidden_own.shape[1]
    block = min(256, rows // 2)
    count = rows // block
    owned = count // 2

    def own_rows_first(i, place):
        return (i + place[0] * owned) % count

    def own_rows(columns):
        return pl.BlockSpec((block, columns), lambda i, place: (jnp.minimum(i, owned - 1), 0))

    return pl.pallas_call(
        functools.partial(first_body, layout),
        grid_spec=pltpu.PrefetchScalarGridSpec(
            num_scalar_prefetch=1,
            grid=(count,),
            in_specs=[
                pl.BlockSpec((3, block, half), lambda i, place: (0, own_rows_first(i, place), 0)),
                pl.BlockSpec((block, half), lambda i, place: (own_rows_first(i, place), 0)),
                pl.BlockSpec((block, half), lambda i, place: (own_rows_first(i, place), 0)),
                own_rows(units),
                own_rows(units),
                own_rows(2 * half),
            ]
            + [ANYWHERE] * len(weights),
            out_specs=[
                own_rows(2 * half),
                pl.BlockSpec((block, 2 * half), lambda i, place: (jnp.maximum(i - owned, 0), 0)),
                pl.BlockSpec((8, 2 * half), lambda i, place: (0, 0)),
                pl.BlockSpec(
                    (block, half),
                    lambda i, place: (jnp.minimum(i, owned - 1) + place[0] * owned, 0),
                ),
                own_rows(half),
            ],
            scratch_shapes=[
                layout.scratch(3 * half),
                layout.scratch(2 * units),
                pltpu.SemaphoreType.DMA((96,)),
            ],
        ),
        out_shape=[
            like(rows // 2, 2 * half),
            like(rows // 2, 2 * half),
            like(8, 2 * half),
            like(rows, half),
            like(rows // 2, half),
        ],
        compiler_params=params(40),
        cost_estimate=cost(11),
        name="first_backward",
    )(place, grad_mixed, mine, other, hidden_own, hidden_send, residual, *weights)


def token_body(place, own_ref, there_ref, mine_ref, other_ref, norms_ref, residual_ref, keep_ref, send_ref):
    half = mine_ref.shape[1]
    normed, inv_std = norm_of(joined(mine_ref, other_ref).astype(F32))
    grad = own_ref[...] + turned(there_ref[...])
    result = residual_ref[...] + norm_back(grad, normed, inv_std, norms_ref[0:1, :])
    keep_ref[...] = result[:, :half]
    send_ref[...] = result[:, half:]


def token_backward(place, own, there, mine, other, norms, residual):
    rows, half = own.shape[0], mine.shape[1]
    block = min(256, rows)
    shift = rows // block
    return pl.pallas_call(
        token_body,
        grid_spec=pltpu.PrefetchScalarGridSpec(
            num_scalar_prefetch=1,
            grid=(rows // block,),
            in_specs=[
                rows_of(block, 2 * half),
                rows_of(block, 2 * half),
                rows_of(block, half, shift),
                rows_of(block, half, shift),
                whole_block(norms),
                rows_of(block, 2 * half),
            ],
            out_specs=[rows_of(block, half, shift), rows_of(block, half)],
        ),
        out_shape=[like(2 * rows, half), like(rows, half)],
        compiler_params=params(24),
        cost_estimate=cost(3),
        name="token_backward",
    )(place, own, there, mine, other, norms, residual)


def fill_body(place, there_ref, whole_ref, out_ref):
    out_ref[...] = there_ref[...]


def fill_there(place, whole, there):
    rows, columns = there.shape
    return pl.pallas_call(
        fill_body,
        grid_spec=pltpu.PrefetchScalarGridSpec(
            num_scalar_prefetch=1,
            grid=(1,),
            in_specs=[pl.BlockSpec((rows, columns), lambda i, place: (0, 0)), ANYWHERE],
            out_specs=pl.BlockSpec((rows, columns), lambda i, place: (1 - place[0], 0)),
        ),
        out_shape=like(2 * rows, columns),
        input_output_aliases={2: 0},
        cost_estimate=cost(2),
        name="fill_there",
    )(place, there, whole)


def adam_moments(grad, first, second):
    new_first = BETA_ONE * first + (1.0 - BETA_ONE) * grad
    new_second = BETA_TWO * second + (1.0 - BETA_TWO) * grad * grad
    step_dir = (
        new_first
        / (1.0 - BETA_ONE**STEP)
        / (jnp.sqrt(new_second / (1.0 - BETA_TWO**STEP)) + EPS_ADAM)
    )
    return (new_first, new_second, step_dir)


def at_lane(row, lane, value):
    rows = lax.broadcasted_iota(jnp.int32, (8, 128), 0)
    lanes = lax.broadcasted_iota(jnp.int32, (8, 128), 1)
    return jnp.where((rows == row) & (lanes == lane), value, 0.0)


def sum_of(source):
    return jnp.sum(jnp.sum(source * source, axis=1, keepdims=True), axis=0, keepdims=True)


def moments_body(numbers, cuts, counts, *refs):
    kept, arrived, refs = refs[: counts[0]], refs[counts[0] : sum(counts)], refs[sum(counts) :]
    count = len(numbers)
    states, outs, squares_ref = refs[: 3 * count], refs[3 * count : 6 * count], refs[6 * count]
    whole = []
    for at, keep_ref in enumerate(kept):
        total = keep_ref[...]
        for ref in arrived[at :: len(kept)]:
            total = total + ref[...].astype(F32)
        whole.append(total)
    whole = jnp.concatenate(whole, axis=1) if len(whole) > 1 else whole[0]
    squares = jnp.zeros((8, 128), F32)
    for number in range(count):
        master_ref, first_ref, second_ref = states[3 * number : 3 * number + 3]
        new_first_ref, new_second_ref, update_ref = outs[3 * number : 3 * number + 3]
        start, stop = cuts[number]
        parts = master_ref.shape[0] if master_ref.ndim == 3 else 1
        width = (stop - start) // parts
        for part in range(parts):
            pick = (lambda ref: ref.at[part]) if master_ref.ndim == 3 else (lambda ref: ref)
            master = pick(master_ref)[...]
            new_first, new_second, step_dir = adam_moments(
                whole[:, start + part * width : start + (part + 1) * width],
                pick(first_ref)[...],
                pick(second_ref)[...],
            )
            update = step_dir + DECAY * master
            pick(new_first_ref)[...] = new_first
            pick(new_second_ref)[...] = new_second
            pick(update_ref)[...] = update
            squares = squares + at_lane(0, numbers[number], sum_of(master))
            squares = squares + at_lane(1, numbers[number], sum_of(update))
    squares_ref[...] = squares


def moments(numbers, cuts, kept, arrived, states, name):
    in_vmem = pl.BlockSpec(memory_space=pltpu.VMEM)
    outs = [like(*state.shape) for state in states]
    counts = (len(kept), len(arrived))
    return pl.pallas_call(
        functools.partial(moments_body, numbers, cuts, counts),
        in_specs=[in_vmem] * (sum(counts) + len(states)),
        out_specs=[in_vmem] * (len(states) + 1),
        out_shape=outs + [like(8, 128)],
        compiler_params=params(40),
        cost_estimate=cost(3),
        name=name,
    )(*kept, *arrived, *states)


def norm_moments_body(packed_ref, *refs):
    states, outs, squares_ref = refs[:6], refs[6:12], refs[12]
    units = states[3].shape[1]
    squares = jnp.zeros((8, 128), F32)
    lane = 4
    for number, (rows, start) in enumerate(((6, units), (2, 0))):
        master_ref, first_ref, second_ref = states[3 * number : 3 * number + 3]
        grad = packed_ref[0:rows, start : start + master_ref.shape[1]]
        master = master_ref[...]
        results = adam_moments(grad, first_ref[...], second_ref[...])
        for ref, result in zip(outs[3 * number : 3 * number + 3], results):
            ref[...] = result
        for row in range(rows):
            squares = squares + at_lane(0, lane, sum_of(master[row : row + 1]))
            squares = squares + at_lane(1, lane, sum_of(results[2][row : row + 1]))
            lane += 1
    squares_ref[...] = squares


def norm_moments(packed, states):
    in_vmem = pl.BlockSpec(memory_space=pltpu.VMEM)
    return pl.pallas_call(
        norm_moments_body,
        in_specs=[in_vmem] * 7,
        out_specs=[in_vmem] * 7,
        out_shape=[like(*state.shape) for state in states] + [like(8, 128)],
        cost_estimate=cost(1),
        name="norm_moments",
    )(packed, *states)


def apply_body(squares_ref, squares_there_ref, *refs):
    masters, updates, outs = refs[:6], refs[6:12], refs[12:]
    squares = squares_ref[...] + squares_there_ref[...]
    ratio = jnp.sqrt(squares[0:1, :] / (squares[1:2, :] + 1e-06)) * RATE
    lanes = lax.broadcasted_iota(jnp.int32, ratio.shape, 1)

    def scale(lane):
        return jnp.sum(jnp.where(lanes == lane, ratio, 0.0), axis=1, keepdims=True)

    lane = 0
    for master_ref, update_ref, out_ref in zip(masters, updates, outs):
        if out_ref.ndim == 3:
            for part in range(out_ref.shape[0]):
                out_ref[part] = master_ref[part] - scale(lane) * update_ref[part]
            lane += 1
        elif lane < 4:
            out_ref[...] = master_ref[...] - scale(lane) * update_ref[...]
            lane += 1
        else:
            rows = out_ref.shape[0]
            factors = jnp.concatenate([scale(lane + row) for row in range(rows)], axis=0)
            out_ref[...] = master_ref[...] - factors * update_ref[...]
            lane += rows


def apply_updates(squares, squares_there, masters, updates):
    in_vmem = pl.BlockSpec(memory_space=pltpu.VMEM)
    return pl.pallas_call(
        apply_body,
        in_specs=[in_vmem] * 14,
        out_specs=[in_vmem] * 6,
        out_shape=[like(*master.shape) for master in masters],
        compiler_params=params(40),
        cost_estimate=cost(3),
        name="apply_updates",
    )(squares, squares_there, *masters, *updates)


def shards(
    paths,
    tokens,
    cotangent,
    seq_lengths,
    attn_in,
    attn_out,
    ffn_up,
    ffn_down,
    first_attn_in,
    second_attn_in,
    first_attn_out,
    second_attn_out,
    first_ffn_up,
    second_ffn_up,
    first_ffn_down,
    second_ffn_down,
    width_norm_params,
    first_width_norms,
    second_width_norms,
    hidden_norm_params,
    first_hidden_norms,
    second_hidden_norms,
):
    core = lax.axis_index("tensor")
    index = lax.axis_index("dp")
    mine = index ^ (core * (paths.count // 2))
    place = jnp.stack([core, index, mine]).astype(jnp.int32)
    tok_rows, half = tokens.shape
    units = ffn_up.shape[1]
    layout = Layout(paths, ffn_up.shape[0])

    shard_in = jnp.transpose(attn_in, (1, 0, 2)).reshape(attn_in.shape[1], -1).astype(LOW)
    shard_mid = jnp.concatenate([ffn_up, attn_out.T], axis=1).astype(LOW)
    shard_down = ffn_down.T.astype(LOW)
    cut_in, cut_mid, cut_down = 512, 1024, units // 2
    get_in, get_mid, get_down = [Gather(paths, cut, mine) for cut in (cut_in, cut_mid, cut_down)]
    scatter = Scatter(paths)

    arrived_in = get_in.send_shared(shard_in, 0)
    tok_other = swap(tokens)
    cot_other = swap(cotangent)
    norms = jnp.concatenate([width_norm_params, swap(width_norm_params)], axis=1)
    gains = jnp.concatenate([hidden_norm_params, swap(hidden_norm_params)], axis=1)
    ends = jnp.cumsum(seq_lengths[0])
    shard_in, arrived_in, shard_mid, shard_down = tie(shard_in, arrived_in, shard_mid, shard_down)
    pair_in = get_in.join_shared(shard_in, arrived_in, 0)
    arrived_in = get_in.send_shared(pair_in, 1)
    pair_in, arrived_in, shard_mid, shard_down, tok_other, cot_other, norms, gains, ends = tie(
        pair_in, arrived_in, shard_mid, shard_down, tok_other, cot_other, norms, gains, ends
    )
    line_in = get_in.join_shared(pair_in, arrived_in, 1).reshape(1, -1, *shard_in.shape)
    held_in = get_in.send_one(line_in)
    arrived_mid = get_mid.send_shared(shard_mid, 0)
    held_in, shard_down = tie(held_in, shard_down)
    pieces_in = get_in.send_two(get_in.join_one(held_in))
    pair_mid = get_mid.join_shared(shard_mid, arrived_mid, 0)
    arrived_mid = get_mid.send_shared(pair_mid, 1)
    if get_down.even():
        early_down = get_down.send_one(shard_down[None])
        stack_down = jnp.concatenate(get_down.join_one(early_down), axis=2)
    else:
        stack_down = shard_down
    pieces_in, stack_down = tie(pieces_in, stack_down)
    line_mid = get_mid.join_shared(pair_mid, arrived_mid, 1).reshape(1, -1, *shard_mid.shape)
    held_mid = get_mid.send_one(line_mid)
    arrived_down = get_down.send_shared(stack_down, 0)
    weights_in = layout.prepare(pieces_in, mine)
    mixed, feat_one = qkv_forward(layout, place, tokens, tok_other, norms, weights_in)
    mixed, feat_one, held_mid, stack_down, arrived_down = tie(
        mixed, feat_one, held_mid, stack_down, arrived_down
    )
    stack_down = get_down.join_shared(stack_down, arrived_down, 0)
    arrived_down = get_down.send_shared(stack_down, 1)
    stacks_mid = get_mid.join_one(held_mid)
    pieces_mid = get_mid.send_two(stacks_mid)
    early_mid = [swap(pieces_mid[0]), swap(pieces_mid[2])]
    att_own, att_send, logs = attn_forward(place, ends, mixed)
    att_own, att_send, pieces_mid, early_mid, stack_down, arrived_down = tie(
        att_own, att_send, pieces_mid, early_mid, stack_down, arrived_down
    )
    att_other = swap(att_send)
    late_mid = [swap(pieces_mid[1]), swap(pieces_mid[3])]
    line_down = get_down.join_shared(stack_down, arrived_down, 1)
    if get_down.even():
        line_down = line_down.reshape(-1, *line_down.shape[2:])
        stacks_down = [line_down[..., :cut_down], line_down[..., cut_down:]]
    else:
        line_down = line_down.reshape(1, -1, *shard_down.shape)
        stacks_down = get_down.join_one(get_down.send_one(line_down))
    pieces_down = get_down.send_two(stacks_down)
    att_other, late_mid = tie(att_other, late_mid)
    weights_mid = layout.prepare(pieces_mid, mine) + layout.prepare(
        [early_mid[0], late_mid[0], early_mid[1], late_mid[1]], mine, True
    )
    early_down = [swap(pieces_down[0]), swap(pieces_down[2])]
    (
        inner_own,
        inner_send,
        residual,
        feat_two,
        hidden_own,
        hidden_send,
        hidden_normed,
        slope,
        hidden_inv,
    ) = up_forward(
        layout, place, att_own, att_other, tokens, tok_other, norms, gains, weights_mid
    )
    pieces_down, early_down, hidden_send, feat_two, inner_send = tie(
        pieces_down, early_down, hidden_send, feat_two, inner_send
    )
    hidden_there = swap(hidden_send)
    late_down = [swap(pieces_down[1]), swap(pieces_down[3])]
    hidden_there, hidden_own = tie(hidden_there, hidden_own)
    grad_down = weight_grad(
        layout,
        layout.outer,
        down_grad_body,
        "down_grad",
        place,
        cut_down,
        units,
        tok_rows,
        (cotangent, cot_other, hidden_own, hidden_there),
        4,
    )
    grad_down, hidden_own, feat_two, inner_send, late_down = tie(
        grad_down, hidden_own, feat_two, inner_send, late_down
    )
    weights_down = layout.prepare(pieces_down, mine) + layout.prepare(
        [early_down[0], late_down[0], early_down[1], late_down[1]], mine, True
    )
    feat_two_there, inner_there = swap(feat_two), swap(inner_send)
    held_down = scatter.send_one(grad_down)
    (
        raised_own,
        raised_send,
        residual_grad,
        residual_low,
        att_grad_own,
        att_grad_send,
        width_sum,
        hidden_sum,
    ) = down_backward(
        layout,
        place,
        (
            hidden_normed,
            slope,
            hidden_inv,
            residual,
            cotangent,
            cot_other,
            att_own,
            att_other,
        ),
        norms,
        gains,
        weights_mid + weights_down,
    )
    held_down, raised_send, residual_low, att_grad_send, feat_two_there, inner_there = tie(
        held_down, raised_send, residual_low, att_grad_send, feat_two_there, inner_there
    )
    raised_there, residual_there = swap(raised_send), swap(residual_low)
    att_grad_other = swap(att_grad_send)
    held_down = scatter.send_two(held_down)
    raised_there, residual_there = tie(raised_there, residual_there)
    grad_mid = weight_grad(
        layout,
        layout.outer,
        mid_grad_body,
        "mid_grad",
        place,
        cut_mid,
        units + half,
        tok_rows,
        (
            feat_two,
            feat_two_there,
            raised_own,
            raised_there,
            residual_low,
            residual_there,
            inner_own,
            inner_there,
        ),
        6,
    )
    grad_mid, held_down, att_grad_other = tie(grad_mid, held_down, att_grad_other)
    held_mid = scatter.send_one(grad_mid)
    held_down = scatter.send_shared(scatter.join(held_down))
    grad_mixed = attn_backward(place, ends, mixed, att_grad_own, att_grad_other, logs)
    grad_mixed, held_mid, held_down = tie(grad_mixed, held_mid, held_down)
    keep_down, arrived_down = scatter.send_last(held_down)
    settled_mid = [scatter.settle(pair) for pair in held_mid]
    grad_mixed, settled_mid = tie(grad_mixed, settled_mid)
    held_mid = scatter.send_settled(settled_mid)
    grad_in = weight_grad(
        layout, layout.outer, in_grad_body, "in_grad", place, cut_in, 3 * half, tok_rows, (feat_one, grad_mixed), 5
    )
    grad_in, grad_mixed, held_mid = tie(grad_in, grad_mixed, held_mid)
    held_in = scatter.send_one(grad_in)
    held_mid = scatter.send_shared(scatter.join(held_mid))
    first_own, first_send, first_sum, output_own, output_send = first_backward(
        layout,
        place,
        grad_mixed,
        tokens,
        tok_other,
        hidden_own,
        hidden_send,
        residual,
        weights_in + weights_down,
    )
    held_in, first_own, first_send, first_sum, output_send, arrived_down, held_mid = tie(
        held_in, first_own, first_send, first_sum, output_send, arrived_down, held_mid
    )
    held_in = scatter.send_two(held_in)
    keep_mid, arrived_mid = scatter.send_last(held_mid)
    first_there = swap(first_send)
    down_state = moments(
        (3,),
        ((0, units),),
        [keep_down],
        [arrived_down],
        (ffn_down.T, first_ffn_down.T, second_ffn_down.T),
        "down_moments",
    )
    width_sum = width_sum + first_sum
    packed = jnp.concatenate([hidden_sum[:, :units], width_sum[:, :half]], axis=1) + swap(
        jnp.concatenate([hidden_sum[:, units:], width_sum[:, half:]], axis=1)
    )
    held_in, arrived_mid, first_there, output_send, down_state, packed = tie(
        held_in, arrived_mid, first_there, output_send, down_state, packed
    )
    held_in = scatter.send_shared(scatter.join(held_in))
    packed = paths.sum_send(packed, 0)
    output_there = swap(output_send)
    mid_state = moments(
        (2, 1),
        ((0, units), (units, units + half)),
        [keep_mid],
        [arrived_mid],
        (ffn_up, first_ffn_up, second_ffn_up, attn_out.T, first_attn_out.T, second_attn_out.T),
        "mid_moments",
    )
    held_in, packed, first_there, output_there, mid_state = tie(
        held_in, packed, first_there, output_there, mid_state
    )
    keep_in, arrived_in = scatter.send_last(held_in)
    token_own, token_send = token_backward(
        place, first_own, first_there, tokens, tok_other, norms, residual_grad
    )
    packed = paths.sum_send(sum(packed), 1)
    arrived_in, token_send, packed = tie(arrived_in, token_send, packed)
    packed = sum(packed)
    token_there = swap(token_send)
    in_state = moments(
        (0,),
        ((0, 3 * half),),
        [keep_in],
        [arrived_in],
        (attn_in, first_attn_in, second_attn_in),
        "in_moments",
    )
    squares = in_state[3] + (mid_state[6] + down_state[3])
    squares, packed = tie(squares, packed)
    squares = paths.sum_send(squares, 0)
    packed = paths.sum_send(packed, 2)
    block_output = fill_there(place, output_own, output_there)
    squares, packed, block_output, token_there = tie(squares, packed, block_output, token_there)
    squares = paths.sum_send(sum(squares), 1)
    for step in range(3, paths.steps()):
        packed = paths.sum_send(sum(packed), step)
    squares, packed = tie(squares, packed)
    squares = paths.sum_send(sum(squares), 2)
    norm_state = norm_moments(
        sum(packed),
        (
            width_norm_params,
            first_width_norms,
            second_width_norms,
            hidden_norm_params,
            first_hidden_norms,
            second_hidden_norms,
        ),
    )
    squares, norm_state = tie(squares, norm_state)
    squares = paths.sum_send(sum(squares), 3)
    grad_tokens = fill_there(place, token_own, token_there)
    squares, grad_tokens = tie(squares, grad_tokens)
    for step in range(4, paths.steps()):
        squares = paths.sum_send(sum(squares), step)
    squares = sum(squares) + norm_state[6]
    squares_there = swap(squares)
    new_in, new_out, new_up, new_down, new_width, new_hidden = apply_updates(
        squares,
        squares_there,
        (attn_in, attn_out.T, ffn_up, ffn_down.T, width_norm_params, hidden_norm_params),
        (in_state[2], mid_state[5], mid_state[2], down_state[2], norm_state[2], norm_state[5]),
    )
    return (
        block_output,
        grad_tokens,
        new_in,
        new_out.T,
        new_up,
        new_down.T,
        in_state[0],
        mid_state[3].T,
        mid_state[0],
        down_state[0].T,
        in_state[1],
        mid_state[4].T,
        mid_state[1],
        down_state[1].T,
        new_width,
        norm_state[0],
        norm_state[1],
        new_hidden,
        norm_state[3],
        norm_state[4],
    )


def solution(mesh):
    rows = P("dp", "tensor")
    stacked_rows = P(None, "dp", "tensor")
    upright_rows = P("tensor", "dp")
    narrow = P(None, "tensor")
    in_specs = (
        (rows, rows, P("dp", None), stacked_rows, upright_rows, rows, upright_rows)
        + (stacked_rows, stacked_rows, upright_rows, upright_rows)
        + (rows, rows, upright_rows, upright_rows)
        + (narrow,) * 6
    )
    out_specs = (rows, rows) + (stacked_rows, upright_rows, rows, upright_rows) * 3 + (narrow,) * 6
    paths = Paths(mesh.shape["dp"])

    def body(*arrays):
        return shards(paths, *arrays)

    return jax.shard_map(
        body, mesh=mesh, in_specs=in_specs, out_specs=out_specs, check_vma=False
    )
```
